32 devices in a mesh: seq: 8 (over z, x), head: 4 (over y, core).
Axes of the slice: x: 2, y: 2, z: 4, core: 2. Of those that a mesh axis runs over, the one named last changes fastest.
Arguments:
- queries: bfloat16 [8192, 2048], P('seq', 'head'), may hold values from -1.796875 to 1.796875
- keys: bfloat16 [8192, 2048], P('seq', 'head'), may hold values from -1.796875 to 1.796875
- values: bfloat16 [8192, 2048], P('seq', 'head'), may hold values from -16 to 16
- grad_out: bfloat16 [8192, 2048], P('seq', 'head'), may hold values from -1.1953125 to 1.1953125
Outputs:
- output: bfloat16 [8192, 2048], P('seq', 'head')
- grad_query: bfloat16 [8192, 2048], P('seq', 'head')
- grad_key: bfloat16 [8192, 2048], P('seq', 'head')
- grad_value: bfloat16 [8192, 2048], P('seq', 'head')
The draws below stay inside these ranges and needn't reach their ends.
All inputs are finite; a program needn't handle non-finite values.
Results may differ from the reference program's by a relative error of at most 0.0065.
Values sent between devices are 32-bit elements; how exact they have to be, the bound alone decides.
No kernel may reach another device: no remote copies, remote signals or barrier semaphores. Data moves between devices by JAX's collectives and lax.ppermute only.
A program may use at most 128 MiB of HBM per device.

```python
import jax
import jax.numpy as jnp
from jax import lax

HEADS = 16
HEAD_DIM = 128
TOK_DEV = 1024
TOKENS = 8192


def draw_values(key, part):
    key_scale, key_body = jax.random.split(key, 2)
    head_index = jnp.arange(HEADS, dtype=jnp.float32)
    jitter = jax.random.uniform(key_scale, (HEADS,), jnp.float32)
    head_scale = 0.4 * 10.0 ** ((head_index + jitter) / HEADS)
    base = jnp.clip(jax.random.normal(key_body, (TOKENS, HEADS, HEAD_DIM), jnp.float32), -4.0, 4.0)
    return (base * head_scale[None, :, None]).reshape(TOKENS, HEADS * HEAD_DIM).astype(jnp.bfloat16)


def block_levels(key, dims, cuts, low, high):
    def one(dim, parts):
        draws = jax.random.uniform(jax.random.fold_in(jax.random.fold_in(key, 6), dim), (parts,), jnp.float32, low / len(cuts), high / len(cuts))
        return jnp.repeat(jnp.exp(draws), dims[dim] // parts).reshape((-1,) + (1,) * (len(dims) - dim - 1))

    gain = one(*cuts[0])
    for cut in cuts[1:]:
        gain = gain * one(*cut)
    return gain


def normal_values(rng, shape, width, most, cuts=(), kind=jnp.bfloat16):
    level = block_levels(rng, shape, cuts, -0.22, 0.18) if cuts else 1.0
    result = jax.random.normal(rng, shape, jnp.float32) * width * level
    return jnp.minimum(jnp.maximum(result, -most), most).astype(kind)


def setup_inputs(seed: int = 0) -> dict:
    streams_of = jax.random.split(jax.random.key(seed), 5)
    queries = normal_values(streams_of[0], (TOKENS, HEADS * HEAD_DIM), 0.3, 1.796875, ((0, 8), (1, 4)))
    keys = normal_values(streams_of[1], (TOKENS, HEADS * HEAD_DIM), 0.3, 1.796875, ((0, 8), (1, 4)))
    values = draw_values(jax.random.fold_in(streams_of[4], 71), 0)
    grad_out = normal_values(streams_of[3], (TOKENS, HEADS * HEAD_DIM), 0.2, 1.1953125, ((0, 8), (1, 4)))
    return {"queries": queries, "keys": keys, "values": values, "grad_out": grad_out}


EPSILON = 1e-06

def rounded(tensor):
    return lax.optimization_barrier(tensor.astype(jnp.bfloat16)).astype(jnp.float32)

def causal_scores(query_side, key_side):
    raw_scores = jnp.einsum('thd,shd->hts', query_side, key_side)
    row_index = jnp.arange(query_side.shape[0], dtype=jnp.int32)
    keep = row_index[:, None] >= row_index[None, :]
    return rounded(jnp.where(keep[None], raw_scores, jnp.zeros_like(raw_scores)))

def reference(queries, keys, values, grad_out):
    n_blocks = TOKENS // TOK_DEV
    block_shape = (n_blocks, TOK_DEV, HEADS, HEAD_DIM)
    query_blocks = queries.reshape(block_shape)
    key_blocks = keys.reshape(block_shape)
    value_blocks = values.reshape(block_shape)

    def forward_step(prefix, block_data):
        query_block = block_data[0].astype(jnp.float32)
        key_block = block_data[1].astype(jnp.float32)
        value_block = block_data[2].astype(jnp.float32)
        scores = causal_scores(query_block, key_block)
        mixed = jnp.einsum('hts,she->the', scores, value_block)
        mixed = mixed + jnp.einsum('thd,hde->the', query_block, rounded(prefix))
        local_state = jnp.einsum('thd,the->hde', key_block, value_block)
        return (prefix + local_state, (mixed, prefix))
    zero_state = jnp.zeros((HEADS, HEAD_DIM, HEAD_DIM), jnp.float32)
    unused, (mixed, prefixes) = lax.scan(forward_step, zero_state, (query_blocks, key_blocks, value_blocks))
    mixed_rows = mixed.reshape(TOKENS, HEADS * HEAD_DIM)
    inverse_rms = lax.rsqrt(lax.optimization_barrier(jnp.mean(mixed_rows * mixed_rows, axis=1, keepdims=True)) + EPSILON)
    normed = mixed_rows * inverse_rms
    output = normed.astype(jnp.bfloat16)
    grad_float = grad_out.astype(jnp.float32)
    cross_mean = lax.optimization_barrier(jnp.mean(grad_float * normed, axis=1, keepdims=True))
    grad_mixed = (inverse_rms * (grad_float - normed * cross_mean)).astype(jnp.bfloat16)
    grad_blocks = grad_mixed.reshape(block_shape)

    def grad_state(block_data):
        return jnp.einsum('thd,the->hde', block_data[0].astype(jnp.float32), block_data[1].astype(jnp.float32))
    local_grads = lax.map(grad_state, (query_blocks, grad_blocks))

    def suffix_step(carry, term):
        return (carry + term, carry)
    unused_two, suffixes = lax.scan(suffix_step, zero_state, local_grads, reverse=True)

    def backward_block(block_data):
        query_block = block_data[0].astype(jnp.float32)
        key_block = block_data[1].astype(jnp.float32)
        value_block = block_data[2].astype(jnp.float32)
        grad_block = block_data[3].astype(jnp.float32)
        prefix_round = rounded(block_data[4])
        suffix_round = rounded(block_data[5])
        scores = causal_scores(query_block, key_block)
        grad_scores = causal_scores(grad_block, value_block)
        grad_q = jnp.einsum('hts,shd->thd', grad_scores, key_block) + jnp.einsum('the,hde->thd', grad_block, prefix_round)
        grad_k = jnp.einsum('hts,thd->shd', grad_scores, query_block) + jnp.einsum('she,hde->shd', value_block, suffix_round)
        grad_v = jnp.einsum('hts,the->she', scores, grad_block) + jnp.einsum('shd,hde->she', key_block, suffix_round)
        return (grad_q.astype(jnp.bfloat16), grad_k.astype(jnp.bfloat16), grad_v.astype(jnp.bfloat16))
    grad_q, grad_k, grad_v = lax.map(backward_block, (query_blocks, key_blocks, value_blocks, grad_blocks, prefixes, suffixes))
    flat_shape = (TOKENS, HEADS * HEAD_DIM)
    return (output, grad_q.reshape(flat_shape), grad_k.reshape(flat_shape), grad_v.reshape(flat_shape))
```

```python
import functools

import jax
import jax.numpy as jnp
from jax import lax
from jax.experimental import pallas as pl
from jax.experimental.pallas import tpu as pltpu
from jax.sharding import PartitionSpec as P

HEAD_DIM = 128
EPSILON = 1e-06
CHUNK = 256
PAIR = 2 * HEAD_DIM
F32 = jnp.float32
BF16 = jnp.bfloat16


def dot(a, b, ca, cb):
    return lax.dot_general(a, b, (((ca,), (cb,)), ((), ())), preferred_element_type=F32)


def pair_state(left, right):
    full = dot(left, right, 0, 0)
    return jnp.concatenate(
        [full[:HEAD_DIM, :HEAD_DIM], full[HEAD_DIM:, HEAD_DIM:]], axis=0
    )


def store_halves(pairs, own_ref, oth_ref):
    odd = lax.rem(lax.axis_index("seq"), 2) == 1
    own_ref[...] = jnp.where(odd, pairs[1], pairs[0])
    oth_ref[...] = jnp.where(odd, pairs[0], pairs[1])


def merge_halves(own, oth):
    odd = lax.rem(lax.axis_index("seq"), 2) == 1
    return jnp.where(odd, oth, own), jnp.where(odd, own, oth)


def causal(count):
    rows = lax.broadcasted_iota(jnp.int32, (count, count), 0)
    cols = lax.broadcasted_iota(jnp.int32, (count, count), 1)
    return rows >= cols


def call(body, out_shape, args, flops, name, limit=48):
    size = sum(a.size * a.dtype.itemsize for a in args)
    size += sum(a.size * a.dtype.itemsize for a in out_shape)
    return pl.pallas_call(
        body,
        out_shape=out_shape,
        in_specs=[pl.BlockSpec(memory_space=pltpu.VMEM)] * len(args),
        out_specs=[pl.BlockSpec(memory_space=pltpu.VMEM)] * len(out_shape),
        compiler_params=pltpu.CompilerParams(vmem_limit_bytes=limit * 2**20),
        cost_estimate=pl.CostEstimate(flops=flops, bytes_accessed=size, transcendentals=0),
        name=name,
    )(*args)


def chain_scan(own, oth, size, reverse):
    def dev(level, side):
        place = 2 * level + side
        return size - 1 - place if reverse else place

    def permute(value, pairs):
        both = [(dev(*a), dev(*b)) for a, b in pairs]
        return lax.ppermute(value, "seq", both + [(b, a) for a, b in both])

    sides = (0, 1)
    inner = [((level, 0), (level, 1)) for level in range(4)]
    outer = [inner[0], inner[3]]
    straight = [((level, s), (level + 1, s)) for level in (0, 2) for s in sides]
    crossed = [((level, s), (level + 1, 1 - s)) for level in (0, 2) for s in sides]
    middle = [((1, s), (2, s)) for s in sides]
    middle_crossed = [((1, s), (2, 1 - s)) for s in sides]

    place = lax.axis_index("seq")
    if reverse:
        place = size - 1 - place
    level = place // 2

    a1 = permute(own, straight)
    a2 = permute(oth, crossed)
    a3 = permute(oth, inner)
    a4 = permute(own, inner)
    total = own + a3
    window = total + (a1 + a2)
    b1 = permute(window, middle + outer)
    b2 = permute(window, middle_crossed + outer)
    running = jnp.where(level == 2, b1, jnp.zeros_like(b1)) + total
    c1 = permute(running, straight)
    c2 = permute(running, crossed)
    return [a3, a4, b1, b2, c1, c2]


def chain_merge(refs, size, reverse):
    a3, a4, b1, b2, c1, c2 = [r[...] for r in refs]
    place = lax.axis_index("seq")
    if reverse:
        place = size - 1 - place
    level, side = place // 2, lax.rem(place, 2)
    zero = jnp.zeros_like(a3)

    def pick(a, b, c):
        before = jnp.where(lax.rem(level, 2) == 1, c, jnp.where(level == 2, b, zero))
        return before + jnp.where(side == 1, a, zero)

    return merge_halves(pick(a3, b1, c1), pick(a4, b2, c2))


def doubling_scan(own, oth, size, reverse):
    def shift(value, by):
        pairs = [(i, i + by) for i in range(size - by)]
        if reverse:
            pairs = [(b, a) for a, b in pairs]
        return lax.ppermute(value, "seq", pairs)

    odd = lax.rem(lax.axis_index("seq"), 2) == 1
    both = jnp.stack([jnp.where(odd, oth, own), jnp.where(odd, own, oth)])
    by = 1
    while by < size:
        both = both + shift(both, by)
        by *= 2
    both = shift(both, 1)
    return [both[0], both[1]]


def doubling_merge(refs, size, reverse):
    return refs[0][...], refs[1][...]


def state_kernel(k, v, own, oth):
    pairs = [
        pair_state(k[:, p * PAIR : (p + 1) * PAIR], v[:, p * PAIR : (p + 1) * PAIR])
        for p in range(2)
    ]
    store_halves(pairs, own, oth)


def intra_kernel(q, k, v, intra):
    rows = q.shape[0]
    keep = causal(CHUNK)
    for h in range(q.shape[1] // HEAD_DIM):
        cols = slice(h * HEAD_DIM, (h + 1) * HEAD_DIM)
        state = None
        for start in range(0, rows, CHUNK):
            at = slice(start, start + CHUNK)
            qi, ki, vi = q[at, cols], k[at, cols], v[at, cols]
            scores = jnp.where(keep, dot(qi, ki, 1, 1), 0.0).astype(BF16)
            out = dot(scores, vi, 1, 0)
            if state is not None:
                out = out + dot(qi, state.astype(BF16), 1, 0)
            intra[at, cols] = out
            if start + CHUNK < rows:
                new = dot(ki, vi, 0, 0)
                state = new if state is None else state + new


def row_sums(tile):
    return jnp.sum(tile.T, axis=0, keepdims=True)


def mixed_kernel(merge, n_parts, intra, q, g, *refs):
    parts, (mixed, stats, prefix) = refs[:n_parts], refs[n_parts:]
    pairs = merge(parts)
    heads = q.shape[1] // HEAD_DIM
    rounded = [p.astype(BF16) for p in pairs]
    for p in range(2):
        prefix[p * PAIR : (p + 1) * PAIR, :] = rounded[p]
    blocks = q.shape[0] // HEAD_DIM
    for start in range(0, q.shape[0], CHUNK):
        at = slice(start, start + CHUNK)
        square = cross = None
        for h in range(heads):
            cols = slice(h * HEAD_DIM, (h + 1) * HEAD_DIM)
            state = rounded[h // 2][(h % 2) * HEAD_DIM : (h % 2 + 1) * HEAD_DIM]
            m = intra[at, cols] + dot(q[at, cols], state, 1, 0)
            mixed[at, cols] = m
            s, c = m * m, m * g[at, cols].astype(F32)
            square = s if square is None else square + s
            cross = c if cross is None else cross + c
        for j in range(CHUNK // HEAD_DIM):
            part = slice(j * HEAD_DIM, (j + 1) * HEAD_DIM)
            i = start // HEAD_DIM + j
            stats[i : i + 1, :] = row_sums(square[part])
            stats[blocks + i : blocks + i + 1, :] = row_sums(cross[part])


def norm_kernel(width, n_stats, mixed, q, g, *refs):
    stat_refs, (out, gm, own, oth) = refs[:n_stats], refs[n_stats:]
    total = stat_refs[0][...]
    for r in stat_refs[1:]:
        total = total + r[...]
    blocks = q.shape[0] // HEAD_DIM
    inverse = lax.rsqrt(total[:blocks] / width + EPSILON)
    cross_mean = total[blocks:] * inverse / width
    scale = inverse * inverse * cross_mean
    shape = (HEAD_DIM, HEAD_DIM)
    for i in range(blocks):
        at = slice(i * HEAD_DIM, (i + 1) * HEAD_DIM)
        a = jnp.broadcast_to(inverse[i : i + 1], shape).T
        b = jnp.broadcast_to(scale[i : i + 1], shape).T
        for h in range(q.shape[1] // HEAD_DIM):
            cols = slice(h * HEAD_DIM, (h + 1) * HEAD_DIM)
            m = mixed[at, cols]
            out[at, cols] = (m * a).astype(BF16)
            gm[at, cols] = (g[at, cols].astype(F32) * a - m * b).astype(BF16)
    pairs = [
        pair_state(q[:, p * PAIR : (p + 1) * PAIR], gm[:, p * PAIR : (p + 1) * PAIR])
        for p in range(2)
    ]
    store_halves(pairs, own, oth)


def grads_kernel(q, k, v, gm, prefix, gq, gk, gv):
    rows = q.shape[0]
    keep = causal(CHUNK)
    starts = list(range(0, rows, CHUNK))
    for h in range(q.shape[1] // HEAD_DIM):
        cols = slice(h * HEAD_DIM, (h + 1) * HEAD_DIM)
        first = prefix[cols, :]
        sums = None
        states = []
        for start in starts[:-1]:
            at = slice(start, start + CHUNK)
            new = dot(k[at, cols], v[at, cols], 0, 0)
            sums = new if sums is None else sums + new
            states.append(sums.astype(BF16))
        after = None
        for n, start in reversed(list(enumerate(starts))):
            at = slice(start, start + CHUNK)
            qi, ki, vi, gi = q[at, cols], k[at, cols], v[at, cols], gm[at, cols]
            scores = jnp.where(keep, dot(qi, ki, 1, 1), 0.0).astype(BF16)
            grad_scores = jnp.where(keep, dot(gi, vi, 1, 1), 0.0).astype(BF16)
            gq_i = dot(grad_scores, ki, 1, 0) + dot(gi, first, 1, 1)
            if n:
                gq_i = gq_i + dot(gi, states[n - 1], 1, 1)
            gk_i = dot(grad_scores, qi, 0, 0)
            gv_i = dot(scores, gi, 0, 0)
            if after is not None:
                later = after.astype(BF16)
                gk_i = gk_i + dot(vi, later, 1, 1)
                gv_i = gv_i + dot(ki, later, 1, 0)
            gq[at, cols] = gq_i.astype(BF16)
            gk[at, cols] = gk_i
            gv[at, cols] = gv_i
            if n:
                new = dot(qi, gi, 0, 0)
                after = new if after is None else after + new


def last_kernel(merge, n_parts, k, v, gk_part, gv_part, *refs):
    parts, (gk, gv) = refs[:n_parts], refs[n_parts:]
    rounded = [p.astype(BF16) for p in merge(parts)]
    for start in range(0, k.shape[0], CHUNK):
        at = slice(start, start + CHUNK)
        for h in range(k.shape[1] // HEAD_DIM):
            cols = slice(h * HEAD_DIM, (h + 1) * HEAD_DIM)
            state = rounded[h // 2][(h % 2) * HEAD_DIM : (h % 2 + 1) * HEAD_DIM]
            gk[at, cols] = (gk_part[at, cols] + dot(v[at, cols], state, 1, 1)).astype(BF16)
            gv[at, cols] = (gv_part[at, cols] + dot(k[at, cols], state, 1, 0)).astype(BF16)


def all_parts(value, axis, size):
    power = size & (size - 1) == 0
    parts = [value]
    for by in range(1, size):
        pairs = [(i, i ^ by if power else (i + by) % size) for i in range(size)]
        parts.append(lax.ppermute(value, axis, pairs))
    return parts


def shards(sizes, queries, keys, values, grad_out):
    seq, heads = sizes
    rows, cols = queries.shape
    width = cols * heads
    scan, merge = (chain_scan, chain_merge) if seq == 8 else (doubling_scan, doubling_merge)
    half = jax.ShapeDtypeStruct((PAIR, HEAD_DIM), F32)
    wide = jax.ShapeDtypeStruct((rows, cols), F32)
    narrow = jax.ShapeDtypeStruct((rows, cols), BF16)
    stats_shape = jax.ShapeDtypeStruct((2 * rows // HEAD_DIM, HEAD_DIM), F32)
    state_flops = 2 * rows * cols * HEAD_DIM
    chunk_flops = 2 * rows * cols * CHUNK

    own, oth = call(state_kernel, [half, half], [keys, values], state_flops, "local_state")
    parts = scan(own, oth, seq, False)
    (intra,) = call(
        intra_kernel, [wide], [queries, keys, values], 2 * chunk_flops + 2 * state_flops, "intra"
    )
    n = len(parts)
    mixed, stats, prefix = call(
        functools.partial(mixed_kernel, lambda r: merge(r, seq, False), n),
        [wide, stats_shape, jax.ShapeDtypeStruct((cols, HEAD_DIM), BF16)],
        [intra, queries, grad_out, *parts],
        state_flops,
        "mixed",
    )
    stats_parts = all_parts(stats, "head", heads)
    output, grad_mixed, own, oth = call(
        functools.partial(norm_kernel, width, len(stats_parts)),
        [narrow, narrow, half, half],
        [mixed, queries, grad_out, *stats_parts],
        state_flops,
        "norm",
    )
    parts = scan(own, oth, seq, True)
    grad_q, gk_part, gv_part = call(
        grads_kernel,
        [narrow, wide, wide],
        [queries, keys, values, grad_mixed, prefix],
        5 * chunk_flops + 6 * state_flops,
        "grads",
    )
    grad_k, grad_v = call(
        functools.partial(last_kernel, lambda r: merge(r, seq, True), n),
        [narrow, narrow],
        [keys, values, gk_part, gv_part, *parts],
        2 * state_flops,
        "last",
    )
    return output, grad_q, grad_k, grad_v


def solution(mesh):
    sizes = (mesh.shape["seq"], mesh.shape["head"])
    spec = P("seq", "head")
    return jax.shard_map(
        functools.partial(shards, sizes),
        mesh=mesh,
        in_specs=(spec,) * 4,
        out_specs=(spec,) * 4,
        check_vma=False,
    )
```

```python
import functools

import jax
import jax.numpy as jnp
from jax import lax
from jax.experimental import pallas as pl
from jax.experimental.pallas import tpu as pltpu
from jax.sharding import PartitionSpec as P

HEAD_DIM = 128
EPSILON = 1e-06
CHUNK = 256
PAIR = 2 * HEAD_DIM
F32 = jnp.float32
BF16 = jnp.bfloat16


def dot(a, b, ca, cb):
    return lax.dot_general(a, b, (((ca,), (cb,)), ((), ())), preferred_element_type=F32)


def causal(count):
    rows = lax.broadcasted_iota(jnp.int32, (count, count), 0)
    cols = lax.broadcasted_iota(jnp.int32, (count, count), 1)
    return rows >= cols


def call(body, out_shape, args, flops, name, spaces=None, outs=None, scratch=(), limit=20):
    size = sum(a.size * a.dtype.itemsize for a in args)
    size += sum(a.size * a.dtype.itemsize for a in out_shape)
    spaces, outs = spaces or {}, outs or {}
    kernel = pl.pallas_call(
        body,
        out_shape=out_shape,
        in_specs=[
            pl.BlockSpec(memory_space=spaces.get(i, pltpu.VMEM)) for i in range(len(args))
        ],
        out_specs=[
            pl.BlockSpec(memory_space=outs.get(i, pltpu.VMEM)) for i in range(len(out_shape))
        ],
        scratch_shapes=list(scratch),
        compiler_params=pltpu.CompilerParams(vmem_limit_bytes=limit * 2**20),
        cost_estimate=pl.CostEstimate(flops=flops, bytes_accessed=size, transcendentals=0),
        name=name,
    )
    return list(kernel(*args))


def exchange(value, size, by):
    return lax.ppermute(value, "seq", [(i, i ^ by) for i in range(size)])


def sum_kernel(*refs):
    parts, out = refs[:4], refs[-1]
    out[...] = (parts[0][...] + parts[1][...]) + (parts[2][...] + parts[3][...])


def quad_scan(state, size, between):
    near = [exchange(state, size, by) for by in (3, 2, 1)]
    done = between(None)
    (total,) = call(
        sum_kernel,
        [jax.ShapeDtypeStruct(state.shape, F32)],
        [state, *near, *done[:1]],
        0,
        "quad_sum",
        spaces={4: pl.ANY},
    )
    far = exchange(total, size, 4)
    done = done + between(total)
    return near + [far], done


def quad_merge(refs, size, reverse):
    place = lax.axis_index("seq")
    if reverse:
        place = size - 1 - place
    inner = lax.rem(place, 4)
    zero = jnp.zeros(refs[0].shape, F32)
    total = jnp.where(place >= 4, refs[3][...], zero)
    for ref, by in zip(refs, (3, 2, 1)):
        total = total + jnp.where((inner ^ by) < inner, ref[...], zero)
    return total.astype(BF16)


def doubling_scan(state, size, reverse):
    def shift(value, by):
        pairs = [(i, i + by) for i in range(size - by)]
        if reverse:
            pairs = [(b, a) for a, b in pairs]
        return lax.ppermute(value, "seq", pairs)

    by = 1
    while by < size:
        state = state + shift(state, by)
        by *= 2
    return [shift(state, 1)]


def scan(state, size, reverse, between):
    if size == 8:
        return quad_scan(state, size, between)
    done = between(None)
    return doubling_scan(state, size, reverse), done + between(done[0])


def merge(refs, size, reverse):
    if size == 8:
        return quad_merge(refs, size, reverse)
    return refs[0][...].astype(BF16)


def state_kernel(k_hbm, v_hbm, state, k, v, sems):
    rows = k.shape[0]
    starts = range(0, rows, CHUNK)
    copies = []
    for n, start in enumerate(starts):
        at = slice(start, start + CHUNK)
        for j, (src, dst) in enumerate(((k_hbm, k), (v_hbm, v))):
            copies.append(pltpu.make_async_copy(src.at[at], dst.at[at], sems.at[j, n]))
            copies[-1].start()
    pairs = k.shape[1] // PAIR
    sums = [None] * pairs
    for n, start in enumerate(starts):
        at = slice(start, start + CHUNK)
        copies[2 * n].wait()
        copies[2 * n + 1].wait()
        for p in range(pairs):
            cols = slice(p * PAIR, (p + 1) * PAIR)
            new = dot(k[at, cols], v[at, cols], 0, 0)
            sums[p] = new if sums[p] is None else sums[p] + new
    for p in range(pairs):
        store_pair(state, p, sums[p])


def store_pair(state, p, full):
    state[p * PAIR : p * PAIR + HEAD_DIM, :] = full[:HEAD_DIM, :HEAD_DIM]
    state[p * PAIR + HEAD_DIM : (p + 1) * PAIR, :] = full[HEAD_DIM:, HEAD_DIM:]


def intra_kernel(q, k, v, intra):
    rows = q.shape[0]
    keep = causal(CHUNK)
    for h in range(q.shape[1] // HEAD_DIM):
        cols = slice(h * HEAD_DIM, (h + 1) * HEAD_DIM)
        state = None
        for start in range(0, rows, CHUNK):
            at = slice(start, start + CHUNK)
            qi, ki, vi = q[at, cols], k[at, cols], v[at, cols]
            scores = jnp.where(keep, dot(qi, ki, 1, 1), 0.0).astype(BF16)
            out = dot(scores, vi, 1, 0)
            if state is not None:
                out = out + dot(qi, state.astype(BF16), 1, 0)
            intra[at, cols] = out
            if start + CHUNK < rows:
                new = dot(ki, vi, 0, 0)
                state = new if state is None else state + new


def row_sums(tile):
    return jnp.sum(tile.T, axis=0, keepdims=True)


def mixed_kernel(merge, n_parts, intra, q, g, *refs):
    parts, (mixed, stats, prefix) = refs[:n_parts], refs[n_parts:]
    prefix[...] = merge(parts)
    heads = q.shape[1] // HEAD_DIM
    blocks = q.shape[0] // HEAD_DIM
    for start in range(0, q.shape[0], CHUNK):
        at = slice(start, start + CHUNK)
        square = cross = None
        for h in range(heads):
            cols = slice(h * HEAD_DIM, (h + 1) * HEAD_DIM)
            m = intra[at, cols] + dot(q[at, cols], prefix[cols, :], 1, 0)
            mixed[at, cols] = m
            s, c = m * m, m * g[at, cols].astype(F32)
            square = s if square is None else square + s
            cross = c if cross is None else cross + c
        for j in range(CHUNK // HEAD_DIM):
            part = slice(j * HEAD_DIM, (j + 1) * HEAD_DIM)
            i = start // HEAD_DIM + j
            stats[i : i + 1, :] = row_sums(square[part])
            stats[blocks + i : blocks + i + 1, :] = row_sums(cross[part])


def norm_kernel(width, n_stats, mixed, q, g, *refs):
    stat_refs, (gm, state, inverse_out) = refs[:n_stats], refs[n_stats:]
    total = stat_refs[0][...]
    for r in stat_refs[1:]:
        total = total + r[...]
    blocks = q.shape[0] // HEAD_DIM
    inverse = lax.rsqrt(total[:blocks] / width + EPSILON)
    inverse_out[...] = inverse
    cross_mean = total[blocks:] * inverse / width
    scale = inverse * inverse * cross_mean
    shape = (HEAD_DIM, HEAD_DIM)
    for i in range(blocks):
        at = slice(i * HEAD_DIM, (i + 1) * HEAD_DIM)
        a = jnp.broadcast_to(inverse[i : i + 1], shape).T
        b = jnp.broadcast_to(scale[i : i + 1], shape).T
        for h in range(q.shape[1] // HEAD_DIM):
            cols = slice(h * HEAD_DIM, (h + 1) * HEAD_DIM)
            m = mixed[at, cols]
            gm[at, cols] = (g[at, cols].astype(F32) * a - m * b).astype(BF16)
    for p in range(q.shape[1] // PAIR):
        cols = slice(p * PAIR, (p + 1) * PAIR)
        store_pair(state, p, dot(q[:, cols], gm[:, cols], 0, 0))


def head_grads(heads, q, k, v, gm, prefix, gq, gk, gv):
    rows = q.shape[0]
    keep = causal(CHUNK)
    starts = list(range(0, rows, CHUNK))
    for j, h in enumerate(heads):
        cols = slice(h * HEAD_DIM, (h + 1) * HEAD_DIM)
        part = slice(j * HEAD_DIM, (j + 1) * HEAD_DIM)
        sums = prefix[cols, :].astype(F32)
        states = [prefix[cols, :]]
        for start in starts[:-1]:
            at = slice(start, start + CHUNK)
            sums = sums + dot(k[at, cols], v[at, cols], 0, 0)
            states.append(sums.astype(BF16))
        after = None
        for n, start in reversed(list(enumerate(starts))):
            at = slice(start, start + CHUNK)
            qi, ki, vi, gi = q[at, cols], k[at, cols], v[at, cols], gm[at, cols]
            scores = jnp.where(keep, dot(qi, ki, 1, 1), 0.0).astype(BF16)
            grad_scores = jnp.where(keep, dot(gi, vi, 1, 1), 0.0).astype(BF16)
            gq_i = dot(grad_scores, ki, 1, 0) + dot(gi, states[n], 1, 1)
            gk_i = dot(grad_scores, qi, 0, 0)
            gv_i = dot(scores, gi, 0, 0)
            if after is not None:
                later = after.astype(BF16)
                gk_i = gk_i + dot(vi, later, 1, 1)
                gv_i = gv_i + dot(ki, later, 1, 0)
            gq[at, part] = gq_i.astype(BF16)
            gk[at, part] = gk_i
            gv[at, part] = gv_i
            if n:
                new = dot(qi, gi, 0, 0)
                after = new if after is None else after + new


def first_grads_kernel(heads, q, k, v, gm, prefix, mixed, inverse, gq, gk, gv, out):
    head_grads(heads, q, k, v, gm, prefix, gq, gk, gv)
    shape = (HEAD_DIM, HEAD_DIM)
    for i in range(q.shape[0] // HEAD_DIM):
        at = slice(i * HEAD_DIM, (i + 1) * HEAD_DIM)
        a = jnp.broadcast_to(inverse[i : i + 1, :], shape).T
        for h in range(q.shape[1] // HEAD_DIM):
            cols = slice(h * HEAD_DIM, (h + 1) * HEAD_DIM)
            out[at, cols] = (mixed[at, cols] * a).astype(BF16)


def second_grads_kernel(heads, q, k, v, gm, prefix, gq_first, token, gq, gk, gv):
    head_grads(heads, q, k, v, gm, prefix, gq.at[:, heads[0] * HEAD_DIM :], gk, gv)
    gq[:, : heads[0] * HEAD_DIM] = gq_first[...]


def last_kernel(merge, n_parts, k, v, gk0, gv0, gk1, gv1, *refs):
    parts, (gk_hbm, gv_hbm, gk, gv, sems) = refs[:n_parts], refs[n_parts:]
    suffix = merge(parts)
    heads = k.shape[1] // HEAD_DIM
    copies = []
    for n, start in enumerate(range(0, k.shape[0], CHUNK)):
        at = slice(start, start + CHUNK)
        for h in range(heads):
            cols = slice(h * HEAD_DIM, (h + 1) * HEAD_DIM)
            state = suffix[cols]
            first = h < heads // 2
            part = cols if first else slice(cols.start - gk0.shape[1], cols.stop - gk0.shape[1])
            gk_part, gv_part = (gk0, gv0) if first else (gk1, gv1)
            gk[at, cols] = (gk_part[at, part] + dot(v[at, cols], state, 1, 1)).astype(BF16)
            gv[at, cols] = (gv_part[at, part] + dot(k[at, cols], state, 1, 0)).astype(BF16)
        for j, (src, dst) in enumerate(((gk, gk_hbm), (gv, gv_hbm))):
            copies.append(pltpu.make_async_copy(src.at[at], dst.at[at], sems.at[j, n]))
            copies[-1].start()
    for copy in copies:
        copy.wait()


def all_parts(value, axis, size):
    power = size & (size - 1) == 0
    parts = [value]
    for by in reversed(range(1, size)):
        pairs = [(i, i ^ by if power else (i + by) % size) for i in range(size)]
        parts.append(lax.ppermute(value, axis, pairs))
    return parts


def shards(sizes, queries, keys, values, grad_out):
    seq, head_size = sizes
    rows, cols = queries.shape
    heads = list(range(cols // HEAD_DIM))
    halves = heads[: len(heads) // 2], heads[len(heads) // 2 :]
    chunks = rows // CHUNK
    width = cols * head_size
    state_shape = jax.ShapeDtypeStruct((cols, HEAD_DIM), F32)
    wide = jax.ShapeDtypeStruct((rows, cols), F32)
    narrow = jax.ShapeDtypeStruct((rows, cols), BF16)
    half_wide = jax.ShapeDtypeStruct((rows, cols // 2), F32)
    half_narrow = jax.ShapeDtypeStruct((rows, cols // 2), BF16)
    stats_shape = jax.ShapeDtypeStruct((2 * rows // HEAD_DIM, HEAD_DIM), F32)
    inverse_shape = jax.ShapeDtypeStruct((rows // HEAD_DIM, HEAD_DIM), F32)
    state_flops = 2 * rows * cols * HEAD_DIM
    chunk_flops = 2 * rows * cols * CHUNK
    slots = [pltpu.VMEM((rows, cols), BF16)] * 2 + [pltpu.SemaphoreType.DMA((2, chunks))]

    (state,) = call(
        state_kernel,
        [state_shape],
        [keys, values],
        state_flops,
        "local_state",
        spaces={0: pl.ANY, 1: pl.ANY},
        scratch=slots,
        limit=60,
    )

    def forward(token):
        if token is not None:
            return []
        return call(
            intra_kernel,
            [wide],
            [queries, keys, values],
            2 * chunk_flops + 2 * state_flops,
            "intra",
        )

    parts, (intra,) = scan(state, seq, False, forward)
    n = len(parts)
    mixed, stats, prefix = call(
        functools.partial(mixed_kernel, lambda r: merge(r, seq, False), n),
        [wide, stats_shape, jax.ShapeDtypeStruct((cols, HEAD_DIM), BF16)],
        [intra, queries, grad_out, *parts],
        state_flops,
        "mixed",
    )
    stats_parts = all_parts(stats, "head", head_size)
    grad_mixed, state, inverse = call(
        functools.partial(norm_kernel, width, len(stats_parts)),
        [narrow, state_shape, inverse_shape],
        [mixed, queries, grad_out, *stats_parts],
        state_flops,
        "norm",
    )
    grads_args = [queries, keys, values, grad_mixed, prefix]
    grads_flops = (5 * chunk_flops + 6 * state_flops) // 2
    first = []

    def backward(token):
        if token is None:
            first.extend(
                call(
                    functools.partial(first_grads_kernel, halves[0]),
                    [half_narrow, half_wide, half_wide, narrow],
                    grads_args + [mixed, inverse],
                    grads_flops,
                    "first_grads",
                )
            )
            return first[1:3] + first[3:]
        return call(
            functools.partial(second_grads_kernel, halves[1]),
            [narrow, half_wide, half_wide],
            grads_args + [first[0], token],
            grads_flops,
            "second_grads",
            spaces={6: pl.ANY},
        )

    parts, (gk0, gv0, output, grad_q, gk1, gv1) = scan(state, seq, True, backward)
    grad_k, grad_v = call(
        functools.partial(last_kernel, lambda r: merge(r, seq, True), n),
        [narrow, narrow],
        [keys, values, gk0, gv0, gk1, gv1, *parts],
        2 * state_flops,
        "last",
        outs={0: pl.ANY, 1: pl.ANY},
        scratch=slots,
    )
    return output, grad_q, grad_k, grad_v


def solution(mesh):
    sizes = (mesh.shape["seq"], mesh.shape["head"])
    spec = P("seq", "head")
    return jax.shard_map(
        functools.partial(shards, sizes),
        mesh=mesh,
        in_specs=(spec,) * 4,
        out_specs=(spec,) * 4,
        check_vma=False,
    )
```

```python
import functools

import jax
import jax.numpy as jnp
from jax import lax
from jax.experimental import pallas as pl
from jax.experimental.pallas import tpu as pltpu
from jax.sharding import PartitionSpec as P

HEAD_DIM = 128
EPSILON = 1e-06
CHUNK = 256
PAIR = 2 * HEAD_DIM
F32 = jnp.float32
BF16 = jnp.bfloat16


def dot(a, b, ca, cb):
    return lax.dot_general(a, b, (((ca,), (cb,)), ((), ())), preferred_element_type=F32)


def causal(count):
    rows = lax.broadcasted_iota(jnp.int32, (count, count), 0)
    cols = lax.broadcasted_iota(jnp.int32, (count, count), 1)
    return rows >= cols


def call(body, out_shape, args, flops, name, spaces=None, outs=None, scratch=(), limit=20):
    size = sum(a.size * a.dtype.itemsize for a in args)
    size += sum(a.size * a.dtype.itemsize for a in out_shape)
    spaces, outs = spaces or {}, outs or {}
    kernel = pl.pallas_call(
        body,
        out_shape=out_shape,
        in_specs=[
            pl.BlockSpec(memory_space=spaces.get(i, pltpu.VMEM)) for i in range(len(args))
        ],
        out_specs=[
            pl.BlockSpec(memory_space=outs.get(i, pltpu.VMEM)) for i in range(len(out_shape))
        ],
        scratch_shapes=list(scratch),
        compiler_params=pltpu.CompilerParams(vmem_limit_bytes=limit * 2**20),
        cost_estimate=pl.CostEstimate(flops=flops, bytes_accessed=size, transcendentals=0),
        name=name,
    )
    return list(kernel(*args))


def exchange(value, size, by):
    return lax.ppermute(value, "seq", [(i, i ^ by) for i in range(size)])


def place_of(size, reverse):
    place = lax.axis_index("seq")
    return size - 1 - place if reverse else place


def window_kernel(own, near3, near2, near1, *refs):
    outs = refs[-2:]
    total = (own[...] + near1[...]) + (near2[...] + near3[...])
    for n, out in enumerate(outs):
        out[...] = total[n * HEAD_DIM : (n + 1) * HEAD_DIM]


def finish_kernel(size, reverse, n, own, near3, near2, near1, far, *refs):
    mine, theirs = refs[-2:]
    place = place_of(size, reverse)
    at = slice(n * HEAD_DIM, (n + 1) * HEAD_DIM)
    zero = jnp.zeros(far.shape, F32)
    before = jnp.where(place >= 4, far[...], zero)
    before = before + jnp.where(lax.rem(place, 4) >= 2, near2[at] + near3[at], zero)
    second = lax.rem(place, 2) == 1
    mine[...] = before + jnp.where(second, near1[at], zero)
    theirs[...] = before + jnp.where(second, zero, own[at])


def quad_scan(halves, size, reverse, between):
    own, oth = halves
    half = jax.ShapeDtypeStruct(own.shape, F32)
    head = jax.ShapeDtypeStruct((HEAD_DIM, HEAD_DIM), F32)
    near = [exchange(v, size, by) for v, by in ((oth, 3), (own, 2), (oth, 1))]
    done = between(None)
    pieces = call(
        window_kernel,
        [head, head],
        [own, *near, done[0]],
        0,
        "quad_sum",
        spaces={4: pl.ANY},
    )
    far = [exchange(piece, size, 4) for piece in pieces]
    later = between(pieces[1])
    mine, theirs = [], []
    for n in range(2):
        a, b = call(
            functools.partial(finish_kernel, size, reverse, n),
            [head, head],
            [own, *near, far[n], *later[-1:]],
            0,
            "finish",
            spaces={5: pl.ANY},
        )
        mine.append(a)
        theirs.append(exchange(b, size, 1))
    return mine + theirs, done + later


def quad_merge(refs, size, reverse):
    odd = lax.rem(lax.axis_index("seq"), 2) == 1
    mine, theirs = [r[...] for r in refs[:2]], [r[...] for r in refs[2:]]
    heads = [jnp.where(odd, b, a) for a, b in zip(mine, theirs)]
    heads += [jnp.where(odd, a, b) for a, b in zip(mine, theirs)]
    return jnp.concatenate(heads, axis=0).astype(BF16)


def doubling_scan(halves, size, reverse):
    def shift(value, by):
        pairs = [(i, i + by) for i in range(size - by)]
        if reverse:
            pairs = [(b, a) for a, b in pairs]
        return lax.ppermute(value, "seq", pairs)

    odd = lax.rem(lax.axis_index("seq"), 2) == 1
    own, oth = halves
    state = jnp.concatenate([jnp.where(odd, oth, own), jnp.where(odd, own, oth)], axis=0)
    by = 1
    while by < size:
        state = state + shift(state, by)
        by *= 2
    return [shift(state, 1)]


def scan(halves, size, reverse, between):
    if size == 8:
        return quad_scan(halves, size, reverse, between)
    done = between(None)
    return doubling_scan(halves, size, reverse), done + between(done[0])


def merge(refs, size, reverse):
    if size == 8:
        return quad_merge(refs, size, reverse)
    return refs[0][...].astype(BF16)


def state_kernel(k_hbm, v_hbm, own, oth, k, v, sems):
    rows = k.shape[0]
    starts = range(0, rows, CHUNK)
    copies = []
    for n, start in enumerate(starts):
        at = slice(start, start + CHUNK)
        for j, (src, dst) in enumerate(((k_hbm, k), (v_hbm, v))):
            copies.append(pltpu.make_async_copy(src.at[at], dst.at[at], sems.at[j, n]))
            copies[-1].start()
    pairs = k.shape[1] // PAIR
    sums = [None] * pairs
    for n, start in enumerate(starts):
        at = slice(start, start + CHUNK)
        copies[2 * n].wait()
        copies[2 * n + 1].wait()
        for p in range(pairs):
            cols = slice(p * PAIR, (p + 1) * PAIR)
            new = dot(k[at, cols], v[at, cols], 0, 0)
            sums[p] = new if sums[p] is None else sums[p] + new
    store_halves(sums, own, oth)


def store_halves(pairs, own, oth):
    odd = lax.rem(lax.axis_index("seq"), 2) == 1
    blocks = [
        jnp.concatenate([p[:HEAD_DIM, :HEAD_DIM], p[HEAD_DIM:, HEAD_DIM:]], axis=0) for p in pairs
    ]
    own[...] = jnp.where(odd, blocks[1], blocks[0])
    oth[...] = jnp.where(odd, blocks[0], blocks[1])


def intra_kernel(q, k, v, intra):
    rows = q.shape[0]
    keep = causal(CHUNK)
    for h in range(q.shape[1] // HEAD_DIM):
        cols = slice(h * HEAD_DIM, (h + 1) * HEAD_DIM)
        state = None
        for start in range(0, rows, CHUNK):
            at = slice(start, start + CHUNK)
            qi, ki, vi = q[at, cols], k[at, cols], v[at, cols]
            scores = jnp.where(keep, dot(qi, ki, 1, 1), 0.0).astype(BF16)
            out = dot(scores, vi, 1, 0)
            if state is not None:
                out = out + dot(qi, state.astype(BF16), 1, 0)
            intra[at, cols] = out
            if start + CHUNK < rows:
                new = dot(ki, vi, 0, 0)
                state = new if state is None else state + new


def row_sums(tile):
    return jnp.sum(tile.T, axis=0, keepdims=True)


def mixed_kernel(merge, n_parts, intra, q, g, *refs):
    parts, (mixed, stats, prefix) = refs[:n_parts], refs[n_parts:]
    prefix[...] = merge(parts)
    heads = q.shape[1] // HEAD_DIM
    blocks = q.shape[0] // HEAD_DIM
    for start in range(0, q.shape[0], CHUNK):
        at = slice(start, start + CHUNK)
        square = cross = None
        for h in range(heads):
            cols = slice(h * HEAD_DIM, (h + 1) * HEAD_DIM)
            m = intra[at, cols] + dot(q[at, cols], prefix[cols, :], 1, 0)
            mixed[at, cols] = m
            s, c = m * m, m * g[at, cols].astype(F32)
            square = s if square is None else square + s
            cross = c if cross is None else cross + c
        for j in range(CHUNK // HEAD_DIM):
            part = slice(j * HEAD_DIM, (j + 1) * HEAD_DIM)
            i = start // HEAD_DIM + j
            stats[i : i + 1, :] = row_sums(square[part])
            stats[blocks + i : blocks + i + 1, :] = row_sums(cross[part])


def norm_kernel(width, n_stats, mixed, q, g, *refs):
    stat_refs, (gm, own, oth, inverse_out) = refs[:n_stats], refs[n_stats:]
    total = stat_refs[0][...]
    for r in stat_refs[1:]:
        total = total + r[...]
    blocks = q.shape[0] // HEAD_DIM
    inverse = lax.rsqrt(total[:blocks] / width + EPSILON)
    inverse_out[...] = inverse
    cross_mean = total[blocks:] * inverse / width
    scale = inverse * inverse * cross_mean
    shape = (HEAD_DIM, HEAD_DIM)
    for i in range(blocks):
        at = slice(i * HEAD_DIM, (i + 1) * HEAD_DIM)
        a = jnp.broadcast_to(inverse[i : i + 1], shape).T
        b = jnp.broadcast_to(scale[i : i + 1], shape).T
        for h in range(q.shape[1] // HEAD_DIM):
            cols = slice(h * HEAD_DIM, (h + 1) * HEAD_DIM)
            m = mixed[at, cols]
            gm[at, cols] = (g[at, cols].astype(F32) * a - m * b).astype(BF16)
    pairs = [slice(p * PAIR, (p + 1) * PAIR) for p in range(q.shape[1] // PAIR)]
    store_halves([dot(q[:, cols], gm[:, cols], 0, 0) for cols in pairs], own, oth)


def head_grads(heads, q, k, v, gm, prefix, gq, gk, gv):
    rows = q.shape[0]
    keep = causal(CHUNK)
    starts = list(range(0, rows, CHUNK))
    for j, h in enumerate(heads):
        cols = slice(h * HEAD_DIM, (h + 1) * HEAD_DIM)
        part = slice(j * HEAD_DIM, (j + 1) * HEAD_DIM)
        sums = prefix[cols, :].astype(F32)
        states = [prefix[cols, :]]
        for start in starts[:-1]:
            at = slice(start, start + CHUNK)
            sums = sums + dot(k[at, cols], v[at, cols], 0, 0)
            states.append(sums.astype(BF16))
        after = None
        for n, start in reversed(list(enumerate(starts))):
            at = slice(start, start + CHUNK)
            qi, ki, vi, gi = q[at, cols], k[at, cols], v[at, cols], gm[at, cols]
            scores = jnp.where(keep, dot(qi, ki, 1, 1), 0.0).astype(BF16)
            grad_scores = jnp.where(keep, dot(gi, vi, 1, 1), 0.0).astype(BF16)
            gq_i = dot(grad_scores, ki, 1, 0) + dot(gi, states[n], 1, 1)
            gk_i = dot(grad_scores, qi, 0, 0)
            gv_i = dot(scores, gi, 0, 0)
            if after is not None:
                later = after.astype(BF16)
                gk_i = gk_i + dot(vi, later, 1, 1)
                gv_i = gv_i + dot(ki, later, 1, 0)
            gq[at, part] = gq_i.astype(BF16)
            gk[at, part] = gk_i
            gv[at, part] = gv_i
            if n:
                new = dot(qi, gi, 0, 0)
                after = new if after is None else after + new


def first_grads_kernel(heads, q, k, v, gm, prefix, mixed, inverse, gq, gk, gv, out):
    head_grads(heads, q, k, v, gm, prefix, gq, gk, gv)
    shape = (HEAD_DIM, HEAD_DIM)
    for i in range(q.shape[0] // HEAD_DIM):
        at = slice(i * HEAD_DIM, (i + 1) * HEAD_DIM)
        a = jnp.broadcast_to(inverse[i : i + 1, :], shape).T
        for h in range(q.shape[1] // HEAD_DIM):
            cols = slice(h * HEAD_DIM, (h + 1) * HEAD_DIM)
            out[at, cols] = (mixed[at, cols] * a).astype(BF16)


def second_grads_kernel(heads, q, k, v, gm, prefix, gq_first, token, gq, gk, gv):
    head_grads(heads, q, k, v, gm, prefix, gq.at[:, heads[0] * HEAD_DIM :], gk, gv)
    gq[:, : heads[0] * HEAD_DIM] = gq_first[...]


def last_kernel(merge, n_parts, k, v, gk0, gv0, gk1, gv1, *refs):
    parts, (gk_hbm, gv_hbm, gk, gv, sems) = refs[:n_parts], refs[n_parts:]
    suffix = merge(parts)
    heads = k.shape[1] // HEAD_DIM
    copies = []
    for n, start in enumerate(range(0, k.shape[0], CHUNK)):
        at = slice(start, start + CHUNK)
        for h in range(heads):
            cols = slice(h * HEAD_DIM, (h + 1) * HEAD_DIM)
            state = suffix[cols]
            first = h < heads // 2
            part = cols if first else slice(cols.start - gk0.shape[1], cols.stop - gk0.shape[1])
            gk_part, gv_part = (gk0, gv0) if first else (gk1, gv1)
            gk[at, cols] = (gk_part[at, part] + dot(v[at, cols], state, 1, 1)).astype(BF16)
            gv[at, cols] = (gv_part[at, part] + dot(k[at, cols], state, 1, 0)).astype(BF16)
        for j, (src, dst) in enumerate(((gk, gk_hbm), (gv, gv_hbm))):
            copies.append(pltpu.make_async_copy(src.at[at], dst.at[at], sems.at[j, n]))
            copies[-1].start()
    for copy in copies:
        copy.wait()


def all_parts(value, axis, size):
    power = size & (size - 1) == 0
    parts = [value]
    for by in reversed(range(1, size)):
        pairs = [(i, i ^ by if power else (i + by) % size) for i in range(size)]
        parts.append(lax.ppermute(value, axis, pairs))
    return parts


def shards(sizes, queries, keys, values, grad_out):
    seq, head_size = sizes
    rows, cols = queries.shape
    heads = list(range(cols // HEAD_DIM))
    halves = heads[: len(heads) // 2], heads[len(heads) // 2 :]
    chunks = rows // CHUNK
    width = cols * head_size
    half = jax.ShapeDtypeStruct((cols // 2, HEAD_DIM), F32)
    wide = jax.ShapeDtypeStruct((rows, cols), F32)
    narrow = jax.ShapeDtypeStruct((rows, cols), BF16)
    half_wide = jax.ShapeDtypeStruct((rows, cols // 2), F32)
    half_narrow = jax.ShapeDtypeStruct((rows, cols // 2), BF16)
    stats_shape = jax.ShapeDtypeStruct((2 * rows // HEAD_DIM, HEAD_DIM), F32)
    inverse_shape = jax.ShapeDtypeStruct((rows // HEAD_DIM, HEAD_DIM), F32)
    state_flops = 2 * rows * cols * HEAD_DIM
    chunk_flops = 2 * rows * cols * CHUNK
    slots = [pltpu.VMEM((rows, cols), BF16)] * 2 + [pltpu.SemaphoreType.DMA((2, chunks))]

    state = call(
        state_kernel,
        [half, half],
        [keys, values],
        state_flops,
        "local_state",
        spaces={0: pl.ANY, 1: pl.ANY},
        scratch=slots,
        limit=60,
    )

    def forward(token):
        if token is not None:
            return []
        return call(
            intra_kernel,
            [wide],
            [queries, keys, values],
            2 * chunk_flops + 2 * state_flops,
            "intra",
        )

    parts, (intra,) = scan(state, seq, False, forward)
    n = len(parts)
    mixed, stats, prefix = call(
        functools.partial(mixed_kernel, lambda r: merge(r, seq, False), n),
        [wide, stats_shape, jax.ShapeDtypeStruct((cols, HEAD_DIM), BF16)],
        [intra, queries, grad_out, *parts],
        state_flops,
        "mixed",
    )
    stats_parts = all_parts(stats, "head", head_size)
    grad_mixed, *state, inverse = call(
        functools.partial(norm_kernel, width, len(stats_parts)),
        [narrow, half, half, inverse_shape],
        [mixed, queries, grad_out, *stats_parts],
        state_flops,
        "norm",
    )
    grads_args = [queries, keys, values, grad_mixed, prefix]
    grads_flops = (5 * chunk_flops + 6 * state_flops) // 2
    first = []

    def backward(token):
        if token is None:
            first.extend(
                call(
                    functools.partial(first_grads_kernel, halves[0]),
                    [half_narrow, half_wide, half_wide, narrow],
                    grads_args + [mixed, inverse],
                    grads_flops,
                    "first_grads",
                )
            )
            return first[1:3] + first[3:]
        return call(
            functools.partial(second_grads_kernel, halves[1]),
            [narrow, half_wide, half_wide],
            grads_args + [first[0], token],
            grads_flops,
            "second_grads",
            spaces={6: pl.ANY},
        )

    parts, (gk0, gv0, output, grad_q, gk1, gv1) = scan(state, seq, True, backward)
    grad_k, grad_v = call(
        functools.partial(last_kernel, lambda r: merge(r, seq, True), n),
        [narrow, narrow],
        [keys, values, gk0, gv0, gk1, gv1, *parts],
        2 * state_flops,
        "last",
        outs={0: pl.ANY, 1: pl.ANY},
        scratch=slots,
    )
    return output, grad_q, grad_k, grad_v


def solution(mesh):
    sizes = (mesh.shape["seq"], mesh.shape["head"])
    spec = P("seq", "head")
    return jax.shard_map(
        functools.partial(shards, sizes),
        mesh=mesh,
        in_specs=(spec,) * 4,
        out_specs=(spec,) * 4,
        check_vma=False,
    )
```

```python
import functools

import jax
import jax.numpy as jnp
from jax import lax
from jax.experimental import pallas as pl
from jax.experimental.pallas import tpu as pltpu
from jax.sharding import PartitionSpec as P

HEAD_DIM = 128
EPSILON = 1e-06
CHUNK = 256
PAIR = 2 * HEAD_DIM
F32 = jnp.float32
BF16 = jnp.bfloat16


def dot(a, b, ca, cb):
    return lax.dot_general(a, b, (((ca,), (cb,)), ((), ())), preferred_element_type=F32)


def columns(own, head=0, count=1):
    odd = lax.rem(lax.axis_index("seq"), 2)
    side = odd if own else 1 - odd
    start = pl.multiple_of(side * PAIR + head * HEAD_DIM, HEAD_DIM)
    return pl.ds(start, count * HEAD_DIM)


def causal(count):
    rows = lax.broadcasted_iota(jnp.int32, (count, count), 0)
    cols = lax.broadcasted_iota(jnp.int32, (count, count), 1)
    return rows >= cols


def call(
    body, out_shape, args, flops, name, spaces=None, outs=None, scratch=(), limit=20, aliases=None
):
    size = sum(a.size * a.dtype.itemsize for a in args)
    size += sum(a.size * a.dtype.itemsize for a in out_shape)
    spaces, outs = spaces or {}, outs or {}
    kernel = pl.pallas_call(
        body,
        out_shape=out_shape,
        in_specs=[
            pl.BlockSpec(memory_space=spaces.get(i, pltpu.VMEM)) for i in range(len(args))
        ],
        out_specs=[
            pl.BlockSpec(memory_space=outs.get(i, pltpu.VMEM)) for i in range(len(out_shape))
        ],
        scratch_shapes=list(scratch),
        input_output_aliases=aliases or {},
        compiler_params=pltpu.CompilerParams(vmem_limit_bytes=limit * 2**20),
        cost_estimate=pl.CostEstimate(flops=flops, bytes_accessed=size, transcendentals=0),
        name=name,
    )
    return list(kernel(*args))


def exchange(value, size, by):
    return lax.ppermute(value, "seq", [(i, i ^ by) for i in range(size)])


def place_of(size, reverse):
    place = lax.axis_index("seq")
    return size - 1 - place if reverse else place


def window_kernel(own, near3, near2, near1, *refs):
    outs = refs[-2:]
    total = (own[...] + near1[...]) + (near2[...] + near3[...])
    for n, out in enumerate(outs):
        out[...] = total[n * HEAD_DIM : (n + 1) * HEAD_DIM]


def finish_kernel(size, reverse, n, own, near3, near2, near1, far, *refs):
    mine, theirs = refs[-2:]
    place = place_of(size, reverse)
    at = slice(n * HEAD_DIM, (n + 1) * HEAD_DIM)
    zero = jnp.zeros(far.shape, F32)
    before = jnp.where(place >= 4, far[...], zero)
    before = before + jnp.where(lax.rem(place, 4) >= 2, near2[at] + near3[at], zero)
    second = lax.rem(place, 2) == 1
    mine[...] = before + jnp.where(second, near1[at], zero)
    theirs[...] = before + jnp.where(second, zero, own[at])


def quad_scan(own, oth, size, reverse, between):
    half = jax.ShapeDtypeStruct(own.shape, F32)
    head = jax.ShapeDtypeStruct((HEAD_DIM, HEAD_DIM), F32)
    near = [exchange(v, size, by) for v, by in ((oth, 3), (own, 2), (oth, 1))]
    done = between(None)
    pieces = call(
        window_kernel,
        [head, head],
        [own, *near, done[0]],
        0,
        "quad_sum",
        spaces={4: pl.ANY},
    )
    far = [exchange(piece, size, 4) for piece in pieces]
    later = between(pieces[1])
    mine, theirs = [], []
    for n in range(2):
        a, b = call(
            functools.partial(finish_kernel, size, reverse, n),
            [head, head],
            [own, *near, far[n], *later[-1:]],
            0,
            "finish",
            spaces={5: pl.ANY},
        )
        mine.append(a)
        theirs.append(exchange(b, size, 1))
    return mine + theirs, done + later


def doubling_scan(own, oth, size, reverse):
    def shift(value, by):
        pairs = [(i, i + by) for i in range(size - by)]
        if reverse:
            pairs = [(b, a) for a, b in pairs]
        return lax.ppermute(value, "seq", pairs)

    odd = lax.rem(lax.axis_index("seq"), 2) == 1
    state = jnp.stack([jnp.where(odd, oth, own), jnp.where(odd, own, oth)])
    by = 1
    while by < size:
        state = state + shift(state, by)
        by *= 2
    state = shift(state, 1)
    own, oth = jnp.where(odd, state[1], state[0]), jnp.where(odd, state[0], state[1])
    return [half[n * HEAD_DIM : (n + 1) * HEAD_DIM] for half in (own, oth) for n in range(2)]


def scan(own, oth, size, reverse, between):
    if size == 8:
        return quad_scan(own, oth, size, reverse, between)
    done = between(None)
    return doubling_scan(own, oth, size, reverse), done + between(done[0])


def state_kernel(is_own, k_hbm, v_hbm, *refs):
    state, k, v, sems = refs[-4:]
    starts = range(0, k.shape[0], CHUNK)
    cols = columns(is_own, count=2)
    copies = []
    for n, start in enumerate(starts):
        at = slice(start, start + CHUNK)
        for j, (src, dst) in enumerate(((k_hbm, k), (v_hbm, v))):
            copies.append(pltpu.make_async_copy(src.at[at, cols], dst.at[at], sems.at[j, n]))
            copies[-1].start()
    total = None
    for n, start in enumerate(starts):
        at = slice(start, start + CHUNK)
        copies[2 * n].wait()
        copies[2 * n + 1].wait()
        new = dot(k[at], v[at], 0, 0)
        total = new if total is None else total + new
    store_blocks(total, state)


def store_blocks(full, state):
    state[:HEAD_DIM] = full[:HEAD_DIM, :HEAD_DIM]
    state[HEAD_DIM:] = full[HEAD_DIM:, HEAD_DIM:]


def intra_kernel(q, k, v, intra):
    rows = q.shape[0]
    keep = causal(CHUNK)
    for h in range(q.shape[1] // HEAD_DIM):
        cols = slice(h * HEAD_DIM, (h + 1) * HEAD_DIM)
        state = None
        for start in range(0, rows, CHUNK):
            at = slice(start, start + CHUNK)
            qi, ki, vi = q[at, cols], k[at, cols], v[at, cols]
            scores = jnp.where(keep, dot(qi, ki, 1, 1), 0.0).astype(BF16)
            out = dot(scores, vi, 1, 0)
            if state is not None:
                out = out + dot(qi, state.astype(BF16), 1, 0)
            intra[at, cols] = out
            if start + CHUNK < rows:
                new = dot(ki, vi, 0, 0)
                state = new if state is None else state + new


def row_sums(tile):
    return jnp.sum(tile.T, axis=0, keepdims=True)


def mixed_kernel(is_own, intra, q, g, state0, state1, *refs):
    (mixed, stats, prefix), before = refs[-3:], refs[:-3]
    blocks = q.shape[0] // HEAD_DIM
    for j, state in enumerate((state0, state1)):
        prefix[j * HEAD_DIM : (j + 1) * HEAD_DIM] = state[...].astype(BF16)
    for start in range(0, q.shape[0], CHUNK):
        at = slice(start, start + CHUNK)
        square = cross = None
        for j in range(2):
            cols, part = columns(is_own, j), slice(j * HEAD_DIM, (j + 1) * HEAD_DIM)
            m = intra[at, cols] + dot(q[at, cols], prefix[part], 1, 0)
            mixed[at, part] = m
            s, c = m * m, m * g[at, cols].astype(F32)
            square = s if square is None else square + s
            cross = c if cross is None else cross + c
        for n in range(CHUNK // HEAD_DIM):
            part = slice(n * HEAD_DIM, (n + 1) * HEAD_DIM)
            for first, value in ((0, square), (blocks, cross)):
                i = first + start // HEAD_DIM + n
                sums = row_sums(value[part])
                stats[i : i + 1] = sums + before[0][i : i + 1] if before else sums


def half_norm(is_own, inverse, scale, mixed, q, g, gm, state):
    shape = (HEAD_DIM, HEAD_DIM)
    for i in range(q.shape[0] // HEAD_DIM):
        at = slice(i * HEAD_DIM, (i + 1) * HEAD_DIM)
        a = jnp.broadcast_to(inverse[i : i + 1], shape).T
        b = jnp.broadcast_to(scale[i : i + 1], shape).T
        for j in range(2):
            part = slice(j * HEAD_DIM, (j + 1) * HEAD_DIM)
            value = g[at, columns(is_own, j)].astype(F32) * a - mixed[at, part] * b
            gm[at, part] = value.astype(BF16)
    store_blocks(dot(q[:, columns(is_own, count=2)], gm[...], 0, 0), state)


def first_norm_kernel(width, mixed, q, g, *refs):
    stats, (gm, state, inverse_out, scale_out) = refs[:-4], refs[-4:]
    total = stats[0][...]
    for r in stats[1:]:
        total = total + r[...]
    blocks = q.shape[0] // HEAD_DIM
    inverse = lax.rsqrt(total[:blocks] / width + EPSILON)
    cross_mean = total[blocks:] * inverse / width
    scale = inverse * inverse * cross_mean
    inverse_out[...] = inverse
    scale_out[...] = scale
    half_norm(False, inverse, scale, mixed, q, g, gm, state)


def second_norm_kernel(mixed, q, g, inverse, scale, gm, state):
    half_norm(True, inverse[...], scale[...], mixed, q, g, gm, state)


def head_grads(cols, part, q, k, v, gm, prefix, gq, gk, gv):
    keep = causal(CHUNK)
    starts = list(range(0, q.shape[0], CHUNK))
    sums = prefix[part].astype(F32)
    states = [prefix[part]]
    for start in starts[:-1]:
        at = slice(start, start + CHUNK)
        sums = sums + dot(k[at, cols], v[at, cols], 0, 0)
        states.append(sums.astype(BF16))
    after = None
    for n, start in reversed(list(enumerate(starts))):
        at = slice(start, start + CHUNK)
        qi, ki, vi, gi = q[at, cols], k[at, cols], v[at, cols], gm[at, part]
        scores = jnp.where(keep, dot(qi, ki, 1, 1), 0.0).astype(BF16)
        grad_scores = jnp.where(keep, dot(gi, vi, 1, 1), 0.0).astype(BF16)
        gq_i = dot(grad_scores, ki, 1, 0) + dot(gi, states[n], 1, 1)
        gk_i = dot(grad_scores, qi, 0, 0)
        gv_i = dot(scores, gi, 0, 0)
        if after is not None:
            later = after.astype(BF16)
            gk_i = gk_i + dot(vi, later, 1, 1)
            gv_i = gv_i + dot(ki, later, 1, 0)
        gq[at] = gq_i.astype(BF16)
        gk[at] = gk_i
        gv[at] = gv_i
        if n:
            new = dot(qi, gi, 0, 0)
            after = new if after is None else after + new


def first_grads_kernel(q, k, v, gm, prefix, oth_gm, oth_prefix, mixed, oth_mixed, inverse, *refs):
    gqs, gks, gvs, out = refs[:3], refs[3:6], refs[6:9], refs[9]
    for n, (is_own, j) in enumerate(((True, 0), (True, 1), (False, 0))):
        part = slice(j * HEAD_DIM, (j + 1) * HEAD_DIM)
        halves = (gm, prefix) if is_own else (oth_gm, oth_prefix)
        head_grads(columns(is_own, j), part, q, k, v, *halves, gqs[n], gks[n], gvs[n])
    shape = (HEAD_DIM, HEAD_DIM)
    for i in range(q.shape[0] // HEAD_DIM):
        at = slice(i * HEAD_DIM, (i + 1) * HEAD_DIM)
        a = jnp.broadcast_to(inverse[i : i + 1], shape).T
        for is_own, value in ((True, mixed), (False, oth_mixed)):
            for j in range(2):
                part = slice(j * HEAD_DIM, (j + 1) * HEAD_DIM)
                out[at, columns(is_own, j)] = (value[at, part] * a).astype(BF16)


def second_grads_kernel(q, k, v, oth_gm, oth_prefix, gq0, gq1, gq2, token, gq, gk, gv):
    gq[:, columns(True, 0)] = gq0[...]
    gq[:, columns(True, 1)] = gq1[...]
    gq[:, columns(False, 0)] = gq2[...]
    cols, part = columns(False, 1), slice(HEAD_DIM, PAIR)
    head_grads(cols, part, q, k, v, oth_gm, oth_prefix, gq.at[:, cols], gk, gv)


def last_kernel(heads, k, v, *refs):
    count = len(heads)
    gk_parts, gv_parts, states = (refs[i * count : (i + 1) * count] for i in range(3))
    gk_hbm, gv_hbm, gk, gv, sems = refs[-5:]
    rounded = [state[...].astype(BF16) for state in states]
    copies = []
    for n, start in enumerate(range(0, k.shape[0], CHUNK)):
        at = slice(start, start + CHUNK)
        for i, head in enumerate(heads):
            cols, part = columns(*head), slice(i * HEAD_DIM, (i + 1) * HEAD_DIM)
            gk[at, part] = (gk_parts[i][at] + dot(v[at, cols], rounded[i], 1, 1)).astype(BF16)
            gv[at, part] = (gv_parts[i][at] + dot(k[at, cols], rounded[i], 1, 0)).astype(BF16)
        cols = columns(*heads[0], count=count)
        for j, (src, dst) in enumerate(((gk, gk_hbm), (gv, gv_hbm))):
            copies.append(pltpu.make_async_copy(src.at[at], dst.at[at, cols], sems.at[j, n]))
            copies[-1].start()
    for copy in copies:
        copy.wait()


def all_parts(value, axis, size):
    power = size & (size - 1) == 0
    parts = [value]
    for by in reversed(range(1, size)):
        pairs = [(i, i ^ by if power else (i + by) % size) for i in range(size)]
        parts.append(lax.ppermute(value, axis, pairs))
    return parts


def shards(sizes, queries, keys, values, grad_out):
    seq, head_size = sizes
    rows, cols = queries.shape
    chunks = rows // CHUNK
    blocks = rows // HEAD_DIM
    width = cols * head_size

    def shape(count, lanes, kind):
        return jax.ShapeDtypeStruct((count, lanes), kind)

    half = shape(PAIR, HEAD_DIM, F32)
    narrow = shape(rows, cols, BF16)
    half_wide, half_narrow = shape(rows, PAIR, F32), shape(rows, PAIR, BF16)
    head_wide, head_narrow = shape(rows, HEAD_DIM, F32), shape(rows, HEAD_DIM, BF16)
    head_flops = 2 * rows * HEAD_DIM * HEAD_DIM
    chunk_flops = 2 * rows * CHUNK * HEAD_DIM

    def slots(count):
        return [pltpu.VMEM((rows, count * HEAD_DIM), BF16)] * 2 + [
            pltpu.SemaphoreType.DMA((2, chunks))
        ]

    def state_of(is_own, *token):
        return call(
            functools.partial(state_kernel, is_own),
            [half],
            [keys, values, *token],
            2 * head_flops,
            "local_state",
            spaces={0: pl.ANY, 1: pl.ANY, 2: pl.ANY},
            scratch=slots(2),
            limit=63,
        )[0]

    oth_state = state_of(False)
    own_state = state_of(True, oth_state)

    def forward(token):
        if token is not None:
            return []
        return call(
            intra_kernel,
            [shape(rows, cols, F32)],
            [queries, keys, values],
            8 * (chunk_flops + head_flops),
            "intra",
        )

    (mine0, mine1, theirs0, theirs1), (intra,) = scan(own_state, oth_state, seq, False, forward)

    def mix(is_own, *args):
        return call(
            functools.partial(mixed_kernel, is_own),
            [half_wide, shape(2 * blocks, HEAD_DIM, F32), shape(PAIR, HEAD_DIM, BF16)],
            [intra, queries, grad_out, *args],
            2 * head_flops,
            "mixed",
        )

    mixed, stats, prefix = mix(True, mine0, mine1)
    oth_mixed, stats, oth_prefix = mix(False, theirs0, theirs1, stats)
    oth_gm, oth_state, inverse, scale = call(
        functools.partial(first_norm_kernel, width),
        [half_narrow, half, shape(blocks, HEAD_DIM, F32), shape(blocks, HEAD_DIM, F32)],
        [oth_mixed, queries, grad_out, *all_parts(stats, "head", head_size)],
        2 * head_flops,
        "first_norm",
    )
    gm, own_state = call(
        second_norm_kernel,
        [half_narrow, half],
        [mixed, queries, grad_out, inverse, scale],
        2 * head_flops,
        "second_norm",
    )
    grads_flops = 5 * chunk_flops + 6 * head_flops
    first = []

    def backward(token):
        if token is None:
            first.extend(
                call(
                    first_grads_kernel,
                    [head_narrow] * 3 + [head_wide] * 6 + [narrow],
                    [queries, keys, values, gm, prefix, oth_gm, oth_prefix]
                    + [mixed, oth_mixed, inverse],
                    3 * grads_flops,
                    "first_grads",
                )
            )
            return first[3:]
        return call(
            second_grads_kernel,
            [narrow, head_wide, head_wide],
            [queries, keys, values, oth_gm, oth_prefix, *first[:3], token],
            grads_flops,
            "second_grads",
            spaces={8: pl.ANY},
        )

    (mine0, mine1, theirs0, theirs1), done = scan(own_state, oth_state, seq, True, backward)
    gk_parts, gv_parts, (output, grad_q) = done[:3], done[3:6], done[6:8]
    gk_parts, gv_parts = gk_parts + done[8:9], gv_parts + done[9:]

    def last(heads, states, *before):
        picked = [(0 if is_own else 2) + j for is_own, j in heads]
        args = [keys, values]
        args += [gk_parts[i] for i in picked] + [gv_parts[i] for i in picked] + states
        return call(
            functools.partial(last_kernel, heads),
            [narrow, narrow],
            args + list(before),
            2 * len(heads) * head_flops,
            "last",
            spaces={len(args) + i: pl.ANY for i in range(len(before))},
            outs={0: pl.ANY, 1: pl.ANY},
            scratch=slots(len(heads)),
            aliases={len(args) + i: i for i in range(len(before))},
        )

    grads = last(((True, 0), (True, 1)), [mine0, mine1])
    grads = last(((False, 1),), [theirs1], *grads)
    grad_k, grad_v = last(((False, 0),), [theirs0], *grads)
    return output, grad_q, grad_k, grad_v


def solution(mesh):
    sizes = (mesh.shape["seq"], mesh.shape["head"])
    spec = P("seq", "head")
    return jax.shard_map(
        functools.partial(shards, sizes),
        mesh=mesh,
        in_specs=(spec,) * 4,
        out_specs=(spec,) * 4,
        check_vma=False,
    )
```

```python
import functools
import math

import jax
import jax.numpy as jnp
from jax import lax
from jax.experimental import pallas as pl
from jax.experimental.pallas import tpu as pltpu
from jax.sharding import PartitionSpec as P

HEAD_DIM = 128
EPSILON = 1e-06
CHUNK = 256
PAIR = 2 * HEAD_DIM
F32 = jnp.float32
BF16 = jnp.bfloat16


def dot(a, b, ca, cb):
    return lax.dot_general(a, b, (((ca,), (cb,)), ((), ())), preferred_element_type=F32)


def columns(own, head=0, count=1):
    odd = lax.rem(lax.axis_index("seq"), 2)
    side = odd if own else 1 - odd
    start = pl.multiple_of(side * PAIR + head * HEAD_DIM, HEAD_DIM)
    return pl.ds(start, count * HEAD_DIM)


def causal(count):
    rows = lax.broadcasted_iota(jnp.int32, (count, count), 0)
    cols = lax.broadcasted_iota(jnp.int32, (count, count), 1)
    return rows >= cols


def call(
    body, out_shape, args, flops, name, spaces=None, outs=None, scratch=(), limit=20, aliases=None
):
    size = sum(a.size * a.dtype.itemsize for a in args)
    size += sum(math.prod(a.shape) * a.dtype.itemsize for a in out_shape)
    spaces, outs = spaces or {}, outs or {}
    kernel = pl.pallas_call(
        body,
        out_shape=out_shape,
        in_specs=[
            pl.BlockSpec(memory_space=spaces.get(i, pltpu.VMEM)) for i in range(len(args))
        ],
        out_specs=[
            pl.BlockSpec(memory_space=outs.get(i, pltpu.VMEM)) for i in range(len(out_shape))
        ],
        scratch_shapes=list(scratch),
        input_output_aliases=aliases or {},
        compiler_params=pltpu.CompilerParams(vmem_limit_bytes=limit * 2**20),
        cost_estimate=pl.CostEstimate(flops=flops, bytes_accessed=size, transcendentals=0),
        name=name,
    )
    return list(kernel(*args))


def exchange(value, size, by):
    return lax.ppermute(value, "seq", [(i, i ^ by) for i in range(size)])


def place_of(size, reverse):
    place = lax.axis_index("seq")
    return size - 1 - place if reverse else place


def window_kernel(own, near3, near2, near1, *refs):
    outs = refs[-2:]
    total = (own[...] + near1[...]) + (near2[...] + near3[...])
    for n, out in enumerate(outs):
        out[...] = total[n * HEAD_DIM : (n + 1) * HEAD_DIM]


def finish_kernel(size, reverse, n, own, near3, near2, near1, far, *refs):
    mine, theirs = refs[-2:]
    place = place_of(size, reverse)
    at = slice(n * HEAD_DIM, (n + 1) * HEAD_DIM)
    zero = jnp.zeros(far.shape, F32)
    before = jnp.where(place >= 4, far[...], zero)
    before = before + jnp.where(lax.rem(place, 4) >= 2, near2[at] + near3[at], zero)
    second = lax.rem(place, 2) == 1
    mine[...] = before + jnp.where(second, near1[at], zero)
    theirs[...] = before + jnp.where(second, zero, own[at])


def quad_scan(own, oth, size, reverse, between):
    half = jax.ShapeDtypeStruct(own.shape, F32)
    head = jax.ShapeDtypeStruct((HEAD_DIM, HEAD_DIM), F32)
    near = [exchange(v, size, by) for v, by in ((oth, 3), (own, 2), (oth, 1))]
    done = between(None)
    pieces = call(
        window_kernel,
        [head, head],
        [own, *near, done[0]],
        0,
        "quad_sum",
        spaces={4: pl.ANY},
    )
    far = [exchange(piece, size, 4) for piece in pieces]
    later = between(pieces[1])
    mine, theirs = [], []
    for n in range(2):
        a, b = call(
            functools.partial(finish_kernel, size, reverse, n),
            [head, head],
            [own, *near, far[n], *later[-1:]],
            0,
            "finish",
            spaces={5: pl.ANY},
        )
        mine.append(a)
        theirs.append(exchange(b, size, 1))
    return mine + theirs, done + later


def doubling_scan(own, oth, size, reverse):
    def shift(value, by):
        pairs = [(i, i + by) for i in range(size - by)]
        if reverse:
            pairs = [(b, a) for a, b in pairs]
        return lax.ppermute(value, "seq", pairs)

    odd = lax.rem(lax.axis_index("seq"), 2) == 1
    state = jnp.stack([jnp.where(odd, oth, own), jnp.where(odd, own, oth)])
    by = 1
    while by < size:
        state = state + shift(state, by)
        by *= 2
    state = shift(state, 1)
    own, oth = jnp.where(odd, state[1], state[0]), jnp.where(odd, state[0], state[1])
    return [half[n * HEAD_DIM : (n + 1) * HEAD_DIM] for half in (own, oth) for n in range(2)]


def scan(own, oth, size, reverse, between):
    if size == 8:
        return quad_scan(own, oth, size, reverse, between)
    done = between(None)
    return doubling_scan(own, oth, size, reverse), done + between(done[0])


def store_halves(fulls, own, oth):
    odd = lax.rem(lax.axis_index("seq"), 2) == 1
    blocks = [
        jnp.concatenate([f[:HEAD_DIM, :HEAD_DIM], f[HEAD_DIM:, HEAD_DIM:]], axis=0) for f in fulls
    ]
    own[...] = jnp.where(odd, blocks[1], blocks[0])
    oth[...] = jnp.where(odd, blocks[0], blocks[1])


def state_kernel(k_hbm, v_hbm, own, oth, k, v, sems):
    starts = range(0, k.shape[0], CHUNK)
    copies = []
    for n, start in enumerate(starts):
        at = slice(start, start + CHUNK)
        for j, (src, dst) in enumerate(((k_hbm, k), (v_hbm, v))):
            copies.append(pltpu.make_async_copy(src.at[at], dst.at[at], sems.at[j, n]))
            copies[-1].start()
    totals = [None, None]
    for n, start in enumerate(starts):
        at = slice(start, start + CHUNK)
        copies[2 * n].wait()
        copies[2 * n + 1].wait()
        for p in range(2):
            cols = slice(p * PAIR, (p + 1) * PAIR)
            new = dot(k[at, cols], v[at, cols], 0, 0)
            totals[p] = new if totals[p] is None else totals[p] + new
    store_halves(totals, own, oth)


def intra_kernel(q, k, v, intra):
    rows = q.shape[0]
    keep = causal(CHUNK)
    for h in range(q.shape[1] // HEAD_DIM):
        cols = slice(h * HEAD_DIM, (h + 1) * HEAD_DIM)
        state = None
        for start in range(0, rows, CHUNK):
            at = slice(start, start + CHUNK)
            qi, ki, vi = q[at, cols], k[at, cols], v[at, cols]
            scores = jnp.where(keep, dot(qi, ki, 1, 1), 0.0).astype(BF16)
            out = dot(scores, vi, 1, 0)
            if state is not None:
                out = out + dot(qi, state.astype(BF16), 1, 0)
            intra[at, cols] = out
            if start + CHUNK < rows:
                new = dot(ki, vi, 0, 0)
                state = new if state is None else state + new


def row_sums(tile):
    return jnp.sum(tile.T, axis=0, keepdims=True)


def mixed_kernel(is_own, intra, q, g, state0, state1, *refs):
    (mixed, stats, prefix), before = refs[-3:], refs[:-3]
    blocks = q.shape[0] // HEAD_DIM
    for j, state in enumerate((state0, state1)):
        prefix[j * HEAD_DIM : (j + 1) * HEAD_DIM] = state[...].astype(BF16)
    for start in range(0, q.shape[0], CHUNK):
        at = slice(start, start + CHUNK)
        square = cross = None
        for j in range(2):
            cols, part = columns(is_own, j), slice(j * HEAD_DIM, (j + 1) * HEAD_DIM)
            m = intra[at, cols] + dot(q[at, cols], prefix[part], 1, 0)
            mixed[at, part] = m
            s, c = m * m, m * g[at, cols].astype(F32)
            square = s if square is None else square + s
            cross = c if cross is None else cross + c
        for n in range(CHUNK // HEAD_DIM):
            part = slice(n * HEAD_DIM, (n + 1) * HEAD_DIM)
            for first, value in ((0, square), (blocks, cross)):
                i = first + start // HEAD_DIM + n
                sums = row_sums(value[part])
                stats[i : i + 1] = sums + before[0][i : i + 1] if before else sums


def norm_kernel(width, mixed, oth_mixed, q, g, *refs):
    stats, (gm, oth_gm, own, oth, inverse_out) = refs[:-5], refs[-5:]
    total = stats[0][...]
    for r in stats[1:]:
        total = total + r[...]
    blocks = q.shape[0] // HEAD_DIM
    inverse = lax.rsqrt(total[:blocks] / width + EPSILON)
    cross_mean = total[blocks:] * inverse / width
    scale = inverse * inverse * cross_mean
    inverse_out[...] = inverse
    shape = (HEAD_DIM, HEAD_DIM)
    halves = ((False, oth_mixed, oth_gm, oth), (True, mixed, gm, own))
    for i in range(blocks):
        at = slice(i * HEAD_DIM, (i + 1) * HEAD_DIM)
        a = jnp.broadcast_to(inverse[i : i + 1], shape).T
        b = jnp.broadcast_to(scale[i : i + 1], shape).T
        for is_own, value, out, unused in halves:
            for j in range(2):
                part = slice(j * HEAD_DIM, (j + 1) * HEAD_DIM)
                grad = g[at, columns(is_own, j)].astype(F32)
                out[at, part] = (grad * a - value[at, part] * b).astype(BF16)
    for is_own, unused, out, state in halves:
        full = dot(q[:, columns(is_own, count=2)], out[...], 0, 0)
        state[:HEAD_DIM] = full[:HEAD_DIM, :HEAD_DIM]
        state[HEAD_DIM:] = full[HEAD_DIM:, HEAD_DIM:]


def head_grads(cols, part, q, k, v, gm, prefix, gq, gk, gv):
    keep = causal(CHUNK)
    starts = list(range(0, q.shape[0], CHUNK))
    sums = prefix[part].astype(F32)
    states = [prefix[part]]
    for start in starts[:-1]:
        at = slice(start, start + CHUNK)
        sums = sums + dot(k[at, cols], v[at, cols], 0, 0)
        states.append(sums.astype(BF16))
    after = None
    for n, start in reversed(list(enumerate(starts))):
        at = slice(start, start + CHUNK)
        qi, ki, vi, gi = q[at, cols], k[at, cols], v[at, cols], gm[at, part]
        scores = jnp.where(keep, dot(qi, ki, 1, 1), 0.0).astype(BF16)
        grad_scores = jnp.where(keep, dot(gi, vi, 1, 1), 0.0).astype(BF16)
        gq_i = dot(grad_scores, ki, 1, 0) + dot(gi, states[n], 1, 1)
        gk_i = dot(grad_scores, qi, 0, 0)
        gv_i = dot(scores, gi, 0, 0)
        if after is not None:
            later = after.astype(BF16)
            gk_i = gk_i + dot(vi, later, 1, 1)
            gv_i = gv_i + dot(ki, later, 1, 0)
        gq[at] = gq_i.astype(BF16)
        gk[at] = gk_i
        gv[at] = gv_i
        if n:
            new = dot(qi, gi, 0, 0)
            after = new if after is None else after + new


def first_grads_kernel(q, k, v, gm, prefix, mixed, oth_mixed, inverse, *refs):
    gqs, gks, gvs, out = refs[:2], refs[2:4], refs[4:6], refs[6]
    for j in range(2):
        part = slice(j * HEAD_DIM, (j + 1) * HEAD_DIM)
        head_grads(columns(True, j), part, q, k, v, gm, prefix, gqs[j], gks[j], gvs[j])
    shape = (HEAD_DIM, HEAD_DIM)
    for i in range(q.shape[0] // HEAD_DIM):
        at = slice(i * HEAD_DIM, (i + 1) * HEAD_DIM)
        a = jnp.broadcast_to(inverse[i : i + 1], shape).T
        for is_own, value in ((True, mixed), (False, oth_mixed)):
            for j in range(2):
                part = slice(j * HEAD_DIM, (j + 1) * HEAD_DIM)
                out[at, columns(is_own, j)] = (value[at, part] * a).astype(BF16)


def second_grads_kernel(q, k, v, gm, prefix, gq0, gq1, token, gq, *refs):
    gks, gvs = refs[:2], refs[2:]
    gq[:, columns(True, 0)] = gq0[...]
    gq[:, columns(True, 1)] = gq1[...]
    for j in range(2):
        cols, part = columns(False, j), slice(j * HEAD_DIM, (j + 1) * HEAD_DIM)
        head_grads(cols, part, q, k, v, gm, prefix, gq.at[:, cols], gks[j], gvs[j])


def last_kernel(heads, k, v, *refs):
    count = len(heads)
    gk_parts, gv_parts, states = (refs[i * count : (i + 1) * count] for i in range(3))
    gk_hbm, gv_hbm, gk, gv, sems = refs[-5:]
    rounded = [state[...].astype(BF16) for state in states]
    copies = []
    for n, start in enumerate(range(0, k.shape[0], CHUNK)):
        at = slice(start, start + CHUNK)
        for i, head in enumerate(heads):
            cols, part = columns(*head), slice(i * HEAD_DIM, (i + 1) * HEAD_DIM)
            gk[at, part] = (gk_parts[i][at] + dot(v[at, cols], rounded[i], 1, 1)).astype(BF16)
            gv[at, part] = (gv_parts[i][at] + dot(k[at, cols], rounded[i], 1, 0)).astype(BF16)
        cols = columns(*heads[0], count=count)
        for j, (src, dst) in enumerate(((gk, gk_hbm), (gv, gv_hbm))):
            copies.append(pltpu.make_async_copy(src.at[at], dst.at[at, cols], sems.at[j, n]))
            copies[-1].start()
    for copy in copies:
        copy.wait()


def all_parts(value, axis, size):
    power = size & (size - 1) == 0
    parts = [value]
    for by in reversed(range(1, size)):
        pairs = [(i, i ^ by if power else (i + by) % size) for i in range(size)]
        parts.append(lax.ppermute(value, axis, pairs))
    return parts


def shards(sizes, queries, keys, values, grad_out):
    seq, head_size = sizes
    rows, cols = queries.shape
    chunks = rows // CHUNK
    blocks = rows // HEAD_DIM
    width = cols * head_size

    def shape(count, lanes, kind):
        return jax.ShapeDtypeStruct((count, lanes), kind)

    half = shape(PAIR, HEAD_DIM, F32)
    narrow = shape(rows, cols, BF16)
    half_wide, half_narrow = shape(rows, PAIR, F32), shape(rows, PAIR, BF16)
    head_wide, head_narrow = shape(rows, HEAD_DIM, F32), shape(rows, HEAD_DIM, BF16)
    head_flops = 2 * rows * HEAD_DIM * HEAD_DIM
    chunk_flops = 2 * rows * CHUNK * HEAD_DIM

    def slots(count):
        return [pltpu.VMEM((rows, count * HEAD_DIM), BF16)] * 2 + [
            pltpu.SemaphoreType.DMA((2, chunks))
        ]

    own_state, oth_state, keys, values = call(
        state_kernel,
        [half, half, pltpu.VMEM((rows, cols), BF16), pltpu.VMEM((rows, cols), BF16)],
        [pltpu.with_memory_space_constraint(a, pltpu.HBM) for a in (keys, values)],
        4 * head_flops,
        "local_state",
        spaces={0: pltpu.HBM, 1: pltpu.HBM},
        scratch=[pltpu.SemaphoreType.DMA((2, chunks))],
    )

    def forward(token):
        if token is not None:
            return []
        return call(
            intra_kernel,
            [shape(rows, cols, F32)],
            [queries, keys, values],
            8 * (chunk_flops + head_flops),
            "intra",
        )

    (mine0, mine1, theirs0, theirs1), (intra,) = scan(own_state, oth_state, seq, False, forward)

    def mix(is_own, *args):
        return call(
            functools.partial(mixed_kernel, is_own),
            [half_wide, shape(2 * blocks, HEAD_DIM, F32), shape(PAIR, HEAD_DIM, BF16)],
            [intra, queries, grad_out, *args],
            2 * head_flops,
            "mixed",
        )

    mixed, stats, prefix = mix(True, mine0, mine1)
    oth_mixed, stats, oth_prefix = mix(False, theirs0, theirs1, stats)
    gm, oth_gm, own_state, oth_state, inverse = call(
        functools.partial(norm_kernel, width),
        [half_narrow, half_narrow, half, half, shape(blocks, HEAD_DIM, F32)],
        [mixed, oth_mixed, queries, grad_out, *all_parts(stats, "head", head_size)],
        4 * head_flops,
        "norm",
    )
    grads_flops = 2 * (5 * chunk_flops + 6 * head_flops)
    first = []

    def backward(token):
        if token is None:
            first.extend(
                call(
                    first_grads_kernel,
                    [head_narrow] * 2 + [head_wide] * 4 + [narrow],
                    [queries, keys, values, gm, prefix, mixed, oth_mixed, inverse],
                    grads_flops,
                    "first_grads",
                )
            )
            return first[2:]
        return call(
            second_grads_kernel,
            [narrow] + [head_wide] * 4,
            [queries, keys, values, oth_gm, oth_prefix, *first[:2], token],
            grads_flops,
            "second_grads",
            spaces={7: pl.ANY},
        )

    (mine0, mine1, theirs0, theirs1), done = scan(own_state, oth_state, seq, True, backward)
    gk_parts, gv_parts, (output, grad_q) = done[:2], done[2:4], done[4:6]
    gk_parts, gv_parts = gk_parts + done[6:8], gv_parts + done[8:]

    def last(heads, states, *before):
        picked = [(0 if is_own else 2) + j for is_own, j in heads]
        args = [keys, values]
        args += [gk_parts[i] for i in picked] + [gv_parts[i] for i in picked] + states
        return call(
            functools.partial(last_kernel, heads),
            [narrow, narrow],
            args + list(before),
            2 * len(heads) * head_flops,
            "last",
            spaces={len(args) + i: pl.ANY for i in range(len(before))},
            outs={0: pl.ANY, 1: pl.ANY},
            scratch=slots(len(heads)),
            aliases={len(args) + i: i for i in range(len(before))},
        )

    grads = last(((True, 0), (True, 1)), [mine0, mine1])
    grad_k, grad_v = last(((False, 0), (False, 1)), [theirs0, theirs1], *grads)
    return output, grad_q, grad_k, grad_v


def solution(mesh):
    sizes = (mesh.shape["seq"], mesh.shape["head"])
    spec = P("seq", "head")
    return jax.shard_map(
        functools.partial(shards, sizes),
        mesh=mesh,
        in_specs=(spec,) * 4,
        out_specs=(spec,) * 4,
        check_vma=False,
    )
```

```python
import functools
import math

import jax
import jax.numpy as jnp
from jax import lax
from jax.experimental import pallas as pl
from jax.experimental.pallas import tpu as pltpu
from jax.sharding import PartitionSpec as P

HEAD_DIM = 128
EPSILON = 1e-06
CHUNK = 256
PAIR = 2 * HEAD_DIM
QUAD = 4
F32 = jnp.float32
BF16 = jnp.bfloat16


def dot(a, b, ca, cb):
    return lax.dot_general(a, b, (((ca,), (cb,)), ((), ())), preferred_element_type=F32)


def head_slice(h):
    return slice(h * HEAD_DIM, (h + 1) * HEAD_DIM)


def chunk_slices(rows):
    return [slice(start, start + CHUNK) for start in range(0, rows, CHUNK)]


def causal(transposed=False):
    rows = lax.broadcasted_iota(jnp.int32, (CHUNK, CHUNK), 0)
    cols = lax.broadcasted_iota(jnp.int32, (CHUNK, CHUNK), 1)
    return cols >= rows if transposed else rows >= cols


def call(body, out_shape, args, flops, name, spaces=None, outs=None, scratch=()):
    size = sum(a.size * a.dtype.itemsize for a in args)
    size += sum(math.prod(a.shape) * a.dtype.itemsize for a in out_shape)
    spaces, outs = spaces or {}, outs or {}
    kernel = pl.pallas_call(
        body,
        out_shape=out_shape,
        in_specs=[
            pl.BlockSpec(memory_space=spaces.get(i, pltpu.VMEM)) for i in range(len(args))
        ],
        out_specs=[
            pl.BlockSpec(memory_space=outs.get(i, pltpu.VMEM)) for i in range(len(out_shape))
        ],
        scratch_shapes=list(scratch),
        compiler_params=pltpu.CompilerParams(vmem_limit_bytes=20 * 2**20),
        cost_estimate=pl.CostEstimate(flops=flops, bytes_accessed=size, transcendentals=0),
        name=name,
    )
    return list(kernel(*args))


def head_of(n):
    number = lax.rem(lax.axis_index("seq"), QUAD) ^ n
    return pl.ds(pl.multiple_of(number * HEAD_DIM, HEAD_DIM), HEAD_DIM)


def exchange(value, size, by):
    return lax.ppermute(value, "seq", [(i, i ^ by) for i in range(size)])


def quad_kernel(piece0, piece1, piece2, piece3, *refs):
    refs[-1][...] = (piece0[...] + piece1[...]) + (piece2[...] + piece3[...])


def finish_kernel(reverse, piece0, piece1, piece2, piece3, far, *refs):
    place = lax.axis_index("seq")
    number = lax.rem(place, QUAD)
    pieces = [p[...] for p in (piece0, piece1, piece2, piece3)]
    zero = jnp.zeros(far.shape, F32)
    second = place < QUAD if reverse else place >= QUAD
    before = jnp.where(second, far[...], zero)
    for to, out in enumerate(refs[-QUAD:]):
        total = before
        for n, piece in enumerate(pieces):
            ahead = (number ^ n) > (number ^ to) if reverse else (number ^ n) < (number ^ to)
            if n != to:
                total = total + jnp.where(ahead, piece, zero)
        out[...] = total


def quad_scan(pieces, size, reverse, between):
    head = jax.ShapeDtypeStruct((HEAD_DIM, HEAD_DIM), F32)
    got = {by: exchange(pieces[by], size, by) for by in (3, 2, 1)}
    pieces = [pieces[0], got[1], got[2], got[3]]
    first = between(0, None)
    (total,) = call(
        quad_kernel, [head], [*pieces, *first[-1:]], 0, "quad_sum", spaces={4: pl.ANY}
    )
    far = exchange(total, size, QUAD)
    second = between(1, total)
    finished = call(
        functools.partial(finish_kernel, reverse),
        [head] * QUAD,
        [*pieces, far, *second[-1:]],
        0,
        "finish",
        spaces={5: pl.ANY},
    )
    got = {by: exchange(finished[by], size, by) for by in (3, 2, 1)}
    third = between(2, finished[0])
    return [finished[0], got[1], got[2], got[3]], first + second + third


def doubling_scan(pieces, size, reverse, between):
    def shift(value, by):
        pairs = [(i, i + by) for i in range(size - by)]
        if reverse:
            pairs = [(b, a) for a, b in pairs]
        return lax.ppermute(value, "seq", pairs)

    def reorder(state):
        number = lax.rem(lax.axis_index("seq"), QUAD)
        return jnp.take(state, number ^ jnp.arange(QUAD), axis=0)

    state = reorder(jnp.stack(pieces))
    by = 1
    while by < size:
        state = state + shift(state, by)
        by *= 2
    state = reorder(shift(state, 1))
    done = []
    for phase in range(3):
        done += between(phase, done[-1] if done else None)
    return [state[n] for n in range(QUAD)], done


def store_pieces(states, pieces, scratch):
    for h, state in enumerate(states):
        scratch[head_slice(h), :] = state
    for n, piece in enumerate(pieces):
        piece[...] = scratch[head_of(n), :]


def load_pieces(pieces, rounded):
    for n, piece in enumerate(pieces):
        rounded[head_of(n), :] = piece[...].astype(BF16)


def pair_blocks(left, right, contract):
    blocks = []
    for p in range(right.shape[1] // PAIR):
        cols = slice(p * PAIR, (p + 1) * PAIR)
        full = dot(left[:, cols] if contract == 0 else left[cols, :], right[:, cols], contract, 0)
        blocks += [full[:HEAD_DIM, :HEAD_DIM], full[HEAD_DIM:, HEAD_DIM:]]
    return blocks


def add_all(a, b):
    return b if a is None else [x + y for x, y in zip(a, b)]


def state_kernel(k_hbm, v_hbm, *refs):
    pieces, (k, v, scratch, sems) = refs[:QUAD], refs[QUAD:]
    chunks = chunk_slices(k.shape[0])
    copies = []
    for n, at in enumerate(chunks):
        for j, (src, dst) in enumerate(((k_hbm, k), (v_hbm, v))):
            copies.append(pltpu.make_async_copy(src.at[at], dst.at[at], sems.at[j, n]))
            copies[-1].start()
    total = None
    for n, at in enumerate(chunks):
        copies[2 * n].wait()
        copies[2 * n + 1].wait()
        total = add_all(total, pair_blocks(k[at, :], v[at, :], 0))
    store_pieces(total, pieces, scratch)


def intra_kernel(q, k, v, intra, states, q_t):
    keep = causal()
    cols = q.shape[1]
    q_t[...] = q[...].T
    for h in range(cols // HEAD_DIM):
        part = head_slice(h)
        state = None
        for n, at in enumerate(chunk_slices(q.shape[0])):
            qi, ki, vi = q[at, part], k[at, part], v[at, part]
            scores = jnp.where(keep, dot(qi, ki, 1, 1), 0.0).astype(BF16)
            out = dot(scores, vi, 1, 0)
            if n:
                out = out + dot(qi, state.astype(BF16), 1, 0)
                states[(n - 1) * cols + part.start : (n - 1) * cols + part.stop, :] = state
            intra[at, part] = out
            new = dot(ki, vi, 0, 0)
            state = state + new if n else new


def row_sums(tile):
    return jnp.sum(tile.T, axis=0, keepdims=True)


def mixed_kernel(intra, q, g, *refs):
    pieces, (mixed, stats, prefix) = refs[:QUAD], refs[QUAD:]
    load_pieces(pieces, prefix)
    blocks = q.shape[0] // HEAD_DIM
    for at in chunk_slices(q.shape[0]):
        square = cross = None
        for h in range(q.shape[1] // HEAD_DIM):
            part = head_slice(h)
            m = intra[at, part] + dot(q[at, part], prefix[part, :], 1, 0)
            mixed[at, part] = m
            s, c = m * m, m * g[at, part].astype(F32)
            square = s if square is None else square + s
            cross = c if cross is None else cross + c
        for n in range(CHUNK // HEAD_DIM):
            i = at.start // HEAD_DIM + n
            stats[i : i + 1, :] = row_sums(square[head_slice(n)])
            stats[blocks + i : blocks + i + 1, :] = row_sums(cross[head_slice(n)])


def norm_kernel(width, mixed, q_t, g, *refs):
    stats, (gm, inverse_out, states, *pieces, scratch) = refs[: -4 - QUAD], refs[-4 - QUAD :]
    total = stats[0][...]
    for r in stats[1:]:
        total = total + r[...]
    rows, cols = mixed.shape
    blocks = rows // HEAD_DIM
    inverse = lax.rsqrt(total[:blocks] / width + EPSILON)
    cross_mean = total[blocks:] * inverse / width
    scale = inverse * inverse * cross_mean
    inverse_out[...] = inverse
    shape = (HEAD_DIM, HEAD_DIM)
    after = None
    for n, at in reversed(list(enumerate(chunk_slices(rows)))):
        for i in range(at.start // HEAD_DIM, at.stop // HEAD_DIM):
            block = head_slice(i)
            a = jnp.broadcast_to(inverse[i : i + 1], shape).T
            b = jnp.broadcast_to(scale[i : i + 1], shape).T
            for h in range(cols // HEAD_DIM):
                part = head_slice(h)
                grad = g[block, part].astype(F32)
                gm[block, part] = (grad * a - mixed[block, part] * b).astype(BF16)
        after = add_all(after, pair_blocks(q_t[:, at], gm[at, :], 1))
        if n:
            for h, state in enumerate(after):
                first = (n - 1) * cols + h * HEAD_DIM
                states[first : first + HEAD_DIM, :] = state
    store_pieces(after, pieces, scratch)


def head_grads(h, q, k, v, gm, prefix, states, after, gq, gk, gv):
    cols, part = q.shape[1], head_slice(h)
    keep, keep_t = causal(), causal(True)
    chunks = chunk_slices(q.shape[0])
    first = prefix[part, :].astype(F32)
    for n, at in enumerate(chunks):
        qi, ki, vi, gi = q[at, part], k[at, part], v[at, part], gm[at, part]
        scores_t = jnp.where(keep_t, dot(ki, qi, 1, 1), 0.0).astype(BF16)
        grad_scores = jnp.where(keep, dot(gi, vi, 1, 1), 0.0).astype(BF16)
        grad_scores_t = jnp.where(keep_t, dot(vi, gi, 1, 1), 0.0).astype(BF16)
        entering = first
        if n:
            entering = first + states[pl.ds((n - 1) * cols + part.start, HEAD_DIM), :]
        gq_i = dot(grad_scores, ki, 1, 0) + dot(gi, entering.astype(BF16), 1, 1)
        gk_i = dot(grad_scores_t, qi, 1, 0)
        gv_i = dot(scores_t, gi, 1, 0)
        if n < len(chunks) - 1:
            later = after[pl.ds(n * cols + part.start, HEAD_DIM), :].astype(BF16)
            gk_i = gk_i + dot(vi, later, 1, 1)
            gv_i = gv_i + dot(ki, later, 1, 0)
        gq[at, :] = gq_i.astype(BF16)
        gk[at, :] = gk_i
        gv[at, :] = gv_i


def grads_kernel(heads, q, k, v, gm, prefix, states, after, *refs):
    count = len(heads)
    outs = refs[-3 * count :]
    gqs, gks, gvs = (outs[i * count : (i + 1) * count] for i in range(3))
    for j, h in enumerate(heads):
        head_grads(h, q, k, v, gm, prefix, states, after, gqs[j], gks[j], gvs[j])


def output_kernel(mixed, inverse, *refs):
    (gqs, (out, gq)) = refs[:QUAD], refs[-2:]
    shape = (HEAD_DIM, HEAD_DIM)
    for i in range(mixed.shape[0] // HEAD_DIM):
        a = jnp.broadcast_to(inverse[i : i + 1, :], shape).T
        for h in range(mixed.shape[1] // HEAD_DIM):
            out[head_slice(i), head_slice(h)] = (
                mixed[head_slice(i), head_slice(h)] * a
            ).astype(BF16)
    for h in range(QUAD):
        gq[:, head_slice(h)] = gqs[h][...]


def last_kernel(k, v, *refs):
    gks, gvs, pieces = (refs[i * QUAD : (i + 1) * QUAD] for i in range(3))
    gk_hbm, gv_hbm, gk, gv, suffix, sems = refs[-6:]
    load_pieces(pieces, suffix)
    copies = []
    for n, at in enumerate(chunk_slices(k.shape[0])):
        for h in range(QUAD):
            part = head_slice(h)
            state = suffix[part, :]
            gk[at, part] = (gks[h][at, :] + dot(v[at, part], state, 1, 1)).astype(BF16)
            gv[at, part] = (gvs[h][at, :] + dot(k[at, part], state, 1, 0)).astype(BF16)
        for j, (src, dst) in enumerate(((gk, gk_hbm), (gv, gv_hbm))):
            copies.append(pltpu.make_async_copy(src.at[at], dst.at[at], sems.at[j, n]))
            copies[-1].start()
    for copy in copies:
        copy.wait()


def all_parts(value, axis, size):
    power = size & (size - 1) == 0
    parts = [value]
    for by in reversed(range(1, size)):
        pairs = [(i, i ^ by if power else (i + by) % size) for i in range(size)]
        parts.append(lax.ppermute(value, axis, pairs))
    return parts


def shards(sizes, queries, keys, values, grad_out):
    seq, head_size = sizes
    rows, cols = queries.shape
    chunks = rows // CHUNK
    blocks = rows // HEAD_DIM
    scan = quad_scan if seq == 2 * QUAD else doubling_scan

    def shape(count, lanes, kind=F32):
        return jax.ShapeDtypeStruct((count, lanes), kind)

    wide, narrow = shape(rows, cols), shape(rows, cols, BF16)
    head_wide, head_narrow = shape(rows, HEAD_DIM), shape(rows, HEAD_DIM, BF16)
    pieces_shape = [shape(HEAD_DIM, HEAD_DIM)] * QUAD
    states_shape = shape((chunks - 1) * cols, HEAD_DIM)
    pieces_scratch = pltpu.VMEM((cols, HEAD_DIM), F32)
    head_flops = 2 * rows * HEAD_DIM * HEAD_DIM
    chunk_flops = 2 * rows * CHUNK * HEAD_DIM

    *pieces, keys, values = call(
        state_kernel,
        pieces_shape + [pltpu.VMEM((rows, cols), BF16)] * 2,
        [pltpu.with_memory_space_constraint(a, pltpu.HBM) for a in (keys, values)],
        QUAD * head_flops,
        "local_state",
        spaces={0: pltpu.HBM, 1: pltpu.HBM},
        scratch=[pieces_scratch, pltpu.SemaphoreType.DMA((2, chunks))],
    )

    def forward(phase, token):
        if phase:
            return []
        return call(
            intra_kernel,
            [wide, states_shape, shape(cols, rows, BF16)],
            [queries, keys, values],
            QUAD * (2 * chunk_flops + 2 * head_flops),
            "intra",
        )

    prefixes, (intra, states, queries_t) = scan(pieces, seq, False, forward)
    mixed, stats, prefix = call(
        mixed_kernel,
        [wide, shape(2 * blocks, HEAD_DIM), shape(cols, HEAD_DIM, BF16)],
        [intra, queries, grad_out, *prefixes],
        QUAD * head_flops,
        "mixed",
    )
    gm, inverse, after, *pieces = call(
        functools.partial(norm_kernel, cols * head_size),
        [narrow, shape(blocks, HEAD_DIM), states_shape] + pieces_shape,
        [mixed, queries_t, grad_out, *all_parts(stats, "head", head_size)],
        QUAD * head_flops,
        "norm",
        scratch=[pieces_scratch],
    )
    gqs, gks, gvs = [], [], []

    def backward(phase, token):
        heads = ((0,), (1, 2), (3,))[phase]
        count = len(heads)
        args = [queries, keys, values, gm, prefix, states, after]
        done = call(
            functools.partial(grads_kernel, heads),
            [head_narrow] * count + [head_wide] * (2 * count),
            args + ([] if token is None else [token]),
            count * (6 * chunk_flops + 3 * head_flops),
            "grads",
            spaces={len(args): pl.ANY},
        )
        gqs.extend(done[:count])
        gks.extend(done[count : 2 * count])
        gvs.extend(done[2 * count :])
        if phase == 2:
            done += call(
                output_kernel,
                [narrow, narrow],
                [mixed, inverse, *gqs],
                0,
                "outputs",
            )
        return done

    suffixes, done = scan(pieces, seq, True, backward)
    output, grad_q = done[-2:]
    grad_k, grad_v = call(
        last_kernel,
        [narrow, narrow],
        [keys, values, *gks, *gvs, *suffixes],
        2 * QUAD * head_flops,
        "last",
        outs={0: pl.ANY, 1: pl.ANY},
        scratch=[pltpu.VMEM((rows, cols), BF16)] * 2
        + [pltpu.VMEM((cols, HEAD_DIM), BF16), pltpu.SemaphoreType.DMA((2, chunks))],
    )
    return output, grad_q, grad_k, grad_v


def solution(mesh):
    sizes = (mesh.shape["seq"], mesh.shape["head"])
    spec = P("seq", "head")
    return jax.shard_map(
        functools.partial(shards, sizes),
        mesh=mesh,
        in_specs=(spec,) * 4,
        out_specs=(spec,) * 4,
        check_vma=False,
    )
```

```python
import functools
import math

import jax
import jax.numpy as jnp
from jax import lax
from jax.experimental import pallas as pl
from jax.experimental.pallas import tpu as pltpu
from jax.sharding import PartitionSpec as P

HEAD_DIM = 128
EPSILON = 1e-06
CHUNK = 256
PAIR = 2 * HEAD_DIM
QUAD = 4
ORDER = (0, 3, 2, 1)
F32 = jnp.float32
BF16 = jnp.bfloat16


def dot(a, b, ca, cb):
    return lax.dot_general(a, b, (((ca,), (cb,)), ((), ())), preferred_element_type=F32)


def head_slice(h):
    return slice(h * HEAD_DIM, (h + 1) * HEAD_DIM)


def chunk_slices(rows):
    return [slice(start, start + CHUNK) for start in range(0, rows, CHUNK)]


def causal(transposed=False):
    rows = lax.broadcasted_iota(jnp.int32, (CHUNK, CHUNK), 0)
    cols = lax.broadcasted_iota(jnp.int32, (CHUNK, CHUNK), 1)
    return cols >= rows if transposed else rows >= cols


def call(body, out_shape, args, flops, name, spaces=None, outs=None, scratch=()):
    size = sum(a.size * a.dtype.itemsize for a in args)
    size += sum(math.prod(a.shape) * a.dtype.itemsize for a in out_shape)
    spaces, outs = spaces or {}, outs or {}
    kernel = pl.pallas_call(
        body,
        out_shape=out_shape,
        in_specs=[
            pl.BlockSpec(memory_space=spaces.get(i, pltpu.VMEM)) for i in range(len(args))
        ],
        out_specs=[
            pl.BlockSpec(memory_space=outs.get(i, pltpu.VMEM)) for i in range(len(out_shape))
        ],
        scratch_shapes=list(scratch),
        compiler_params=pltpu.CompilerParams(vmem_limit_bytes=20 * 2**20),
        cost_estimate=pl.CostEstimate(flops=flops, bytes_accessed=size, transcendentals=0),
        name=name,
    )
    return list(kernel(*args))


def head_of(n):
    number = lax.rem(lax.axis_index("seq"), QUAD) ^ n
    return pl.ds(pl.multiple_of(number * HEAD_DIM, HEAD_DIM), HEAD_DIM)


def exchange(value, size, by):
    return lax.ppermute(value, "seq", [(i, i ^ by) for i in range(size)])


def quad_kernel(piece0, piece3, piece2, piece1, *refs):
    refs[-1][...] = (piece0[...] + piece1[...]) + (piece2[...] + piece3[...])


def finish_kernel(reverse, piece0, piece3, piece2, piece1, far, *refs):
    place = lax.axis_index("seq")
    number = lax.rem(place, QUAD)
    pieces = [p[...] for p in (piece0, piece1, piece2, piece3)]
    zero = jnp.zeros(far.shape, F32)
    second = place < QUAD if reverse else place >= QUAD
    before = jnp.where(second, far[...], zero)
    for to, out in enumerate(refs[-QUAD:]):
        total = before
        for n, piece in enumerate(pieces):
            ahead = (number ^ n) > (number ^ to) if reverse else (number ^ n) < (number ^ to)
            if n != to:
                total = total + jnp.where(ahead, piece, zero)
        out[...] = total


def quad_scan(pieces, size, reverse, between):
    head = jax.ShapeDtypeStruct((HEAD_DIM, HEAD_DIM), F32)
    got = {by: exchange(pieces[by], size, by) for by in (3, 2, 1)}
    pieces = [pieces[0], got[3], got[2], got[1]]
    first = between(0, None)
    (total,) = call(
        quad_kernel, [head], [*pieces, *first[-1:]], 0, "quad_sum", spaces={4: pl.ANY}
    )
    far = exchange(total, size, QUAD)
    second = between(1, total)
    finished = call(
        functools.partial(finish_kernel, reverse),
        [head] * QUAD,
        [*pieces, far, *second[-1:]],
        0,
        "finish",
        spaces={5: pl.ANY},
    )
    got = {by: exchange(finished[by], size, by) for by in (3, 2, 1)}
    third = between(2, finished[0])
    return [finished[0], got[3], got[2], got[1]], first + second + third


def doubling_scan(pieces, size, reverse, between):
    def shift(value, by):
        pairs = [(i, i + by) for i in range(size - by)]
        if reverse:
            pairs = [(b, a) for a, b in pairs]
        return lax.ppermute(value, "seq", pairs)

    def reorder(state):
        number = lax.rem(lax.axis_index("seq"), QUAD)
        return jnp.take(state, number ^ jnp.arange(QUAD), axis=0)

    state = reorder(jnp.stack(pieces))
    by = 1
    while by < size:
        state = state + shift(state, by)
        by *= 2
    state = reorder(shift(state, 1))
    done = []
    for phase in range(3):
        done += between(phase, done[-1] if done else None)
    return [state[n] for n in ORDER], done


def store_pieces(states, pieces, scratch):
    for h, state in enumerate(states):
        scratch[head_slice(h), :] = state
    for n, piece in enumerate(pieces):
        piece[...] = scratch[head_of(n), :]


def load_pieces(pieces, rounded):
    for n, piece in zip(ORDER, pieces):
        rounded[head_of(n), :] = piece[...].astype(BF16)


def pair_blocks(left, right, contract):
    blocks = []
    for p in range(right.shape[1] // PAIR):
        cols = slice(p * PAIR, (p + 1) * PAIR)
        full = dot(left[:, cols] if contract == 0 else left[cols, :], right[:, cols], contract, 0)
        blocks += [full[:HEAD_DIM, :HEAD_DIM], full[HEAD_DIM:, HEAD_DIM:]]
    return blocks


def add_all(a, b):
    return b if a is None else [x + y for x, y in zip(a, b)]


def state_kernel(k_hbm, v_hbm, *refs):
    pieces, (k, v, scratch, sems) = refs[:QUAD], refs[QUAD:]
    chunks = chunk_slices(k.shape[0])
    copies = []
    for n, at in enumerate(chunks):
        for j, (src, dst) in enumerate(((k_hbm, k), (v_hbm, v))):
            copies.append(pltpu.make_async_copy(src.at[at], dst.at[at], sems.at[j, n]))
            copies[-1].start()
    total = None
    for n, at in enumerate(chunks):
        copies[2 * n].wait()
        copies[2 * n + 1].wait()
        total = add_all(total, pair_blocks(k[at, :], v[at, :], 0))
    store_pieces(total, pieces, scratch)


def intra_kernel(q, k, v, intra, states, q_t):
    keep = causal()
    cols = q.shape[1]
    q_t[...] = q[...].T
    for h in range(cols // HEAD_DIM):
        part = head_slice(h)
        state = None
        for n, at in enumerate(chunk_slices(q.shape[0])):
            qi, ki, vi = q[at, part], k[at, part], v[at, part]
            scores = jnp.where(keep, dot(qi, ki, 1, 1), 0.0).astype(BF16)
            out = dot(scores, vi, 1, 0)
            if n:
                out = out + dot(qi, state.astype(BF16), 1, 0)
                states[(n - 1) * cols + part.start : (n - 1) * cols + part.stop, :] = state
            intra[at, part] = out
            new = dot(ki, vi, 0, 0)
            state = state + new if n else new


def row_sums(tile):
    return jnp.sum(tile.T, axis=0, keepdims=True)


def mixed_kernel(intra, q, g, *refs):
    pieces, (mixed, stats, prefix) = refs[:QUAD], refs[QUAD:]
    load_pieces(pieces, prefix)
    blocks = q.shape[0] // HEAD_DIM
    for at in chunk_slices(q.shape[0]):
        square = cross = None
        for h in range(q.shape[1] // HEAD_DIM):
            part = head_slice(h)
            m = intra[at, part] + dot(q[at, part], prefix[part, :], 1, 0)
            mixed[at, part] = m
            s, c = m * m, m * g[at, part].astype(F32)
            square = s if square is None else square + s
            cross = c if cross is None else cross + c
        for n in range(CHUNK // HEAD_DIM):
            i = at.start // HEAD_DIM + n
            stats[i : i + 1, :] = row_sums(square[head_slice(n)])
            stats[blocks + i : blocks + i + 1, :] = row_sums(cross[head_slice(n)])


def norm_kernel(width, mixed, q_t, g, *refs):
    stats, (gm, inverse_out, states, *pieces, scratch) = refs[: -4 - QUAD], refs[-4 - QUAD :]
    total = stats[0][...]
    for r in stats[1:]:
        total = total + r[...]
    rows, cols = mixed.shape
    blocks = rows // HEAD_DIM
    inverse = lax.rsqrt(total[:blocks] / width + EPSILON)
    cross_mean = total[blocks:] * inverse / width
    scale = inverse * inverse * cross_mean
    inverse_out[...] = inverse
    shape = (HEAD_DIM, HEAD_DIM)
    after = None
    for n, at in reversed(list(enumerate(chunk_slices(rows)))):
        for i in range(at.start // HEAD_DIM, at.stop // HEAD_DIM):
            block = head_slice(i)
            a = jnp.broadcast_to(inverse[i : i + 1], shape).T
            b = jnp.broadcast_to(scale[i : i + 1], shape).T
            for h in range(cols // HEAD_DIM):
                part = head_slice(h)
                grad = g[block, part].astype(F32)
                gm[block, part] = (grad * a - mixed[block, part] * b).astype(BF16)
        after = add_all(after, pair_blocks(q_t[:, at], gm[at, :], 1))
        if n:
            for h, state in enumerate(after):
                first = (n - 1) * cols + h * HEAD_DIM
                states[first : first + HEAD_DIM, :] = state
    store_pieces(after, pieces, scratch)


def head_grads(h, q, k, v, gm, prefix, states, after, gq, gk, gv):
    cols, part = q.shape[1], head_slice(h)
    keep, keep_t = causal(), causal(True)
    chunks = chunk_slices(q.shape[0])
    first = prefix[part, :].astype(F32)
    for n, at in enumerate(chunks):
        qi, ki, vi, gi = q[at, part], k[at, part], v[at, part], gm[at, part]
        scores_t = jnp.where(keep_t, dot(ki, qi, 1, 1), 0.0).astype(BF16)
        grad_scores = jnp.where(keep, dot(gi, vi, 1, 1), 0.0).astype(BF16)
        grad_scores_t = jnp.where(keep_t, dot(vi, gi, 1, 1), 0.0).astype(BF16)
        entering = first
        if n:
            entering = first + states[pl.ds((n - 1) * cols + part.start, HEAD_DIM), :]
        gq_i = dot(grad_scores, ki, 1, 0) + dot(gi, entering.astype(BF16), 1, 1)
        gk_i = dot(grad_scores_t, qi, 1, 0)
        gv_i = dot(scores_t, gi, 1, 0)
        if n < len(chunks) - 1:
            later = after[pl.ds(n * cols + part.start, HEAD_DIM), :].astype(BF16)
            gk_i = gk_i + dot(vi, later, 1, 1)
            gv_i = gv_i + dot(ki, later, 1, 0)
        gq[at, :] = gq_i.astype(BF16)
        gk[at, :] = gk_i
        gv[at, :] = gv_i


def grads_kernel(heads, q, k, v, gm, prefix, states, after, *refs):
    count = len(heads)
    outs = refs[-3 * count :]
    gqs, gks, gvs = (outs[i * count : (i + 1) * count] for i in range(3))
    for j, h in enumerate(heads):
        head_grads(h, q, k, v, gm, prefix, states, after, gqs[j], gks[j], gvs[j])


def output_kernel(mixed, inverse, token, out, written):
    written[...] = inverse[...]
    shape = (HEAD_DIM, HEAD_DIM)
    for i in range(mixed.shape[0] // HEAD_DIM):
        a = jnp.broadcast_to(inverse[i : i + 1, :], shape).T
        for h in range(mixed.shape[1] // HEAD_DIM):
            out[head_slice(i), head_slice(h)] = (
                mixed[head_slice(i), head_slice(h)] * a
            ).astype(BF16)


def merge_kernel(*refs):
    for h in range(QUAD):
        refs[-1][:, head_slice(h)] = refs[h][...]


def last_kernel(k, v, *refs):
    gks, gvs, pieces = (refs[i * QUAD : (i + 1) * QUAD] for i in range(3))
    gk_hbm, gv_hbm, gk, gv, suffix, sems = refs[-6:]
    load_pieces(pieces, suffix)
    copies = []
    for n, at in enumerate(chunk_slices(k.shape[0])):
        for h in range(QUAD):
            part = head_slice(h)
            state = suffix[part, :]
            gk[at, part] = (gks[h][at, :] + dot(v[at, part], state, 1, 1)).astype(BF16)
            gv[at, part] = (gvs[h][at, :] + dot(k[at, part], state, 1, 0)).astype(BF16)
        for j, (src, dst) in enumerate(((gk, gk_hbm), (gv, gv_hbm))):
            copies.append(pltpu.make_async_copy(src.at[at], dst.at[at], sems.at[j, n]))
            copies[-1].start()
    for copy in copies:
        copy.wait()


def all_parts(value, axis, size):
    power = size & (size - 1) == 0
    parts = [value]
    for by in range(1, size):
        pairs = [(i, i ^ by if power else (i + by) % size) for i in range(size)]
        parts.append(lax.ppermute(value, axis, pairs))
    return parts


def shards(sizes, queries, keys, values, grad_out):
    seq, head_size = sizes
    rows, cols = queries.shape
    chunks = rows // CHUNK
    blocks = rows // HEAD_DIM
    scan = quad_scan if seq == 2 * QUAD else doubling_scan

    def shape(count, lanes, kind=F32):
        return jax.ShapeDtypeStruct((count, lanes), kind)

    wide, narrow = shape(rows, cols), shape(rows, cols, BF16)
    head_wide, head_narrow = shape(rows, HEAD_DIM), shape(rows, HEAD_DIM, BF16)
    pieces_shape = [shape(HEAD_DIM, HEAD_DIM)] * QUAD
    states_shape = shape((chunks - 1) * cols, HEAD_DIM)
    pieces_scratch = pltpu.VMEM((cols, HEAD_DIM), F32)
    head_flops = 2 * rows * HEAD_DIM * HEAD_DIM
    chunk_flops = 2 * rows * CHUNK * HEAD_DIM

    *pieces, keys, values = call(
        state_kernel,
        pieces_shape + [pltpu.VMEM((rows, cols), BF16)] * 2,
        [pltpu.with_memory_space_constraint(a, pltpu.HBM) for a in (keys, values)],
        QUAD * head_flops,
        "local_state",
        spaces={0: pltpu.HBM, 1: pltpu.HBM},
        scratch=[pieces_scratch, pltpu.SemaphoreType.DMA((2, chunks))],
    )

    def forward(phase, token):
        if phase:
            return []
        return call(
            intra_kernel,
            [wide, states_shape, shape(cols, rows, BF16)],
            [queries, keys, values],
            QUAD * (2 * chunk_flops + 2 * head_flops),
            "intra",
        )

    prefixes, (intra, states, queries_t) = scan(pieces, seq, False, forward)
    mixed, stats, prefix = call(
        mixed_kernel,
        [wide, shape(2 * blocks, HEAD_DIM), shape(cols, HEAD_DIM, BF16)],
        [intra, queries, grad_out, *prefixes],
        QUAD * head_flops,
        "mixed",
    )
    gm, inverse, after, *pieces = call(
        functools.partial(norm_kernel, cols * head_size),
        [narrow, shape(blocks, HEAD_DIM), states_shape] + pieces_shape,
        [mixed, queries_t, grad_out, *all_parts(stats, "head", head_size)],
        QUAD * head_flops,
        "norm",
        scratch=[pieces_scratch],
    )
    gqs, gks, gvs, results = [], [], [], []

    def backward(phase, token):
        heads = ((0, 1), (2,), (3,))[phase]
        count = len(heads)
        args = [queries, keys, values, gm, prefix, states, after]
        done = call(
            functools.partial(grads_kernel, heads),
            [head_narrow] * count + [head_wide] * (2 * count),
            args + ([] if token is None else [token]),
            count * (6 * chunk_flops + 3 * head_flops),
            "grads",
            spaces={len(args): pl.ANY},
        )
        gqs.extend(done[:count])
        gks.extend(done[count : 2 * count])
        gvs.extend(done[2 * count :])
        if phase == 1:
            done += call(
                output_kernel,
                [narrow, shape(blocks, HEAD_DIM)],
                [mixed, inverse, done[-1]],
                0,
                "output",
                spaces={2: pl.ANY},
            )
            results.append(done[-2])
        if phase == 2:
            done += call(merge_kernel, [narrow], gqs, 0, "grad_query")
            results.append(done[-1])
        return done

    suffixes, done = scan(pieces, seq, True, backward)
    output, grad_q = results
    grad_k, grad_v = call(
        last_kernel,
        [narrow, narrow],
        [keys, values, *gks, *gvs, *suffixes],
        2 * QUAD * head_flops,
        "last",
        outs={0: pl.ANY, 1: pl.ANY},
        scratch=[pltpu.VMEM((rows, cols), BF16)] * 2
        + [pltpu.VMEM((cols, HEAD_DIM), BF16), pltpu.SemaphoreType.DMA((2, chunks))],
    )
    return output, grad_q, grad_k, grad_v


def solution(mesh):
    sizes = (mesh.shape["seq"], mesh.shape["head"])
    spec = P("seq", "head")
    return jax.shard_map(
        functools.partial(shards, sizes),
        mesh=mesh,
        in_specs=(spec,) * 4,
        out_specs=(spec,) * 4,
        check_vma=False,
    )
```

```python
import functools
import math

import jax
import jax.numpy as jnp
from jax import lax
from jax.experimental import pallas as pl
from jax.experimental.pallas import tpu as pltpu
from jax.sharding import PartitionSpec as P

HEAD_DIM = 128
EPSILON = 1e-06
CHUNK = 256
PAIR = 2 * HEAD_DIM
QUAD = 4
ORDER = (0, 3, 2, 1)
F32 = jnp.float32
BF16 = jnp.bfloat16


def dot(a, b, ca, cb):
    return lax.dot_general(a, b, (((ca,), (cb,)), ((), ())), preferred_element_type=F32)


def head_slice(h):
    return slice(h * HEAD_DIM, (h + 1) * HEAD_DIM)


def chunk_slices(rows):
    return [slice(start, start + CHUNK) for start in range(0, rows, CHUNK)]


def causal(transposed=False):
    rows = lax.broadcasted_iota(jnp.int32, (CHUNK, CHUNK), 0)
    cols = lax.broadcasted_iota(jnp.int32, (CHUNK, CHUNK), 1)
    return cols >= rows if transposed else rows >= cols


def call(body, out_shape, args, flops, name, spaces=None, outs=None, scratch=()):
    size = sum(a.size * a.dtype.itemsize for a in args)
    size += sum(math.prod(a.shape) * a.dtype.itemsize for a in out_shape)
    spaces, outs = spaces or {}, outs or {}
    kernel = pl.pallas_call(
        body,
        out_shape=out_shape,
        in_specs=[
            pl.BlockSpec(memory_space=spaces.get(i, pltpu.VMEM)) for i in range(len(args))
        ],
        out_specs=[
            pl.BlockSpec(memory_space=outs.get(i, pltpu.VMEM)) for i in range(len(out_shape))
        ],
        scratch_shapes=list(scratch),
        compiler_params=pltpu.CompilerParams(vmem_limit_bytes=20 * 2**20),
        cost_estimate=pl.CostEstimate(flops=flops, bytes_accessed=size, transcendentals=0),
        name=name,
    )
    return list(kernel(*args))


def head_of(n):
    number = lax.rem(lax.axis_index("seq"), QUAD) ^ n
    return pl.ds(pl.multiple_of(number * HEAD_DIM, HEAD_DIM), HEAD_DIM)


def exchange(value, size, by):
    return lax.ppermute(value, "seq", [(i, i ^ by) for i in range(size)])


def quad_kernel(piece0, piece3, piece2, piece1, *refs):
    refs[-1][...] = (piece0[...] + piece1[...]) + (piece2[...] + piece3[...])


def finish_kernel(reverse, piece0, piece3, piece2, piece1, far, *refs):
    place = lax.axis_index("seq")
    number = lax.rem(place, QUAD)
    pieces = [p[...] for p in (piece0, piece1, piece2, piece3)]
    zero = jnp.zeros(far.shape, F32)
    second = place < QUAD if reverse else place >= QUAD
    before = jnp.where(second, far[...], zero)
    for to, out in enumerate(refs[-QUAD:]):
        total = before
        for n, piece in enumerate(pieces):
            ahead = (number ^ n) > (number ^ to) if reverse else (number ^ n) < (number ^ to)
            if n != to:
                total = total + jnp.where(ahead, piece, zero)
        out[...] = total


def quad_scan(pieces, size, reverse, between):
    head = jax.ShapeDtypeStruct((HEAD_DIM, HEAD_DIM), F32)
    got = {by: exchange(pieces[by], size, by) for by in (3, 2, 1)}
    pieces = [pieces[0], got[3], got[2], got[1]]
    first = between(0, None)
    (total,) = call(
        quad_kernel, [head], [*pieces, *first[-1:]], 0, "quad_sum", spaces={4: pl.ANY}
    )
    far = exchange(total, size, QUAD)
    second = between(1, total)
    finished = call(
        functools.partial(finish_kernel, reverse),
        [head] * QUAD,
        [*pieces, far, *second[-1:]],
        0,
        "finish",
        spaces={5: pl.ANY},
    )
    got = {by: exchange(finished[by], size, by) for by in (3, 2, 1)}
    third = between(2, finished[0])
    return [finished[0], got[3], got[2], got[1]], first + second + third


def doubling_scan(pieces, size, reverse, between):
    def shift(value, by):
        pairs = [(i, i + by) for i in range(size - by)]
        if reverse:
            pairs = [(b, a) for a, b in pairs]
        return lax.ppermute(value, "seq", pairs)

    def reorder(state):
        number = lax.rem(lax.axis_index("seq"), QUAD)
        return jnp.take(state, number ^ jnp.arange(QUAD), axis=0)

    state = reorder(jnp.stack(pieces))
    by = 1
    while by < size:
        state = state + shift(state, by)
        by *= 2
    state = reorder(shift(state, 1))
    done = []
    for phase in range(3):
        done += between(phase, done[-1] if done else None)
    return [state[n] for n in ORDER], done


def store_pieces(states, pieces, scratch):
    for h, state in enumerate(states):
        scratch[head_slice(h), :] = state
    for n, piece in enumerate(pieces):
        piece[...] = scratch[head_of(n), :]


def load_pieces(pieces, rounded):
    for n, piece in zip(ORDER, pieces):
        rounded[head_of(n), :] = piece[...].astype(BF16)


def pair_blocks(left, right, contract):
    blocks = []
    for p in range(right.shape[1] // PAIR):
        cols = slice(p * PAIR, (p + 1) * PAIR)
        full = dot(left[:, cols] if contract == 0 else left[cols, :], right[:, cols], contract, 0)
        blocks += [full[:HEAD_DIM, :HEAD_DIM], full[HEAD_DIM:, HEAD_DIM:]]
    return blocks


def add_all(a, b):
    return b if a is None else [x + y for x, y in zip(a, b)]


def state_kernel(k_hbm, v_hbm, *refs):
    pieces, (k, v, scratch, sems) = refs[:QUAD], refs[QUAD:]
    chunks = chunk_slices(k.shape[0])
    copies = []
    for n, at in enumerate(chunks):
        for j, (src, dst) in enumerate(((k_hbm, k), (v_hbm, v))):
            copies.append(pltpu.make_async_copy(src.at[at], dst.at[at], sems.at[j, n]))
            copies[-1].start()
    total = None
    for n, at in enumerate(chunks):
        copies[2 * n].wait()
        copies[2 * n + 1].wait()
        total = add_all(total, pair_blocks(k[at, :], v[at, :], 0))
    store_pieces(total, pieces, scratch)


def intra_kernel(q, k, v, intra, states, q_t):
    keep = causal()
    cols = q.shape[1]
    q_t[...] = q[...].T
    for h in range(cols // HEAD_DIM):
        part = head_slice(h)
        state = None
        for n, at in enumerate(chunk_slices(q.shape[0])):
            qi, ki, vi = q[at, part], k[at, part], v[at, part]
            scores = jnp.where(keep, dot(qi, ki, 1, 1), 0.0).astype(BF16)
            out = dot(scores, vi, 1, 0)
            if n:
                out = out + dot(qi, state.astype(BF16), 1, 0)
                states[(n - 1) * cols + part.start : (n - 1) * cols + part.stop, :] = state
            intra[at, part] = out
            new = dot(ki, vi, 0, 0)
            state = state + new if n else new


def row_sums(tile):
    return jnp.sum(tile.T, axis=0, keepdims=True)


def mixed_kernel(intra, q, g, *refs):
    pieces, (mixed, prefix, stats, *copies) = refs[:QUAD], refs[QUAD:]
    load_pieces(pieces, prefix)
    blocks = q.shape[0] // HEAD_DIM
    for at in chunk_slices(q.shape[0]):
        square = cross = None
        for h in range(q.shape[1] // HEAD_DIM):
            part = head_slice(h)
            m = intra[at, part] + dot(q[at, part], prefix[part, :], 1, 0)
            mixed[at, part] = m
            s, c = m * m, m * g[at, part].astype(F32)
            square = s if square is None else square + s
            cross = c if cross is None else cross + c
        for n in range(CHUNK // HEAD_DIM):
            i = at.start // HEAD_DIM + n
            stats[i : i + 1, :] = row_sums(square[head_slice(n)])
            stats[blocks + i : blocks + i + 1, :] = row_sums(cross[head_slice(n)])
    for copy in copies:
        copy[...] = stats[...]


def norm_kernel(width, mixed, q_t, g, *refs):
    stats, (gm, inverse_out, states, *pieces, scratch) = refs[: -4 - QUAD], refs[-4 - QUAD :]
    total = stats[0][...]
    for r in stats[1:]:
        total = total + r[...]
    rows, cols = mixed.shape
    blocks = rows // HEAD_DIM
    inverse = lax.rsqrt(total[:blocks] / width + EPSILON)
    cross_mean = total[blocks:] * inverse / width
    scale = inverse * inverse * cross_mean
    inverse_out[...] = inverse
    shape = (HEAD_DIM, HEAD_DIM)
    after = None
    for n, at in reversed(list(enumerate(chunk_slices(rows)))):
        for i in range(at.start // HEAD_DIM, at.stop // HEAD_DIM):
            block = head_slice(i)
            a = jnp.broadcast_to(inverse[i : i + 1], shape).T
            b = jnp.broadcast_to(scale[i : i + 1], shape).T
            for h in range(cols // HEAD_DIM):
                part = head_slice(h)
                grad = g[block, part].astype(F32)
                gm[block, part] = (grad * a - mixed[block, part] * b).astype(BF16)
        after = add_all(after, pair_blocks(q_t[:, at], gm[at, :], 1))
        if n:
            for h, state in enumerate(after):
                first = (n - 1) * cols + h * HEAD_DIM
                states[first : first + HEAD_DIM, :] = state
    store_pieces(after, pieces, scratch)


def head_grads(h, q, k, v, gm, prefix, states, after, gq, gk, gv, finished=None):
    cols, part = q.shape[1], head_slice(h)
    keep, keep_t = causal(), causal(True)
    chunks = chunk_slices(q.shape[0])
    first = prefix[part, :].astype(F32)
    for n, at in enumerate(chunks):
        qi, ki, vi, gi = q[at, part], k[at, part], v[at, part], gm[at, part]
        scores_t = jnp.where(keep_t, dot(ki, qi, 1, 1), 0.0).astype(BF16)
        grad_scores = jnp.where(keep, dot(gi, vi, 1, 1), 0.0).astype(BF16)
        grad_scores_t = jnp.where(keep_t, dot(vi, gi, 1, 1), 0.0).astype(BF16)
        entering = first
        if n:
            entering = first + states[pl.ds((n - 1) * cols + part.start, HEAD_DIM), :]
        gq_i = dot(grad_scores, ki, 1, 0) + dot(gi, entering.astype(BF16), 1, 1)
        gk_i = dot(grad_scores_t, qi, 1, 0)
        gv_i = dot(scores_t, gi, 1, 0)
        if n < len(chunks) - 1:
            later = after[pl.ds(n * cols + part.start, HEAD_DIM), :].astype(BF16)
            gk_i = gk_i + dot(vi, later, 1, 1)
            gv_i = gv_i + dot(ki, later, 1, 0)
        gq[at, :] = gq_i.astype(BF16)
        gk[at, :] = gk_i
        gv[at, :] = gv_i
        if finished is not None:
            finished(n, at)


def first_grads_kernel(q, k, v, gm, prefix, states, after, *refs):
    gqs, gks, gvs = refs[:2], refs[2:4], refs[4:]
    for h in range(2):
        head_grads(h, q, k, v, gm, prefix, states, after, gqs[h], gks[h], gvs[h])


def second_grads_kernel(q, k, v, gm, prefix, states, after, mixed, inverse, *refs):
    gq, gk, gv, out_hbm, out, sems = refs[-6:]
    shape = (HEAD_DIM, HEAD_DIM)
    copies = []
    for n, at in enumerate(chunk_slices(q.shape[0])):
        for i in range(at.start // HEAD_DIM, at.stop // HEAD_DIM):
            a = jnp.broadcast_to(inverse[i : i + 1, :], shape).T
            for h in range(q.shape[1] // HEAD_DIM):
                block = (head_slice(i), head_slice(h))
                out[block] = (mixed[block] * a).astype(BF16)
        copies.append(pltpu.make_async_copy(out.at[at], out_hbm.at[at], sems.at[n]))
        copies[-1].start()
    head_grads(2, q, k, v, gm, prefix, states, after, gq, gk, gv)
    for copy in copies:
        copy.wait()


def third_grads_kernel(q, k, v, gm, prefix, states, after, *refs):
    gqs, (gk, gv, gq_hbm, gq, sems) = refs[:3], refs[-5:]
    copies = []

    def send(src, h, at, sem):
        copies.append(pltpu.make_async_copy(src.at[at], gq_hbm.at[at, head_slice(h)], sem))
        copies[-1].start()

    for h in range(3):
        send(gqs[h], h, slice(0, q.shape[0]), sems.at[h])
    head_grads(
        3, q, k, v, gm, prefix, states, after, gq, gk, gv, lambda n, at: send(gq, 3, at, sems.at[3 + n])
    )
    for copy in copies:
        copy.wait()


def last_kernel(k, v, *refs):
    gks, gvs, pieces = (refs[i * QUAD : (i + 1) * QUAD] for i in range(3))
    gk_hbm, gv_hbm, gk, gv, suffix, sems = refs[-6:]
    load_pieces(pieces, suffix)
    copies = []
    for n, at in enumerate(chunk_slices(k.shape[0])):
        for h in range(QUAD):
            part = head_slice(h)
            state = suffix[part, :]
            gk[at, part] = (gks[h][at, :] + dot(v[at, part], state, 1, 1)).astype(BF16)
            gv[at, part] = (gvs[h][at, :] + dot(k[at, part], state, 1, 0)).astype(BF16)
        for j, (src, dst) in enumerate(((gk, gk_hbm), (gv, gv_hbm))):
            copies.append(pltpu.make_async_copy(src.at[at], dst.at[at], sems.at[j, n]))
            copies[-1].start()
    for copy in copies:
        copy.wait()


def all_parts(values, axis):
    size = len(values)
    power = size & (size - 1) == 0
    parts = [values[0]]
    for by in reversed(range(1, size)):
        pairs = [(i, i ^ by if power else (i + by) % size) for i in range(size)]
        parts.append(lax.ppermute(values[by], axis, pairs))
    return parts


def shards(sizes, queries, keys, values, grad_out):
    seq, head_size = sizes
    rows, cols = queries.shape
    chunks = rows // CHUNK
    blocks = rows // HEAD_DIM
    scan = quad_scan if seq == 2 * QUAD else doubling_scan

    def shape(count, lanes, kind=F32):
        return jax.ShapeDtypeStruct((count, lanes), kind)

    wide, narrow = shape(rows, cols), shape(rows, cols, BF16)
    head_wide, head_narrow = shape(rows, HEAD_DIM), shape(rows, HEAD_DIM, BF16)
    pieces_shape = [shape(HEAD_DIM, HEAD_DIM)] * QUAD
    states_shape = shape((chunks - 1) * cols, HEAD_DIM)
    pieces_scratch = pltpu.VMEM((cols, HEAD_DIM), F32)
    head_flops = 2 * rows * HEAD_DIM * HEAD_DIM
    chunk_flops = 2 * rows * CHUNK * HEAD_DIM

    *pieces, keys, values = call(
        state_kernel,
        pieces_shape + [pltpu.VMEM((rows, cols), BF16)] * 2,
        [pltpu.with_memory_space_constraint(a, pltpu.HBM) for a in (keys, values)],
        QUAD * head_flops,
        "local_state",
        spaces={0: pltpu.HBM, 1: pltpu.HBM},
        scratch=[pieces_scratch, pltpu.SemaphoreType.DMA((2, chunks))],
    )

    def forward(phase, token):
        if phase:
            return []
        return call(
            intra_kernel,
            [wide, states_shape, shape(cols, rows, BF16)],
            [queries, keys, values],
            QUAD * (2 * chunk_flops + 2 * head_flops),
            "intra",
        )

    prefixes, (intra, states, queries_t) = scan(pieces, seq, False, forward)
    mixed, prefix, *stats = call(
        mixed_kernel,
        [wide, shape(cols, HEAD_DIM, BF16)] + [shape(2 * blocks, HEAD_DIM)] * head_size,
        [intra, queries, grad_out, *prefixes],
        QUAD * head_flops,
        "mixed",
    )
    gm, inverse, after, *pieces = call(
        functools.partial(norm_kernel, cols * head_size),
        [narrow, shape(blocks, HEAD_DIM), states_shape] + pieces_shape,
        [mixed, queries_t, grad_out, *all_parts(stats, "head")],
        QUAD * head_flops,
        "norm",
        scratch=[pieces_scratch],
    )
    args = [queries, keys, values, gm, prefix, states, after]
    grads_flops = 6 * chunk_flops + 3 * head_flops

    def backward(phase, token):
        if phase == 0:
            parts = call(
                first_grads_kernel,
                [head_narrow] * 2 + [head_wide] * 4,
                args,
                2 * grads_flops,
                "first_grads",
            )
        elif phase == 1:
            parts = call(
                second_grads_kernel,
                [head_narrow] + [head_wide] * 2 + [narrow],
                args + [mixed, inverse, token],
                grads_flops,
                "second_grads",
                spaces={len(args) + 2: pl.ANY},
                outs={3: pl.ANY},
                scratch=[pltpu.VMEM((rows, cols), BF16), pltpu.SemaphoreType.DMA((chunks,))],
            )
        else:
            parts = call(
                third_grads_kernel,
                [head_wide] * 2 + [narrow],
                args + gqs + [token],
                grads_flops,
                "third_grads",
                spaces={len(args) + 3: pl.ANY},
                outs={2: pl.ANY},
                scratch=[
                    pltpu.VMEM((rows, HEAD_DIM), BF16),
                    pltpu.SemaphoreType.DMA((3 + chunks,)),
                ],
            )
        if phase < 2:
            count = 2 - phase
            gqs.extend(parts[:count])
            parts = parts[count:]
        count = 2 if phase == 0 else 1
        gks.extend(parts[:count])
        gvs.extend(parts[count : 2 * count])
        results.extend(parts[2 * count :])
        return gks[-1:]

    gqs, gks, gvs, results = [], [], [], []
    suffixes, unused = scan(pieces, seq, True, backward)
    output, grad_q = results
    grad_k, grad_v = call(
        last_kernel,
        [narrow, narrow],
        [keys, values, *gks, *gvs, *suffixes],
        2 * QUAD * head_flops,
        "last",
        outs={0: pl.ANY, 1: pl.ANY},
        scratch=[pltpu.VMEM((rows, cols), BF16)] * 2
        + [pltpu.VMEM((cols, HEAD_DIM), BF16), pltpu.SemaphoreType.DMA((2, chunks))],
    )
    return output, grad_q, grad_k, grad_v


def solution(mesh):
    sizes = (mesh.shape["seq"], mesh.shape["head"])
    spec = P("seq", "head")
    return jax.shard_map(
        functools.partial(shards, sizes),
        mesh=mesh,
        in_specs=(spec,) * 4,
        out_specs=(spec,) * 4,
        check_vma=False,
    )
```

```python
import functools
import math

import jax
import jax.numpy as jnp
from jax import lax
from jax.experimental import pallas as pl
from jax.experimental.pallas import tpu as pltpu
from jax.sharding import PartitionSpec as P

HEAD_DIM = 128
EPSILON = 1e-06
CHUNK = 256
PAIR = 2 * HEAD_DIM
QUAD = 4
ORDERS = {
    False: (((3, 2, 1), (3, 2, 1)), ((3, 2, 1), (3, 2, 1))),
    True: (((3, 1, 2), (3, 1, 2)), ((3, 1, 2), (3, 1, 2))),
}
F32 = jnp.float32
BF16 = jnp.bfloat16


def dot(a, b, ca, cb):
    return lax.dot_general(a, b, (((ca,), (cb,)), ((), ())), preferred_element_type=F32)


def head_slice(h):
    return slice(h * HEAD_DIM, (h + 1) * HEAD_DIM)


def chunk_slices(rows):
    return [slice(start, start + CHUNK) for start in range(0, rows, CHUNK)]


def causal(transposed=False):
    rows = lax.broadcasted_iota(jnp.int32, (CHUNK, CHUNK), 0)
    cols = lax.broadcasted_iota(jnp.int32, (CHUNK, CHUNK), 1)
    return cols >= rows if transposed else rows >= cols


def call(body, out_shape, args, flops, name, spaces=None, outs=None, scratch=()):
    size = sum(a.size * a.dtype.itemsize for a in args)
    size += sum(math.prod(a.shape) * a.dtype.itemsize for a in out_shape)
    spaces, outs = spaces or {}, outs or {}
    kernel = pl.pallas_call(
        body,
        out_shape=out_shape,
        in_specs=[
            pl.BlockSpec(memory_space=spaces.get(i, pltpu.VMEM)) for i in range(len(args))
        ],
        out_specs=[
            pl.BlockSpec(memory_space=outs.get(i, pltpu.VMEM)) for i in range(len(out_shape))
        ],
        scratch_shapes=list(scratch),
        compiler_params=pltpu.CompilerParams(vmem_limit_bytes=20 * 2**20),
        cost_estimate=pl.CostEstimate(flops=flops, bytes_accessed=size, transcendentals=0),
        name=name,
    )
    return list(kernel(*args))


def partner(order, slot):
    if slot == 0:
        return 0
    even, odd = (choice[slot - 1] for choice in order)
    if even == odd:
        return even
    return jnp.where(lax.rem(lax.axis_index("head"), 2) == 1, odd, even)


def number_at(order, slot):
    return lax.rem(lax.axis_index("seq"), QUAD) ^ partner(order, slot)


def rows_at(order, slot):
    return pl.ds(pl.multiple_of(number_at(order, slot) * HEAD_DIM, HEAD_DIM), HEAD_DIM)


def exchange(value, sizes, by):
    size, heads = sizes
    pairs = [
        (i * heads + h, (i ^ by[h % 2]) * heads + h) for i in range(size) for h in range(heads)
    ]
    return lax.ppermute(value, ("seq", "head"), pairs)


def exchange_all(pieces, sizes, order):
    even, odd = order
    return pieces[:1] + [exchange(p, sizes, by) for p, by in zip(pieces[1:], zip(even, odd))]


def quad_kernel(*refs):
    refs[-1][...] = (refs[0][...] + refs[1][...]) + (refs[2][...] + refs[3][...])


def finish_kernel(reverse, *refs):
    into, out_of = ORDERS[reverse]
    place = lax.axis_index("seq")
    zero = jnp.zeros(refs[0].shape, F32)
    second = place < QUAD if reverse else place >= QUAD
    before = jnp.where(second, refs[QUAD][...], zero)
    for to, out in enumerate(refs[-QUAD:]):
        here = number_at(out_of, to)
        total = before
        for slot in range(QUAD):
            number = number_at(into, slot)
            ahead = number > here if reverse else number < here
            total = total + jnp.where(ahead, refs[slot][...], zero)
        out[...] = total


def quad_scan(pieces, sizes, reverse, between):
    head = jax.ShapeDtypeStruct((HEAD_DIM, HEAD_DIM), F32)
    into, out_of = ORDERS[reverse]
    pieces = exchange_all(pieces, sizes, into)
    first = between(0, None)
    (total,) = call(
        quad_kernel, [head], [*pieces, *first[-1:]], 0, "quad_sum", spaces={4: pl.ANY}
    )
    far = exchange(total, sizes, (QUAD, QUAD))
    second = between(1, total)
    finished = call(
        functools.partial(finish_kernel, reverse),
        [head] * QUAD,
        [*pieces, far, *second[-1:]],
        0,
        "finish",
        spaces={5: pl.ANY},
    )
    third = between(2, finished[0])
    return exchange_all(finished, sizes, out_of), first + second + third


def doubling_scan(pieces, sizes, reverse, between):
    size = sizes[0]

    def shift(value, by):
        pairs = [(i, i + by) for i in range(size - by)]
        if reverse:
            pairs = [(b, a) for a, b in pairs]
        return lax.ppermute(value, "seq", pairs)

    into, out_of = (
        jnp.stack([number_at(order, slot) for slot in range(QUAD)]) for order in ORDERS[reverse]
    )
    state = jnp.stack(pieces)[jnp.argsort(into)]
    by = 1
    while by < size:
        state = state + shift(state, by)
        by *= 2
    state = shift(state, 1)[out_of]
    done = []
    for phase in range(3):
        done += between(phase, done[-1] if done else None)
    return [state[n] for n in range(QUAD)], done


def store_pieces(states, order, pieces, scratch):
    for h, state in enumerate(states):
        scratch[head_slice(h), :] = state
    for slot, piece in enumerate(pieces):
        piece[...] = scratch[rows_at(order, slot), :]


def load_pieces(pieces, order, rounded):
    for slot, piece in enumerate(pieces):
        rounded[rows_at(order, slot), :] = piece[...].astype(BF16)


def pair_blocks(left, right, contract):
    blocks = []
    for p in range(right.shape[1] // PAIR):
        cols = slice(p * PAIR, (p + 1) * PAIR)
        full = dot(left[:, cols] if contract == 0 else left[cols, :], right[:, cols], contract, 0)
        blocks += [full[:HEAD_DIM, :HEAD_DIM], full[HEAD_DIM:, HEAD_DIM:]]
    return blocks


def add_all(a, b):
    return b if a is None else [x + y for x, y in zip(a, b)]


def state_kernel(k_hbm, v_hbm, *refs):
    pieces, (k, v, scratch, sems) = refs[:QUAD], refs[QUAD:]
    chunks = chunk_slices(k.shape[0])
    copies = []
    for n, at in enumerate(chunks):
        for j, (src, dst) in enumerate(((k_hbm, k), (v_hbm, v))):
            copies.append(pltpu.make_async_copy(src.at[at], dst.at[at], sems.at[j, n]))
            copies[-1].start()
    total = None
    for n, at in enumerate(chunks):
        copies[2 * n].wait()
        copies[2 * n + 1].wait()
        total = add_all(total, pair_blocks(k[at, :], v[at, :], 0))
    store_pieces(total, ORDERS[False][0], pieces, scratch)


def intra_kernel(q, k, v, intra, states, q_t):
    keep = causal()
    cols = q.shape[1]
    q_t[...] = q[...].T
    for h in range(cols // HEAD_DIM):
        part = head_slice(h)
        state = None
        for n, at in enumerate(chunk_slices(q.shape[0])):
            qi, ki, vi = q[at, part], k[at, part], v[at, part]
            scores = jnp.where(keep, dot(qi, ki, 1, 1), 0.0).astype(BF16)
            out = dot(scores, vi, 1, 0)
            if n:
                out = out + dot(qi, state.astype(BF16), 1, 0)
                states[(n - 1) * cols + part.start : (n - 1) * cols + part.stop, :] = state
            intra[at, part] = out
            new = dot(ki, vi, 0, 0)
            state = state + new if n else new


def row_sums(tile):
    return jnp.sum(tile.T, axis=0, keepdims=True)


def mixed_kernel(intra, q, g, *refs):
    pieces, (mixed, prefix, stats, *copies) = refs[:QUAD], refs[QUAD:]
    load_pieces(pieces, ORDERS[False][1], prefix)
    blocks = q.shape[0] // HEAD_DIM
    for at in chunk_slices(q.shape[0]):
        square = cross = None
        for h in range(q.shape[1] // HEAD_DIM):
            part = head_slice(h)
            m = intra[at, part] + dot(q[at, part], prefix[part, :], 1, 0)
            mixed[at, part] = m
            s, c = m * m, m * g[at, part].astype(F32)
            square = s if square is None else square + s
            cross = c if cross is None else cross + c
        for n in range(CHUNK // HEAD_DIM):
            i = at.start // HEAD_DIM + n
            stats[i : i + 1, :] = row_sums(square[head_slice(n)])
            stats[blocks + i : blocks + i + 1, :] = row_sums(cross[head_slice(n)])
    for copy in copies:
        copy[...] = stats[...]


def norm_kernel(width, mixed, q_t, g, *refs):
    stats, (gm, inverse_out, states, *pieces, scratch) = refs[: -4 - QUAD], refs[-4 - QUAD :]
    total = stats[0][...]
    for r in stats[1:]:
        total = total + r[...]
    rows, cols = mixed.shape
    blocks = rows // HEAD_DIM
    inverse = lax.rsqrt(total[:blocks] / width + EPSILON)
    cross_mean = total[blocks:] * inverse / width
    scale = inverse * inverse * cross_mean
    inverse_out[...] = inverse
    shape = (HEAD_DIM, HEAD_DIM)
    after = None
    for n, at in reversed(list(enumerate(chunk_slices(rows)))):
        for i in range(at.start // HEAD_DIM, at.stop // HEAD_DIM):
            block = head_slice(i)
            a = jnp.broadcast_to(inverse[i : i + 1], shape).T
            b = jnp.broadcast_to(scale[i : i + 1], shape).T
            for h in range(cols // HEAD_DIM):
                part = head_slice(h)
                grad = g[block, part].astype(F32)
                gm[block, part] = (grad * a - mixed[block, part] * b).astype(BF16)
        after = add_all(after, pair_blocks(q_t[:, at], gm[at, :], 1))
        if n:
            for h, state in enumerate(after):
                first = (n - 1) * cols + h * HEAD_DIM
                states[first : first + HEAD_DIM, :] = state
    store_pieces(after, ORDERS[True][0], pieces, scratch)


def head_grads(h, q, k, v, gm, prefix, states, after, gq, gk, gv, finished=None):
    cols, part = q.shape[1], head_slice(h)
    keep, keep_t = causal(), causal(True)
    chunks = chunk_slices(q.shape[0])
    first = prefix[part, :].astype(F32)
    for n, at in enumerate(chunks):
        qi, ki, vi, gi = q[at, part], k[at, part], v[at, part], gm[at, part]
        scores_t = jnp.where(keep_t, dot(ki, qi, 1, 1), 0.0).astype(BF16)
        grad_scores = jnp.where(keep, dot(gi, vi, 1, 1), 0.0).astype(BF16)
        grad_scores_t = jnp.where(keep_t, dot(vi, gi, 1, 1), 0.0).astype(BF16)
        entering = first
        if n:
            entering = first + states[pl.ds((n - 1) * cols + part.start, HEAD_DIM), :]
        gq_i = dot(grad_scores, ki, 1, 0) + dot(gi, entering.astype(BF16), 1, 1)
        gk_i = dot(grad_scores_t, qi, 1, 0)
        gv_i = dot(scores_t, gi, 1, 0)
        if n < len(chunks) - 1:
            later = after[pl.ds(n * cols + part.start, HEAD_DIM), :].astype(BF16)
            gk_i = gk_i + dot(vi, later, 1, 1)
            gv_i = gv_i + dot(ki, later, 1, 0)
        gq[at, :] = gq_i.astype(BF16)
        gk[at, :] = gk_i
        gv[at, :] = gv_i
        if finished is not None:
            finished(n, at)


def first_grads_kernel(q, k, v, gm, prefix, states, after, *refs):
    gqs, gks, gvs = refs[:2], refs[2:4], refs[4:]
    for h in range(2):
        head_grads(h, q, k, v, gm, prefix, states, after, gqs[h], gks[h], gvs[h])


def second_grads_kernel(q, k, v, gm, prefix, states, after, mixed, inverse, *refs):
    gq, gk, gv, out_hbm, out, sems = refs[-6:]
    shape = (HEAD_DIM, HEAD_DIM)
    copies = []
    for n, at in enumerate(chunk_slices(q.shape[0])):
        for i in range(at.start // HEAD_DIM, at.stop // HEAD_DIM):
            a = jnp.broadcast_to(inverse[i : i + 1, :], shape).T
            for h in range(q.shape[1] // HEAD_DIM):
                block = (head_slice(i), head_slice(h))
                out[block] = (mixed[block] * a).astype(BF16)
        copies.append(pltpu.make_async_copy(out.at[at], out_hbm.at[at], sems.at[n]))
        copies[-1].start()
    head_grads(2, q, k, v, gm, prefix, states, after, gq, gk, gv)
    for copy in copies:
        copy.wait()


def third_grads_kernel(q, k, v, gm, prefix, states, after, *refs):
    gqs, (gk, gv, gq_hbm, gq, sems) = refs[:3], refs[-5:]
    copies = []

    def send(src, h, at, sem):
        copies.append(pltpu.make_async_copy(src.at[at], gq_hbm.at[at, head_slice(h)], sem))
        copies[-1].start()

    for h in range(3):
        send(gqs[h], h, slice(0, q.shape[0]), sems.at[h])
    head_grads(
        3, q, k, v, gm, prefix, states, after, gq, gk, gv, lambda n, at: send(gq, 3, at, sems.at[3 + n])
    )
    for copy in copies:
        copy.wait()


def last_kernel(k, v, *refs):
    gks, gvs, pieces = (refs[i * QUAD : (i + 1) * QUAD] for i in range(3))
    gk_hbm, gv_hbm, gk, gv, suffix, sems = refs[-6:]
    load_pieces(pieces, ORDERS[True][1], suffix)
    copies = []
    for n, at in enumerate(chunk_slices(k.shape[0])):
        for h in range(QUAD):
            part = head_slice(h)
            state = suffix[part, :]
            gk[at, part] = (gks[h][at, :] + dot(v[at, part], state, 1, 1)).astype(BF16)
            gv[at, part] = (gvs[h][at, :] + dot(k[at, part], state, 1, 0)).astype(BF16)
        for j, (src, dst) in enumerate(((gk, gk_hbm), (gv, gv_hbm))):
            copies.append(pltpu.make_async_copy(src.at[at], dst.at[at], sems.at[j, n]))
            copies[-1].start()
    for copy in copies:
        copy.wait()


def all_parts(values, axis):
    size = len(values)
    power = size & (size - 1) == 0
    parts = [values[0]]
    for by in reversed(range(1, size)):
        pairs = [(i, i ^ by if power else (i + by) % size) for i in range(size)]
        parts.append(lax.ppermute(values[by], axis, pairs))
    return parts


def shards(sizes, queries, keys, values, grad_out):
    seq, head_size = sizes
    rows, cols = queries.shape
    chunks = rows // CHUNK
    blocks = rows // HEAD_DIM
    scan = quad_scan if seq == 2 * QUAD else doubling_scan

    def shape(count, lanes, kind=F32):
        return jax.ShapeDtypeStruct((count, lanes), kind)

    wide, narrow = shape(rows, cols), shape(rows, cols, BF16)
    head_wide, head_narrow = shape(rows, HEAD_DIM), shape(rows, HEAD_DIM, BF16)
    pieces_shape = [shape(HEAD_DIM, HEAD_DIM)] * QUAD
    states_shape = shape((chunks - 1) * cols, HEAD_DIM)
    pieces_scratch = pltpu.VMEM((cols, HEAD_DIM), F32)
    head_flops = 2 * rows * HEAD_DIM * HEAD_DIM
    chunk_flops = 2 * rows * CHUNK * HEAD_DIM

    *pieces, keys, values = call(
        state_kernel,
        pieces_shape + [pltpu.VMEM((rows, cols), BF16)] * 2,
        [pltpu.with_memory_space_constraint(a, pltpu.HBM) for a in (keys, values)],
        QUAD * head_flops,
        "local_state",
        spaces={0: pltpu.HBM, 1: pltpu.HBM},
        scratch=[pieces_scratch, pltpu.SemaphoreType.DMA((2, chunks))],
    )

    def forward(phase, token):
        if phase:
            return []
        return call(
            intra_kernel,
            [wide, states_shape, shape(cols, rows, BF16)],
            [queries, keys, values],
            QUAD * (2 * chunk_flops + 2 * head_flops),
            "intra",
        )

    prefixes, (intra, states, queries_t) = scan(pieces, sizes, False, forward)
    mixed, prefix, *stats = call(
        mixed_kernel,
        [wide, shape(cols, HEAD_DIM, BF16)] + [shape(2 * blocks, HEAD_DIM)] * head_size,
        [intra, queries, grad_out, *prefixes],
        QUAD * head_flops,
        "mixed",
    )
    gm, inverse, after, *pieces = call(
        functools.partial(norm_kernel, cols * head_size),
        [narrow, shape(blocks, HEAD_DIM), states_shape] + pieces_shape,
        [mixed, queries_t, grad_out, *all_parts(stats, "head")],
        QUAD * head_flops,
        "norm",
        scratch=[pieces_scratch],
    )
    args = [queries, keys, values, gm, prefix, states, after]
    grads_flops = 6 * chunk_flops + 3 * head_flops

    def backward(phase, token):
        if phase == 0:
            parts = call(
                first_grads_kernel,
                [head_narrow] * 2 + [head_wide] * 4,
                args,
                2 * grads_flops,
                "first_grads",
            )
        elif phase == 1:
            parts = call(
                second_grads_kernel,
                [head_narrow] + [head_wide] * 2 + [narrow],
                args + [mixed, inverse, token],
                grads_flops,
                "second_grads",
                spaces={len(args) + 2: pl.ANY},
                outs={3: pl.ANY},
                scratch=[pltpu.VMEM((rows, cols), BF16), pltpu.SemaphoreType.DMA((chunks,))],
            )
        else:
            parts = call(
                third_grads_kernel,
                [head_wide] * 2 + [narrow],
                args + gqs + [token],
                grads_flops,
                "third_grads",
                spaces={len(args) + 3: pl.ANY},
                outs={2: pl.ANY},
                scratch=[
                    pltpu.VMEM((rows, HEAD_DIM), BF16),
                    pltpu.SemaphoreType.DMA((3 + chunks,)),
                ],
            )
        if phase < 2:
            count = 2 - phase
            gqs.extend(parts[:count])
            parts = parts[count:]
        count = 2 if phase == 0 else 1
        gks.extend(parts[:count])
        gvs.extend(parts[count : 2 * count])
        results.extend(parts[2 * count :])
        return gks[-1:]

    gqs, gks, gvs, results = [], [], [], []
    suffixes, unused = scan(pieces, sizes, True, backward)
    output, grad_q = results
    grad_k, grad_v = call(
        last_kernel,
        [narrow, narrow],
        [keys, values, *gks, *gvs, *suffixes],
        2 * QUAD * head_flops,
        "last",
        outs={0: pl.ANY, 1: pl.ANY},
        scratch=[pltpu.VMEM((rows, cols), BF16)] * 2
        + [pltpu.VMEM((cols, HEAD_DIM), BF16), pltpu.SemaphoreType.DMA((2, chunks))],
    )
    return output, grad_q, grad_k, grad_v


def solution(mesh):
    sizes = (mesh.shape["seq"], mesh.shape["head"])
    spec = P("seq", "head")
    return jax.shard_map(
        functools.partial(shards, sizes),
        mesh=mesh,
        in_specs=(spec,) * 4,
        out_specs=(spec,) * 4,
        check_vma=False,
    )
```

```python
import functools
import math

import jax
import jax.numpy as jnp
from jax import lax
from jax.experimental import pallas as pl
from jax.experimental.pallas import tpu as pltpu
from jax.sharding import PartitionSpec as P

HEAD_DIM = 128
EPSILON = 1e-06
CHUNK = 256
PAIR = 2 * HEAD_DIM
QUAD = 4
ORDERS = {
    False: (((3, 2, 1), (3, 2, 1)), ((3, 2, 1), (3, 2, 1))),
    True: (((3, 1, 2), (3, 1, 2)), ((3, 1, 2), (3, 1, 2))),
}
F32 = jnp.float32
BF16 = jnp.bfloat16


def dot(a, b, ca, cb):
    return lax.dot_general(a, b, (((ca,), (cb,)), ((), ())), preferred_element_type=F32)


def head_slice(h):
    return slice(h * HEAD_DIM, (h + 1) * HEAD_DIM)


def chunk_slices(rows):
    return [slice(start, start + CHUNK) for start in range(0, rows, CHUNK)]


def causal(transposed=False):
    rows = lax.broadcasted_iota(jnp.int32, (CHUNK, CHUNK), 0)
    cols = lax.broadcasted_iota(jnp.int32, (CHUNK, CHUNK), 1)
    return cols >= rows if transposed else rows >= cols


def call(body, out_shape, args, flops, name, spaces=None, outs=None, scratch=()):
    size = sum(a.size * a.dtype.itemsize for a in args)
    size += sum(math.prod(a.shape) * a.dtype.itemsize for a in out_shape)
    spaces, outs = spaces or {}, outs or {}
    kernel = pl.pallas_call(
        body,
        out_shape=out_shape,
        in_specs=[
            pl.BlockSpec(memory_space=spaces.get(i, pltpu.VMEM)) for i in range(len(args))
        ],
        out_specs=[
            pl.BlockSpec(memory_space=outs.get(i, pltpu.VMEM)) for i in range(len(out_shape))
        ],
        scratch_shapes=list(scratch),
        compiler_params=pltpu.CompilerParams(vmem_limit_bytes=20 * 2**20),
        cost_estimate=pl.CostEstimate(flops=flops, bytes_accessed=size, transcendentals=0),
        name=name,
    )
    return list(kernel(*args))


def partner(order, slot):
    if slot == 0:
        return 0
    even, odd = (choice[slot - 1] for choice in order)
    if even == odd:
        return even
    return jnp.where(lax.rem(lax.axis_index("head"), 2) == 1, odd, even)


def number_at(order, slot):
    return lax.rem(lax.axis_index("seq"), QUAD) ^ partner(order, slot)


def pair_of(number):
    return lax.rem(number, 2) ^ (number // 2)


def head_at(order, slot):
    number = number_at(order, slot)
    return 2 * pair_of(number) + number // 2


def rows_at(order, slot):
    return pl.ds(pl.multiple_of(head_at(order, slot) * HEAD_DIM, HEAD_DIM), HEAD_DIM)


def by_pair(body, mine, other):
    pair = pair_of(lax.rem(lax.axis_index("seq"), QUAD))
    pl.when(pair == 0)(functools.partial(body, mine, other))
    pl.when(pair == 1)(functools.partial(body, other, mine))


def exchange(value, sizes, by):
    size, heads = sizes
    pairs = [
        (i * heads + h, (i ^ by[h % 2]) * heads + h) for i in range(size) for h in range(heads)
    ]
    return lax.ppermute(value, ("seq", "head"), pairs)


def exchange_all(pieces, sizes, order):
    even, odd = order
    return pieces[:1] + [exchange(p, sizes, by) for p, by in zip(pieces[1:], zip(even, odd))]


def quad_kernel(*refs):
    refs[-1][...] = (refs[0][...] + refs[1][...]) + (refs[2][...] + refs[3][...])


def finish_kernel(reverse, *refs):
    into, out_of = ORDERS[reverse]
    place = lax.axis_index("seq")
    zero = jnp.zeros(refs[0].shape, F32)
    second = place < QUAD if reverse else place >= QUAD
    before = jnp.where(second, refs[QUAD][...], zero)
    for to, out in enumerate(refs[-QUAD:]):
        here = number_at(out_of, to)
        total = before
        for slot in range(QUAD):
            number = number_at(into, slot)
            ahead = number > here if reverse else number < here
            total = total + jnp.where(ahead, refs[slot][...], zero)
        out[...] = total


def quad_scan(pieces, sizes, reverse, between):
    head = jax.ShapeDtypeStruct((HEAD_DIM, HEAD_DIM), F32)
    into, out_of = ORDERS[reverse]
    pieces = exchange_all(pieces, sizes, into)
    first = between(0, None)
    (total,) = call(
        quad_kernel, [head], [*pieces, *first[-1:]], 0, "quad_sum", spaces={4: pl.ANY}
    )
    far = exchange(total, sizes, (QUAD, QUAD))
    second = between(1, total)
    finished = call(
        functools.partial(finish_kernel, reverse),
        [head] * QUAD,
        [*pieces, far, *second[-1:]],
        0,
        "finish",
        spaces={5: pl.ANY},
    )
    third = between(2, finished[0])
    return exchange_all(finished, sizes, out_of), first + second + third


def doubling_scan(pieces, sizes, reverse, between):
    size = sizes[0]

    def shift(value, by):
        pairs = [(i, i + by) for i in range(size - by)]
        if reverse:
            pairs = [(b, a) for a, b in pairs]
        return lax.ppermute(value, "seq", pairs)

    into, out_of = (
        jnp.stack([head_at(order, slot) for slot in range(QUAD)]) for order in ORDERS[reverse]
    )
    state = jnp.stack(pieces)[jnp.argsort(into)]
    by = 1
    while by < size:
        state = state + shift(state, by)
        by *= 2
    state = shift(state, 1)[out_of]
    done = []
    for phase in range(3):
        done += between(phase, done[-1] if done else None)
    return [state[n] for n in range(QUAD)], done


def store_pieces(states, order, pieces, scratch):
    for h, state in enumerate(states):
        scratch[head_slice(h), :] = state
    for slot, piece in enumerate(pieces):
        piece[...] = scratch[rows_at(order, slot), :]


def load_pieces(pieces, order, rounded, first=0):
    for slot, piece in enumerate(pieces, first):
        rounded[rows_at(order, slot), :] = piece[...].astype(BF16)


def pair_blocks(left, right, contract):
    blocks = []
    for p in range(right.shape[1] // PAIR):
        cols = slice(p * PAIR, (p + 1) * PAIR)
        full = dot(left[:, cols] if contract == 0 else left[cols, :], right[:, cols], contract, 0)
        blocks += [full[:HEAD_DIM, :HEAD_DIM], full[HEAD_DIM:, HEAD_DIM:]]
    return blocks


def add_all(a, b):
    return b if a is None else [x + y for x, y in zip(a, b)]


def state_kernel(k_hbm, v_hbm, *refs):
    pieces, (k, v, scratch, sems) = refs[:QUAD], refs[QUAD:]
    chunks = chunk_slices(k.shape[0])
    copies = []
    for n, at in enumerate(chunks):
        for j, (src, dst) in enumerate(((k_hbm, k), (v_hbm, v))):
            copies.append(pltpu.make_async_copy(src.at[at], dst.at[at], sems.at[j, n]))
            copies[-1].start()
    total = None
    for n, at in enumerate(chunks):
        copies[2 * n].wait()
        copies[2 * n + 1].wait()
        total = add_all(total, pair_blocks(k[at, :], v[at, :], 0))
    store_pieces(total, ORDERS[False][0], pieces, scratch)


def intra_kernel(q, k, v, intra, states, q_t):
    keep = causal()
    cols = q.shape[1]
    q_t[...] = q[...].T
    for h in range(cols // HEAD_DIM):
        part = head_slice(h)
        state = None
        for n, at in enumerate(chunk_slices(q.shape[0])):
            qi, ki, vi = q[at, part], k[at, part], v[at, part]
            scores = jnp.where(keep, dot(qi, ki, 1, 1), 0.0).astype(BF16)
            out = dot(scores, vi, 1, 0)
            if n:
                out = out + dot(qi, state.astype(BF16), 1, 0)
                states[(n - 1) * cols + part.start : (n - 1) * cols + part.stop, :] = state
            intra[at, part] = out
            new = dot(ki, vi, 0, 0)
            state = state + new if n else new


def row_sums(tile):
    return jnp.sum(tile.T, axis=0, keepdims=True)


def mixed_kernel(is_own, intra, q, g, *refs):
    pieces, refs = refs[:2], refs[2:]
    before, refs = ([], refs) if is_own else (refs[:2], refs[2:])
    mixed, prefix, *stats, scratch = refs
    load_pieces(pieces, ORDERS[False][1], scratch, 0 if is_own else 2)
    blocks = q.shape[0] // HEAD_DIM

    def pair(p):
        for at in chunk_slices(q.shape[0]):
            square = cross = None
            for j in range(2):
                part, whole = head_slice(j), head_slice(2 * p + j)
                m = intra[at, whole] + dot(q[at, whole], scratch[whole, :], 1, 0)
                mixed[at, part] = m
                s, c = m * m, m * g[at, whole].astype(F32)
                square = s if square is None else square + s
                cross = c if cross is None else cross + c
            for n in range(CHUNK // HEAD_DIM):
                for first, value in ((0, square), (blocks, cross)):
                    i = first + at.start // HEAD_DIM + n
                    sums = row_sums(value[head_slice(n)])
                    if before:
                        sums = sums + before[0][i : i + 1, :]
                    stats[0][i : i + 1, :] = sums
        part = slice(p * PAIR, (p + 1) * PAIR)
        prefix[part, :] = scratch[part, :]
        if before:
            part = slice((1 - p) * PAIR, (2 - p) * PAIR)
            prefix[part, :] = before[1][part, :]

    by_pair(lambda mine, other: pair(0 if mine else 1), is_own, not is_own)
    for copy in stats[1:]:
        copy[...] = stats[0][...]


def norm_kernel(width, mixed, oth_mixed, q_t, g, *refs):
    stats, (gm, inverse_out, states, *pieces, scratch) = refs[: -4 - QUAD], refs[-4 - QUAD :]
    total = stats[0][...]
    for r in stats[1:]:
        total = total + r[...]
    rows, cols = gm.shape
    blocks = rows // HEAD_DIM
    inverse = lax.rsqrt(total[:blocks] / width + EPSILON)
    cross_mean = total[blocks:] * inverse / width
    scale = inverse * inverse * cross_mean
    inverse_out[...] = inverse
    shape = (HEAD_DIM, HEAD_DIM)

    def body(*pairs):
        after = None
        for n, at in reversed(list(enumerate(chunk_slices(rows)))):
            for i in range(at.start // HEAD_DIM, at.stop // HEAD_DIM):
                block = head_slice(i)
                a = jnp.broadcast_to(inverse[i : i + 1], shape).T
                b = jnp.broadcast_to(scale[i : i + 1], shape).T
                for h in range(cols // HEAD_DIM):
                    part = head_slice(h)
                    value = pairs[h // 2][block, head_slice(h % 2)]
                    grad = g[block, part].astype(F32)
                    gm[block, part] = (grad * a - value * b).astype(BF16)
            after = add_all(after, pair_blocks(q_t[:, at], gm[at, :], 1))
            if n:
                for h, state in enumerate(after):
                    first = (n - 1) * cols + h * HEAD_DIM
                    states[first : first + HEAD_DIM, :] = state
        for h, state in enumerate(after):
            scratch[head_slice(h), :] = state

    by_pair(body, mixed, oth_mixed)
    for slot, piece in enumerate(pieces):
        piece[...] = scratch[rows_at(ORDERS[True][0], slot), :]


def head_grads(h, q, k, v, gm, prefix, states, after, gq, gk, gv, finished=None):
    cols, part = q.shape[1], head_slice(h)
    keep, keep_t = causal(), causal(True)
    chunks = chunk_slices(q.shape[0])
    first = prefix[part, :].astype(F32)
    for n, at in enumerate(chunks):
        qi, ki, vi, gi = q[at, part], k[at, part], v[at, part], gm[at, part]
        scores_t = jnp.where(keep_t, dot(ki, qi, 1, 1), 0.0).astype(BF16)
        grad_scores = jnp.where(keep, dot(gi, vi, 1, 1), 0.0).astype(BF16)
        grad_scores_t = jnp.where(keep_t, dot(vi, gi, 1, 1), 0.0).astype(BF16)
        entering = first
        if n:
            entering = first + states[pl.ds((n - 1) * cols + part.start, HEAD_DIM), :]
        gq_i = dot(grad_scores, ki, 1, 0) + dot(gi, entering.astype(BF16), 1, 1)
        gk_i = dot(grad_scores_t, qi, 1, 0)
        gv_i = dot(scores_t, gi, 1, 0)
        if n < len(chunks) - 1:
            later = after[pl.ds(n * cols + part.start, HEAD_DIM), :].astype(BF16)
            gk_i = gk_i + dot(vi, later, 1, 1)
            gv_i = gv_i + dot(ki, later, 1, 0)
        gq[at, :] = gq_i.astype(BF16)
        gk[at, :] = gk_i
        gv[at, :] = gv_i
        if finished is not None:
            finished(n, at)


def first_grads_kernel(q, k, v, gm, prefix, states, after, *refs):
    gqs, gks, gvs = refs[:2], refs[2:4], refs[4:]
    for h in range(2):
        head_grads(h, q, k, v, gm, prefix, states, after, gqs[h], gks[h], gvs[h])


def second_grads_kernel(q, k, v, gm, prefix, states, after, mixed, oth_mixed, inverse, *refs):
    gq, gk, gv, out_hbm, out, sems = refs[-6:]
    shape = (HEAD_DIM, HEAD_DIM)

    def body(*pairs):
        copies = []
        for n, at in enumerate(chunk_slices(q.shape[0])):
            for i in range(at.start // HEAD_DIM, at.stop // HEAD_DIM):
                a = jnp.broadcast_to(inverse[i : i + 1, :], shape).T
                for h in range(q.shape[1] // HEAD_DIM):
                    value = pairs[h // 2][head_slice(i), head_slice(h % 2)]
                    out[head_slice(i), head_slice(h)] = (value * a).astype(BF16)
            copies.append(pltpu.make_async_copy(out.at[at], out_hbm.at[at], sems.at[n]))
            copies[-1].start()
        head_grads(2, q, k, v, gm, prefix, states, after, gq, gk, gv)
        for copy in copies:
            copy.wait()

    by_pair(body, mixed, oth_mixed)


def third_grads_kernel(q, k, v, gm, prefix, states, after, *refs):
    gqs, (gk, gv, gq_hbm, gq, sems) = refs[:3], refs[-5:]
    copies = []

    def send(src, h, at, sem):
        copies.append(pltpu.make_async_copy(src.at[at], gq_hbm.at[at, head_slice(h)], sem))
        copies[-1].start()

    for h in range(3):
        send(gqs[h], h, slice(0, q.shape[0]), sems.at[h])
    head_grads(
        3, q, k, v, gm, prefix, states, after, gq, gk, gv, lambda n, at: send(gq, 3, at, sems.at[3 + n])
    )
    for copy in copies:
        copy.wait()


def last_kernel(k, v, *refs):
    gks, gvs, pieces = (refs[i * QUAD : (i + 1) * QUAD] for i in range(3))
    gk_hbm, gv_hbm, gk, gv, suffix, sems = refs[-6:]
    load_pieces(pieces, ORDERS[True][1], suffix)
    copies = []
    for n, at in enumerate(chunk_slices(k.shape[0])):
        for h in range(QUAD):
            part = head_slice(h)
            state = suffix[part, :]
            gk[at, part] = (gks[h][at, :] + dot(v[at, part], state, 1, 1)).astype(BF16)
            gv[at, part] = (gvs[h][at, :] + dot(k[at, part], state, 1, 0)).astype(BF16)
        for j, (src, dst) in enumerate(((gk, gk_hbm), (gv, gv_hbm))):
            copies.append(pltpu.make_async_copy(src.at[at], dst.at[at], sems.at[j, n]))
            copies[-1].start()
    for copy in copies:
        copy.wait()


def all_parts(values, axis):
    size = len(values)
    power = size & (size - 1) == 0
    parts = [values[0]]
    for by in reversed(range(1, size)):
        pairs = [(i, i ^ by if power else (i + by) % size) for i in range(size)]
        parts.append(lax.ppermute(values[by], axis, pairs))
    return parts


def shards(sizes, queries, keys, values, grad_out):
    seq, head_size = sizes
    rows, cols = queries.shape
    chunks = rows // CHUNK
    blocks = rows // HEAD_DIM
    scan = quad_scan if seq == 2 * QUAD else doubling_scan

    def shape(count, lanes, kind=F32):
        return jax.ShapeDtypeStruct((count, lanes), kind)

    wide, narrow = shape(rows, cols), shape(rows, cols, BF16)
    head_wide, head_narrow = shape(rows, HEAD_DIM), shape(rows, HEAD_DIM, BF16)
    pieces_shape = [shape(HEAD_DIM, HEAD_DIM)] * QUAD
    states_shape = shape((chunks - 1) * cols, HEAD_DIM)
    pieces_scratch = pltpu.VMEM((cols, HEAD_DIM), F32)
    head_flops = 2 * rows * HEAD_DIM * HEAD_DIM
    chunk_flops = 2 * rows * CHUNK * HEAD_DIM

    *pieces, keys, values = call(
        state_kernel,
        pieces_shape + [pltpu.VMEM((rows, cols), BF16)] * 2,
        [pltpu.with_memory_space_constraint(a, pltpu.HBM) for a in (keys, values)],
        QUAD * head_flops,
        "local_state",
        spaces={0: pltpu.HBM, 1: pltpu.HBM},
        scratch=[pieces_scratch, pltpu.SemaphoreType.DMA((2, chunks))],
    )

    def forward(phase, token):
        if phase:
            return []
        return call(
            intra_kernel,
            [wide, states_shape, shape(cols, rows, BF16)],
            [queries, keys, values],
            QUAD * (2 * chunk_flops + 2 * head_flops),
            "intra",
        )

    prefixes, (intra, states, queries_t) = scan(pieces, sizes, False, forward)
    stats_shape = shape(2 * blocks, HEAD_DIM)

    def mix(is_own, pieces, count, *before):
        return call(
            functools.partial(mixed_kernel, is_own),
            [shape(rows, PAIR), shape(cols, HEAD_DIM, BF16)] + [stats_shape] * count,
            [intra, queries, grad_out, *pieces, *before],
            2 * head_flops,
            "mixed",
            scratch=[pltpu.VMEM((cols, HEAD_DIM), BF16)],
        )

    mixed, prefix, stats = mix(True, prefixes[:2], 1)
    oth_mixed, prefix, *stats = mix(False, prefixes[2:], head_size, stats, prefix)
    gm, inverse, after, *pieces = call(
        functools.partial(norm_kernel, cols * head_size),
        [narrow, shape(blocks, HEAD_DIM), states_shape] + pieces_shape,
        [mixed, oth_mixed, queries_t, grad_out, *all_parts(stats, "head")],
        QUAD * head_flops,
        "norm",
        scratch=[pieces_scratch],
    )
    args = [queries, keys, values, gm, prefix, states, after]
    grads_flops = 6 * chunk_flops + 3 * head_flops

    def backward(phase, token):
        if phase == 0:
            parts = call(
                first_grads_kernel,
                [head_narrow] * 2 + [head_wide] * 4,
                args,
                2 * grads_flops,
                "first_grads",
            )
        elif phase == 1:
            parts = call(
                second_grads_kernel,
                [head_narrow] + [head_wide] * 2 + [narrow],
                args + [mixed, oth_mixed, inverse, token],
                grads_flops,
                "second_grads",
                spaces={len(args) + 3: pl.ANY},
                outs={3: pl.ANY},
                scratch=[pltpu.VMEM((rows, cols), BF16), pltpu.SemaphoreType.DMA((chunks,))],
            )
        else:
            parts = call(
                third_grads_kernel,
                [head_wide] * 2 + [narrow],
                args + gqs + [token],
                grads_flops,
                "third_grads",
                spaces={len(args) + 3: pl.ANY},
                outs={2: pl.ANY},
                scratch=[
                    pltpu.VMEM((rows, HEAD_DIM), BF16),
                    pltpu.SemaphoreType.DMA((3 + chunks,)),
                ],
            )
        if phase < 2:
            count = 2 - phase
            gqs.extend(parts[:count])
            parts = parts[count:]
        count = 2 if phase == 0 else 1
        gks.extend(parts[:count])
        gvs.extend(parts[count : 2 * count])
        results.extend(parts[2 * count :])
        return gks[-1:]

    gqs, gks, gvs, results = [], [], [], []
    suffixes, unused = scan(pieces, sizes, True, backward)
    output, grad_q = results
    grad_k, grad_v = call(
        last_kernel,
        [narrow, narrow],
        [keys, values, *gks, *gvs, *suffixes],
        2 * QUAD * head_flops,
        "last",
        outs={0: pl.ANY, 1: pl.ANY},
        scratch=[pltpu.VMEM((rows, cols), BF16)] * 2
        + [pltpu.VMEM((cols, HEAD_DIM), BF16), pltpu.SemaphoreType.DMA((2, chunks))],
    )
    return output, grad_q, grad_k, grad_v


def solution(mesh):
    sizes = (mesh.shape["seq"], mesh.shape["head"])
    spec = P("seq", "head")
    return jax.shard_map(
        functools.partial(shards, sizes),
        mesh=mesh,
        in_specs=(spec,) * 4,
        out_specs=(spec,) * 4,
        check_vma=False,
    )
```

```python
import functools
import math

import jax
import jax.numpy as jnp
from jax import lax
from jax.experimental import pallas as pl
from jax.experimental.pallas import tpu as pltpu
from jax.sharding import PartitionSpec as P

HEAD_DIM = 128
EPSILON = 1e-06
CHUNK = 256
PAIR = 2 * HEAD_DIM
QUAD = 4
ORDERS = {
    False: (((3, 2, 1), (3, 2, 1)), ((3, 2, 1), (3, 2, 1))),
    True: (((3, 1, 2), (3, 1, 2)), ((3, 1, 2), (3, 1, 2))),
}
F32 = jnp.float32
BF16 = jnp.bfloat16


def dot(a, b, ca, cb):
    return lax.dot_general(a, b, (((ca,), (cb,)), ((), ())), preferred_element_type=F32)


def head_slice(h):
    return slice(h * HEAD_DIM, (h + 1) * HEAD_DIM)


def chunk_slices(rows, size=CHUNK):
    return [slice(start, start + size) for start in range(0, rows, size)]


def causal(transposed=False):
    rows = lax.broadcasted_iota(jnp.int32, (CHUNK, CHUNK), 0)
    cols = lax.broadcasted_iota(jnp.int32, (CHUNK, CHUNK), 1)
    return cols >= rows if transposed else rows >= cols


def call(body, out_shape, args, flops, name, spaces=None, outs=None, scratch=()):
    size = sum(a.size * a.dtype.itemsize for a in args)
    size += sum(math.prod(a.shape) * a.dtype.itemsize for a in out_shape)
    spaces, outs = spaces or {}, outs or {}
    kernel = pl.pallas_call(
        body,
        out_shape=out_shape,
        in_specs=[
            pl.BlockSpec(memory_space=spaces.get(i, pltpu.VMEM)) for i in range(len(args))
        ],
        out_specs=[
            pl.BlockSpec(memory_space=outs.get(i, pltpu.VMEM)) for i in range(len(out_shape))
        ],
        scratch_shapes=list(scratch),
        compiler_params=pltpu.CompilerParams(vmem_limit_bytes=20 * 2**20),
        cost_estimate=pl.CostEstimate(flops=flops, bytes_accessed=size, transcendentals=0),
        name=name,
    )
    return list(kernel(*args))


def partner(order, slot):
    if slot == 0:
        return 0
    even, odd = (choice[slot - 1] for choice in order)
    if even == odd:
        return even
    return jnp.where(lax.rem(lax.axis_index("head"), 2) == 1, odd, even)


def number_at(order, slot):
    return lax.rem(lax.axis_index("seq"), QUAD) ^ partner(order, slot)


def pair_of(number):
    return lax.rem(number, 2) ^ (number // 2)


def head_at(order, slot):
    number = number_at(order, slot)
    return 2 * pair_of(number) + number // 2


def rows_at(order, slot):
    return pl.ds(pl.multiple_of(head_at(order, slot) * HEAD_DIM, HEAD_DIM), HEAD_DIM)


def by_pair(body, mine, other):
    pair = pair_of(lax.rem(lax.axis_index("seq"), QUAD))
    pl.when(pair == 0)(functools.partial(body, mine, other))
    pl.when(pair == 1)(functools.partial(body, other, mine))


def exchange(value, sizes, by):
    size, heads = sizes
    pairs = [
        (i * heads + h, (i ^ by[h % 2]) * heads + h) for i in range(size) for h in range(heads)
    ]
    return lax.ppermute(value, ("seq", "head"), pairs)


def exchange_all(pieces, sizes, order):
    even, odd = order
    return pieces[:1] + [exchange(p, sizes, by) for p, by in zip(pieces[1:], zip(even, odd))]


def quad_kernel(*refs):
    refs[-1][...] = (refs[0][...] + refs[1][...]) + (refs[2][...] + refs[3][...])


def finish_kernel(reverse, *refs):
    into, out_of = ORDERS[reverse]
    place = lax.axis_index("seq")
    zero = jnp.zeros(refs[0].shape, F32)
    second = place < QUAD if reverse else place >= QUAD
    before = jnp.where(second, refs[QUAD][...], zero)
    for to, out in enumerate(refs[-QUAD:]):
        here = number_at(out_of, to)
        total = before
        for slot in range(QUAD):
            number = number_at(into, slot)
            ahead = number > here if reverse else number < here
            total = total + jnp.where(ahead, refs[slot][...], zero)
        out[...] = total


def quad_scan(pieces, sizes, reverse, between):
    head = jax.ShapeDtypeStruct((HEAD_DIM, HEAD_DIM), F32)
    into, out_of = ORDERS[reverse]
    pieces = exchange_all(pieces, sizes, into)
    first = between(0, None)
    (total,) = call(
        quad_kernel, [head], [*pieces, *first[-1:]], 0, "quad_sum", spaces={4: pl.ANY}
    )
    far = exchange(total, sizes, (QUAD, QUAD))
    second = between(1, total)
    finished = call(
        functools.partial(finish_kernel, reverse),
        [head] * QUAD,
        [*pieces, far, *second[-1:]],
        0,
        "finish",
        spaces={5: pl.ANY},
    )
    third = between(2, finished[0])
    return exchange_all(finished, sizes, out_of), first + second + third


def doubling_scan(pieces, sizes, reverse, between):
    size = sizes[0]

    def shift(value, by):
        pairs = [(i, i + by) for i in range(size - by)]
        if reverse:
            pairs = [(b, a) for a, b in pairs]
        return lax.ppermute(value, "seq", pairs)

    into, out_of = (
        jnp.stack([head_at(order, slot) for slot in range(QUAD)]) for order in ORDERS[reverse]
    )
    state = jnp.stack(pieces)[jnp.argsort(into)]
    by = 1
    while by < size:
        state = state + shift(state, by)
        by *= 2
    state = shift(state, 1)[out_of]
    done = []
    for phase in range(3):
        done += between(phase, done[-1] if done else None)
    return [state[n] for n in range(QUAD)], done


def store_pieces(states, order, pieces, scratch):
    for h, state in enumerate(states):
        scratch[head_slice(h), :] = state
    for slot, piece in enumerate(pieces):
        piece[...] = scratch[rows_at(order, slot), :]


def load_pieces(pieces, order, rounded, first=0):
    for slot, piece in enumerate(pieces, first):
        rounded[rows_at(order, slot), :] = piece[...].astype(BF16)


def pair_blocks(left, right, contract):
    blocks = []
    for p in range(right.shape[1] // PAIR):
        cols = slice(p * PAIR, (p + 1) * PAIR)
        full = dot(left[:, cols] if contract == 0 else left[cols, :], right[:, cols], contract, 0)
        blocks += [full[:HEAD_DIM, :HEAD_DIM], full[HEAD_DIM:, HEAD_DIM:]]
    return blocks


def add_all(a, b):
    return b if a is None else [x + y for x, y in zip(a, b)]


def state_kernel(k_hbm, v_hbm, *refs):
    pieces, (k, v, scratch, sems) = refs[:QUAD], refs[QUAD:]
    chunks = chunk_slices(k.shape[0])
    copies = []
    for n, at in enumerate(chunks):
        for j, (src, dst) in enumerate(((k_hbm, k), (v_hbm, v))):
            copies.append(pltpu.make_async_copy(src.at[at], dst.at[at], sems.at[j, n]))
            copies[-1].start()
    total = None
    for n, at in enumerate(chunks):
        copies[2 * n].wait()
        copies[2 * n + 1].wait()
        total = add_all(total, pair_blocks(k[at, :], v[at, :], 0))
    store_pieces(total, ORDERS[False][0], pieces, scratch)


def intra_kernel(q, k, v, intra, states, q_t):
    keep = causal()
    cols = q.shape[1]
    q_t[...] = q[...].T
    for h in range(cols // HEAD_DIM):
        part = head_slice(h)
        state = None
        for n, at in enumerate(chunk_slices(q.shape[0])):
            qi, ki, vi = q[at, part], k[at, part], v[at, part]
            scores = jnp.where(keep, dot(qi, ki, 1, 1), 0.0).astype(BF16)
            out = dot(scores, vi, 1, 0)
            if n:
                out = out + dot(qi, state.astype(BF16), 1, 0)
                states[(n - 1) * cols + part.start : (n - 1) * cols + part.stop, :] = state
            intra[at, part] = out
            new = dot(ki, vi, 0, 0)
            state = state + new if n else new


def row_sums(tile):
    return jnp.sum(tile.T, axis=0, keepdims=True)


def mixed_kernel(is_own, intra, q, g, *refs):
    pieces, refs = refs[:2], refs[2:]
    before, refs = ([], refs) if is_own else (refs[:2], refs[2:])
    mixed, prefix, *stats, scratch = refs
    load_pieces(pieces, ORDERS[False][1], scratch, 0 if is_own else 2)
    blocks = q.shape[0] // HEAD_DIM

    def pair(p):
        for at in chunk_slices(q.shape[0]):
            square = cross = None
            for j in range(2):
                part, whole = head_slice(j), head_slice(2 * p + j)
                m = intra[at, whole] + dot(q[at, whole], scratch[whole, :], 1, 0)
                mixed[at, part] = m
                s, c = m * m, m * g[at, whole].astype(F32)
                square = s if square is None else square + s
                cross = c if cross is None else cross + c
            for n in range(CHUNK // HEAD_DIM):
                for first, value in ((0, square), (blocks, cross)):
                    i = first + at.start // HEAD_DIM + n
                    sums = row_sums(value[head_slice(n)])
                    if before:
                        sums = sums + before[0][i : i + 1, :]
                    stats[0][i : i + 1, :] = sums
        part = slice(p * PAIR, (p + 1) * PAIR)
        prefix[part, :] = scratch[part, :]
        if before:
            part = slice((1 - p) * PAIR, (2 - p) * PAIR)
            prefix[part, :] = before[1][part, :]

    by_pair(lambda mine, other: pair(0 if mine else 1), is_own, not is_own)
    for copy in stats[1:]:
        copy[...] = stats[0][...]


def norm_kernel(width, mixed, oth_mixed, q_t, g, *refs):
    stats, (gm, inverse_out, states, *pieces, scratch) = refs[: -4 - QUAD], refs[-4 - QUAD :]
    total = stats[0][...]
    for r in stats[1:]:
        total = total + r[...]
    rows, cols = gm.shape
    blocks = rows // HEAD_DIM
    inverse = lax.rsqrt(total[:blocks] / width + EPSILON)
    cross_mean = total[blocks:] * inverse / width
    scale = inverse * inverse * cross_mean
    inverse_out[...] = inverse
    shape = (HEAD_DIM, HEAD_DIM)

    def body(*pairs):
        after = None
        for n, at in reversed(list(enumerate(chunk_slices(rows)))):
            for i in range(at.start // HEAD_DIM, at.stop // HEAD_DIM):
                block = head_slice(i)
                a = jnp.broadcast_to(inverse[i : i + 1], shape).T
                b = jnp.broadcast_to(scale[i : i + 1], shape).T
                for h in range(cols // HEAD_DIM):
                    part = head_slice(h)
                    value = pairs[h // 2][block, head_slice(h % 2)]
                    grad = g[block, part].astype(F32)
                    gm[block, part] = (grad * a - value * b).astype(BF16)
            after = add_all(after, pair_blocks(q_t[:, at], gm[at, :], 1))
            if n:
                for h, state in enumerate(after):
                    first = (n - 1) * cols + h * HEAD_DIM
                    states[first : first + HEAD_DIM, :] = state
        for h, state in enumerate(after):
            scratch[head_slice(h), :] = state

    by_pair(body, mixed, oth_mixed)
    for slot, piece in enumerate(pieces):
        piece[...] = scratch[rows_at(ORDERS[True][0], slot), :]


def head_grads(h, q, k, v, gm, prefix, states, after, gq, gk, gv, finished=None):
    cols, part = q.shape[1], head_slice(h)
    keep, keep_t = causal(), causal(True)
    chunks = chunk_slices(q.shape[0])
    first = prefix[part, :].astype(F32)
    for n, at in enumerate(chunks):
        qi, ki, vi, gi = q[at, part], k[at, part], v[at, part], gm[at, part]
        scores_t = jnp.where(keep_t, dot(ki, qi, 1, 1), 0.0).astype(BF16)
        grad_scores = jnp.where(keep, dot(gi, vi, 1, 1), 0.0).astype(BF16)
        grad_scores_t = jnp.where(keep_t, dot(vi, gi, 1, 1), 0.0).astype(BF16)
        entering = first
        if n:
            entering = first + states[pl.ds((n - 1) * cols + part.start, HEAD_DIM), :]
        gq_i = dot(grad_scores, ki, 1, 0) + dot(gi, entering.astype(BF16), 1, 1)
        gk_i = dot(grad_scores_t, qi, 1, 0)
        gv_i = dot(scores_t, gi, 1, 0)
        if n < len(chunks) - 1:
            later = after[pl.ds(n * cols + part.start, HEAD_DIM), :].astype(BF16)
            gk_i = gk_i + dot(vi, later, 1, 1)
            gv_i = gv_i + dot(ki, later, 1, 0)
        gq[at, :] = gq_i.astype(BF16)
        gk[at, :] = gk_i
        gv[at, :] = gv_i
        if finished is not None:
            finished(n, at)


def first_grads_kernel(q, k, v, gm, prefix, states, after, *refs):
    gqs, gks, gvs = refs[:2], refs[2:4], refs[4:]
    for h in range(2):
        head_grads(h, q, k, v, gm, prefix, states, after, gqs[h], gks[h], gvs[h])


def second_grads_kernel(q, k, v, gm, prefix, states, after, mixed, oth_mixed, inverse, *refs):
    gq, gk, gv, out_hbm, out, sems = refs[-6:]
    shape = (HEAD_DIM, HEAD_DIM)

    def body(*pairs):
        copies = []
        for n, at in enumerate(chunk_slices(q.shape[0])):
            for i in range(at.start // HEAD_DIM, at.stop // HEAD_DIM):
                a = jnp.broadcast_to(inverse[i : i + 1, :], shape).T
                for h in range(q.shape[1] // HEAD_DIM):
                    value = pairs[h // 2][head_slice(i), head_slice(h % 2)]
                    out[head_slice(i), head_slice(h)] = (value * a).astype(BF16)
            copies.append(pltpu.make_async_copy(out.at[at], out_hbm.at[at], sems.at[n]))
            copies[-1].start()
        head_grads(2, q, k, v, gm, prefix, states, after, gq, gk, gv)
        for copy in copies:
            copy.wait()

    by_pair(body, mixed, oth_mixed)


def third_grads_kernel(q, k, v, gm, prefix, states, after, *refs):
    gqs, (gk, gv, gq_hbm, gq, sems) = refs[:3], refs[-5:]
    copies = []

    def send(src, h, at, sem):
        copies.append(pltpu.make_async_copy(src.at[at], gq_hbm.at[at, head_slice(h)], sem))
        copies[-1].start()

    for h in range(3):
        send(gqs[h], h, slice(0, q.shape[0]), sems.at[h])
    head_grads(
        3, q, k, v, gm, prefix, states, after, gq, gk, gv, lambda n, at: send(gq, 3, at, sems.at[3 + n])
    )
    for copy in copies:
        copy.wait()


def last_kernel(k, v, *refs):
    gks, gvs, pieces = (refs[i * QUAD : (i + 1) * QUAD] for i in range(3))
    gk_hbm, gv_hbm, gk, gv, suffix, sems = refs[-6:]
    load_pieces(pieces, ORDERS[True][1], suffix)
    copies = []
    for j, (parts, left, contract, out, hbm) in enumerate(
        ((gvs, k, 0, gv, gv_hbm), (gks, v, 1, gk, gk_hbm))
    ):
        for n, at in enumerate(chunk_slices(k.shape[0])):
            for h in range(QUAD):
                part = head_slice(h)
                new = dot(left[at, part], suffix[part, :], 1, contract)
                out[at, part] = (parts[h][at, :] + new).astype(BF16)
            copies.append(pltpu.make_async_copy(out.at[at], hbm.at[at], sems.at[j, n]))
            copies[-1].start()
    for copy in copies:
        copy.wait()


def all_parts(values, axis):
    size = len(values)
    power = size & (size - 1) == 0
    parts = [values[0]]
    for by in reversed(range(1, size)):
        pairs = [(i, i ^ by if power else (i + by) % size) for i in range(size)]
        parts.append(lax.ppermute(values[by], axis, pairs))
    return parts


def shards(sizes, queries, keys, values, grad_out):
    seq, head_size = sizes
    rows, cols = queries.shape
    chunks = rows // CHUNK
    blocks = rows // HEAD_DIM
    scan = quad_scan if seq == 2 * QUAD else doubling_scan

    def shape(count, lanes, kind=F32):
        return jax.ShapeDtypeStruct((count, lanes), kind)

    wide, narrow = shape(rows, cols), shape(rows, cols, BF16)
    head_wide, head_narrow = shape(rows, HEAD_DIM), shape(rows, HEAD_DIM, BF16)
    pieces_shape = [shape(HEAD_DIM, HEAD_DIM)] * QUAD
    states_shape = shape((chunks - 1) * cols, HEAD_DIM)
    pieces_scratch = pltpu.VMEM((cols, HEAD_DIM), F32)
    head_flops = 2 * rows * HEAD_DIM * HEAD_DIM
    chunk_flops = 2 * rows * CHUNK * HEAD_DIM

    *pieces, keys, values = call(
        state_kernel,
        pieces_shape + [pltpu.VMEM((rows, cols), BF16)] * 2,
        [pltpu.with_memory_space_constraint(a, pltpu.HBM) for a in (keys, values)],
        QUAD * head_flops,
        "local_state",
        spaces={0: pltpu.HBM, 1: pltpu.HBM},
        scratch=[pieces_scratch, pltpu.SemaphoreType.DMA((2, chunks))],
    )

    def forward(phase, token):
        if phase:
            return []
        return call(
            intra_kernel,
            [wide, states_shape, shape(cols, rows, BF16)],
            [queries, keys, values],
            QUAD * (2 * chunk_flops + 2 * head_flops),
            "intra",
        )

    prefixes, (intra, states, queries_t) = scan(pieces, sizes, False, forward)
    stats_shape = shape(2 * blocks, HEAD_DIM)

    def mix(is_own, pieces, count, *before):
        return call(
            functools.partial(mixed_kernel, is_own),
            [shape(rows, PAIR), shape(cols, HEAD_DIM, BF16)] + [stats_shape] * count,
            [intra, queries, grad_out, *pieces, *before],
            2 * head_flops,
            "mixed",
            scratch=[pltpu.VMEM((cols, HEAD_DIM), BF16)],
        )

    mixed, prefix, stats = mix(True, prefixes[:2], 1)
    oth_mixed, prefix, *stats = mix(False, prefixes[2:], head_size, stats, prefix)
    gm, inverse, after, *pieces = call(
        functools.partial(norm_kernel, cols * head_size),
        [narrow, shape(blocks, HEAD_DIM), states_shape] + pieces_shape,
        [mixed, oth_mixed, queries_t, grad_out, *all_parts(stats, "head")],
        QUAD * head_flops,
        "norm",
        scratch=[pieces_scratch],
    )
    args = [queries, keys, values, gm, prefix, states, after]
    grads_flops = 6 * chunk_flops + 3 * head_flops

    def backward(phase, token):
        if phase == 0:
            parts = call(
                first_grads_kernel,
                [head_narrow] * 2 + [head_wide] * 4,
                args,
                2 * grads_flops,
                "first_grads",
            )
        elif phase == 1:
            parts = call(
                second_grads_kernel,
                [head_narrow] + [head_wide] * 2 + [narrow],
                args + [mixed, oth_mixed, inverse, token],
                grads_flops,
                "second_grads",
                spaces={len(args) + 3: pl.ANY},
                outs={3: pl.ANY},
                scratch=[pltpu.VMEM((rows, cols), BF16), pltpu.SemaphoreType.DMA((chunks,))],
            )
        else:
            parts = call(
                third_grads_kernel,
                [head_wide] * 2 + [narrow],
                args + gqs + [token],
                grads_flops,
                "third_grads",
                spaces={len(args) + 3: pl.ANY},
                outs={2: pl.ANY},
                scratch=[
                    pltpu.VMEM((rows, HEAD_DIM), BF16),
                    pltpu.SemaphoreType.DMA((3 + chunks,)),
                ],
            )
        if phase < 2:
            count = 2 - phase
            gqs.extend(parts[:count])
            parts = parts[count:]
        count = 2 if phase == 0 else 1
        gks.extend(parts[:count])
        gvs.extend(parts[count : 2 * count])
        results.extend(parts[2 * count :])
        return gks[-1:]

    gqs, gks, gvs, results = [], [], [], []
    suffixes, unused = scan(pieces, sizes, True, backward)
    output, grad_q = results
    grad_k, grad_v = call(
        last_kernel,
        [narrow, narrow],
        [keys, values, *gks, *gvs, *suffixes],
        2 * QUAD * head_flops,
        "last",
        outs={0: pl.ANY, 1: pl.ANY},
        scratch=[pltpu.VMEM((rows, cols), BF16)] * 2
        + [pltpu.VMEM((cols, HEAD_DIM), BF16), pltpu.SemaphoreType.DMA((2, chunks))],
    )
    return output, grad_q, grad_k, grad_v


def solution(mesh):
    sizes = (mesh.shape["seq"], mesh.shape["head"])
    spec = P("seq", "head")
    return jax.shard_map(
        functools.partial(shards, sizes),
        mesh=mesh,
        in_specs=(spec,) * 4,
        out_specs=(spec,) * 4,
        check_vma=False,
    )
```

```python
import functools
import math

import jax
import jax.numpy as jnp
from jax import lax
from jax.experimental import pallas as pl
from jax.experimental.pallas import tpu as pltpu
from jax.sharding import PartitionSpec as P

HEAD_DIM = 128
EPSILON = 1e-06
CHUNK = 256
PAIR = 2 * HEAD_DIM
QUAD = 4
ORDERS = {
    False: (((3, 2, 1), (3, 2, 1)), ((3, 2, 1), (3, 2, 1))),
    True: (((3, 1, 2), (3, 1, 2)), ((3, 1, 2), (3, 1, 2))),
}
F32 = jnp.float32
BF16 = jnp.bfloat16


def dot(a, b, ca, cb):
    return lax.dot_general(a, b, (((ca,), (cb,)), ((), ())), preferred_element_type=F32)


def head_slice(h):
    return slice(h * HEAD_DIM, (h + 1) * HEAD_DIM)


def chunk_slices(rows, size=CHUNK):
    return [slice(start, start + size) for start in range(0, rows, size)]


def causal(transposed=False):
    rows = lax.broadcasted_iota(jnp.int32, (CHUNK, CHUNK), 0)
    cols = lax.broadcasted_iota(jnp.int32, (CHUNK, CHUNK), 1)
    return cols >= rows if transposed else rows >= cols


def call(body, out_shape, args, flops, name, spaces=None, outs=None, scratch=()):
    size = sum(a.size * a.dtype.itemsize for a in args)
    size += sum(math.prod(a.shape) * a.dtype.itemsize for a in out_shape)
    spaces, outs = spaces or {}, outs or {}
    kernel = pl.pallas_call(
        body,
        out_shape=out_shape,
        in_specs=[
            pl.BlockSpec(memory_space=spaces.get(i, pltpu.VMEM)) for i in range(len(args))
        ],
        out_specs=[
            pl.BlockSpec(memory_space=outs.get(i, pltpu.VMEM)) for i in range(len(out_shape))
        ],
        scratch_shapes=list(scratch),
        compiler_params=pltpu.CompilerParams(vmem_limit_bytes=20 * 2**20),
        cost_estimate=pl.CostEstimate(flops=flops, bytes_accessed=size, transcendentals=0),
        name=name,
    )
    return list(kernel(*args))


def partner(order, slot):
    if slot == 0:
        return 0
    even, odd = (choice[slot - 1] for choice in order)
    if even == odd:
        return even
    return jnp.where(lax.rem(lax.axis_index("head"), 2) == 1, odd, even)


def number_at(order, slot):
    return lax.rem(lax.axis_index("seq"), QUAD) ^ partner(order, slot)


def pair_of(number):
    return lax.rem(number, 2) ^ (number // 2)


def head_at(order, slot):
    number = number_at(order, slot)
    return 2 * pair_of(number) + number // 2


def rows_at(order, slot):
    return pl.ds(pl.multiple_of(head_at(order, slot) * HEAD_DIM, HEAD_DIM), HEAD_DIM)


def by_pair(body, mine, other):
    pair = pair_of(lax.rem(lax.axis_index("seq"), QUAD))
    pl.when(pair == 0)(functools.partial(body, mine, other))
    pl.when(pair == 1)(functools.partial(body, other, mine))


def exchange(value, sizes, by):
    size, heads = sizes
    pairs = [
        (i * heads + h, (i ^ by[h % 2]) * heads + h) for i in range(size) for h in range(heads)
    ]
    return lax.ppermute(value, ("seq", "head"), pairs)


def exchange_all(pieces, sizes, order):
    even, odd = order
    return pieces[:1] + [exchange(p, sizes, by) for p, by in zip(pieces[1:], zip(even, odd))]


def quad_kernel(*refs):
    refs[-1][...] = (refs[0][...] + refs[1][...]) + (refs[2][...] + refs[3][...])


def finish_kernel(reverse, *refs):
    into, out_of = ORDERS[reverse]
    place = lax.axis_index("seq")
    zero = jnp.zeros(refs[0].shape, F32)
    second = place < QUAD if reverse else place >= QUAD
    before = jnp.where(second, refs[QUAD][...], zero)
    for to, out in enumerate(refs[-QUAD:]):
        here = number_at(out_of, to)
        total = before
        for slot in range(QUAD):
            number = number_at(into, slot)
            ahead = number > here if reverse else number < here
            total = total + jnp.where(ahead, refs[slot][...], zero)
        out[...] = total


def quad_scan(pieces, sizes, reverse, between):
    head = jax.ShapeDtypeStruct((HEAD_DIM, HEAD_DIM), F32)
    into, out_of = ORDERS[reverse]
    pieces = exchange_all(pieces, sizes, into)
    first = between(0, None)
    (total,) = call(
        quad_kernel, [head], [*pieces, *first[-1:]], 0, "quad_sum", spaces={4: pl.ANY}
    )
    far = exchange(total, sizes, (QUAD, QUAD))
    second = between(1, total)
    finished = call(
        functools.partial(finish_kernel, reverse),
        [head] * QUAD,
        [*pieces, far, *second[-1:]],
        0,
        "finish",
        spaces={5: pl.ANY},
    )
    third = between(2, finished[0])
    return exchange_all(finished, sizes, out_of), first + second + third


def doubling_scan(pieces, sizes, reverse, between):
    size = sizes[0]

    def shift(value, by):
        pairs = [(i, i + by) for i in range(size - by)]
        if reverse:
            pairs = [(b, a) for a, b in pairs]
        return lax.ppermute(value, "seq", pairs)

    into, out_of = (
        jnp.stack([head_at(order, slot) for slot in range(QUAD)]) for order in ORDERS[reverse]
    )
    state = jnp.stack(pieces)[jnp.argsort(into)]
    by = 1
    while by < size:
        state = state + shift(state, by)
        by *= 2
    state = shift(state, 1)[out_of]
    done = []
    for phase in range(3):
        done += between(phase, done[-1] if done else None)
    return [state[n] for n in range(QUAD)], done


def store_pieces(states, order, pieces, scratch):
    for h, state in enumerate(states):
        scratch[head_slice(h), :] = state
    for slot, piece in enumerate(pieces):
        piece[...] = scratch[rows_at(order, slot), :]


def load_pieces(pieces, order, rounded, first=0):
    for slot, piece in enumerate(pieces, first):
        rounded[rows_at(order, slot), :] = piece[...].astype(BF16)


def pair_blocks(left, right, contract):
    blocks = []
    for p in range(right.shape[1] // PAIR):
        cols = slice(p * PAIR, (p + 1) * PAIR)
        full = dot(left[:, cols] if contract == 0 else left[cols, :], right[:, cols], contract, 0)
        blocks += [full[:HEAD_DIM, :HEAD_DIM], full[HEAD_DIM:, HEAD_DIM:]]
    return blocks


def add_all(a, b):
    return b if a is None else [x + y for x, y in zip(a, b)]


def state_kernel(k_hbm, v_hbm, *refs):
    pieces, (k, v, scratch, sems) = refs[:QUAD], refs[QUAD:]
    chunks = chunk_slices(k.shape[0])
    copies = []
    for n, at in enumerate(chunks):
        for j, (src, dst) in enumerate(((k_hbm, k), (v_hbm, v))):
            copies.append(pltpu.make_async_copy(src.at[at], dst.at[at], sems.at[j, n]))
            copies[-1].start()
    total = None
    for n, at in enumerate(chunks):
        copies[2 * n].wait()
        copies[2 * n + 1].wait()
        total = add_all(total, pair_blocks(k[at, :], v[at, :], 0))
    store_pieces(total, ORDERS[False][0], pieces, scratch)


def intra_kernel(q, k, v, intra, states, q_t):
    keep = causal()
    cols = q.shape[1]
    q_t[...] = q[...].T
    for h in range(cols // HEAD_DIM):
        part = head_slice(h)
        state = None
        for n, at in enumerate(chunk_slices(q.shape[0])):
            qi, ki, vi = q[at, part], k[at, part], v[at, part]
            scores = jnp.where(keep, dot(qi, ki, 1, 1), 0.0).astype(BF16)
            out = dot(scores, vi, 1, 0)
            if n:
                out = out + dot(qi, state.astype(BF16), 1, 0)
                states[(n - 1) * cols + part.start : (n - 1) * cols + part.stop, :] = state
            intra[at, part] = out
            new = dot(ki, vi, 0, 0)
            state = state + new if n else new


def scores_kernel(q, k, token, scores_t):
    keep = causal(True)
    rows = q.shape[0]
    for h in range(q.shape[1] // HEAD_DIM):
        part = head_slice(h)
        for at in chunk_slices(rows):
            raw = dot(k[at, part], q[at, part], 1, 1)
            to = slice(h * rows + at.start, h * rows + at.stop)
            scores_t[to, :] = jnp.where(keep, raw, 0.0).astype(BF16)


def row_sums(tile):
    return jnp.sum(tile.T, axis=0, keepdims=True)


def mixed_kernel(is_own, intra, q, g, *refs):
    pieces, refs = refs[:2], refs[2:]
    before, refs = ([], refs) if is_own else (refs[:2], refs[2:])
    mixed, prefix, *stats, scratch = refs
    load_pieces(pieces, ORDERS[False][1], scratch, 0 if is_own else 2)
    blocks = q.shape[0] // HEAD_DIM

    def pair(p):
        for at in chunk_slices(q.shape[0]):
            square = cross = None
            for j in range(2):
                part, whole = head_slice(j), head_slice(2 * p + j)
                m = intra[at, whole] + dot(q[at, whole], scratch[whole, :], 1, 0)
                mixed[at, part] = m
                s, c = m * m, m * g[at, whole].astype(F32)
                square = s if square is None else square + s
                cross = c if cross is None else cross + c
            for n in range(CHUNK // HEAD_DIM):
                for first, value in ((0, square), (blocks, cross)):
                    i = first + at.start // HEAD_DIM + n
                    sums = row_sums(value[head_slice(n)])
                    if before:
                        sums = sums + before[0][i : i + 1, :]
                    stats[0][i : i + 1, :] = sums
        part = slice(p * PAIR, (p + 1) * PAIR)
        prefix[part, :] = scratch[part, :]
        if before:
            part = slice((1 - p) * PAIR, (2 - p) * PAIR)
            prefix[part, :] = before[1][part, :]

    by_pair(lambda mine, other: pair(0 if mine else 1), is_own, not is_own)
    for copy in stats[1:]:
        copy[...] = stats[0][...]


def norm_kernel(width, mixed, oth_mixed, q_t, g, *refs):
    stats, (gm, inverse_out, states, *pieces, scratch) = refs[: -4 - QUAD], refs[-4 - QUAD :]
    total = stats[0][...]
    for r in stats[1:]:
        total = total + r[...]
    rows, cols = gm.shape
    blocks = rows // HEAD_DIM
    inverse = lax.rsqrt(total[:blocks] / width + EPSILON)
    cross_mean = total[blocks:] * inverse / width
    scale = inverse * inverse * cross_mean
    inverse_out[...] = inverse
    shape = (HEAD_DIM, HEAD_DIM)

    def body(*pairs):
        after = None
        for n, at in reversed(list(enumerate(chunk_slices(rows)))):
            for i in range(at.start // HEAD_DIM, at.stop // HEAD_DIM):
                block = head_slice(i)
                a = jnp.broadcast_to(inverse[i : i + 1], shape).T
                b = jnp.broadcast_to(scale[i : i + 1], shape).T
                for h in range(cols // HEAD_DIM):
                    part = head_slice(h)
                    value = pairs[h // 2][block, head_slice(h % 2)]
                    grad = g[block, part].astype(F32)
                    gm[block, part] = (grad * a - value * b).astype(BF16)
            after = add_all(after, pair_blocks(q_t[:, at], gm[at, :], 1))
            if n:
                for h, state in enumerate(after):
                    first = (n - 1) * cols + h * HEAD_DIM
                    states[first : first + HEAD_DIM, :] = state
        for h, state in enumerate(after):
            scratch[head_slice(h), :] = state

    by_pair(body, mixed, oth_mixed)
    for slot, piece in enumerate(pieces):
        piece[...] = scratch[rows_at(ORDERS[True][0], slot), :]


def head_grads(h, q, k, v, gm, prefix, states, after, scores, gq, gk, gv, finished=None):
    (rows, cols), part = q.shape, head_slice(h)
    keep, keep_t = causal(), causal(True)
    chunks = chunk_slices(q.shape[0])
    first = prefix[part, :].astype(F32)
    for n, at in enumerate(chunks):
        qi, ki, vi, gi = q[at, part], k[at, part], v[at, part], gm[at, part]
        scores_t = scores[h * rows + at.start : h * rows + at.stop, :]
        grad_scores = jnp.where(keep, dot(gi, vi, 1, 1), 0.0).astype(BF16)
        grad_scores_t = jnp.where(keep_t, dot(vi, gi, 1, 1), 0.0).astype(BF16)
        entering = first
        if n:
            entering = first + states[pl.ds((n - 1) * cols + part.start, HEAD_DIM), :]
        gq_i = dot(grad_scores, ki, 1, 0) + dot(gi, entering.astype(BF16), 1, 1)
        gk_i = dot(grad_scores_t, qi, 1, 0)
        gv_i = dot(scores_t, gi, 1, 0)
        if n < len(chunks) - 1:
            later = after[pl.ds(n * cols + part.start, HEAD_DIM), :].astype(BF16)
            gk_i = gk_i + dot(vi, later, 1, 1)
            gv_i = gv_i + dot(ki, later, 1, 0)
        gq[at, :] = gq_i.astype(BF16)
        gk[at, :] = gk_i
        gv[at, :] = gv_i
        if finished is not None:
            finished(n, at)


def first_grads_kernel(q, k, v, gm, prefix, states, after, scores, *refs):
    gqs, gks, gvs = refs[:2], refs[2:4], refs[4:]
    for h in range(2):
        head_grads(h, q, k, v, gm, prefix, states, after, scores, gqs[h], gks[h], gvs[h])


def second_grads_kernel(q, k, v, gm, prefix, states, after, scores, *refs):
    mixed, oth_mixed, inverse = refs[:3]
    gq, gk, gv, out_hbm, out, sems = refs[-6:]
    shape = (HEAD_DIM, HEAD_DIM)

    def body(*pairs):
        copies = []
        for n, at in enumerate(chunk_slices(q.shape[0])):
            for i in range(at.start // HEAD_DIM, at.stop // HEAD_DIM):
                a = jnp.broadcast_to(inverse[i : i + 1, :], shape).T
                for h in range(q.shape[1] // HEAD_DIM):
                    value = pairs[h // 2][head_slice(i), head_slice(h % 2)]
                    out[head_slice(i), head_slice(h)] = (value * a).astype(BF16)
            copies.append(pltpu.make_async_copy(out.at[at], out_hbm.at[at], sems.at[n]))
            copies[-1].start()
        head_grads(2, q, k, v, gm, prefix, states, after, scores, gq, gk, gv)
        for copy in copies:
            copy.wait()

    by_pair(body, mixed, oth_mixed)


def third_grads_kernel(q, k, v, gm, prefix, states, after, scores, *refs):
    gqs, (gk, gv, gq_hbm, gq, sems) = refs[:3], refs[-5:]
    copies = []

    def send(src, h, at, sem):
        copies.append(pltpu.make_async_copy(src.at[at], gq_hbm.at[at, head_slice(h)], sem))
        copies[-1].start()

    for h in range(3):
        send(gqs[h], h, slice(0, q.shape[0]), sems.at[h])
    head_grads(
        3, q, k, v, gm, prefix, states, after, scores, gq, gk, gv, lambda n, at: send(gq, 3, at, sems.at[3 + n])
    )
    for copy in copies:
        copy.wait()


def last_kernel(k, v, *refs):
    gks, gvs, pieces = (refs[i * QUAD : (i + 1) * QUAD] for i in range(3))
    gk_hbm, gv_hbm, gk, gv, suffix, sems = refs[-6:]
    load_pieces(pieces, ORDERS[True][1], suffix)
    copies = []
    for j, (parts, left, contract, out, hbm) in enumerate(
        ((gvs, k, 0, gv, gv_hbm), (gks, v, 1, gk, gk_hbm))
    ):
        for n, at in enumerate(chunk_slices(k.shape[0])):
            for h in range(QUAD):
                part = head_slice(h)
                new = dot(left[at, part], suffix[part, :], 1, contract)
                out[at, part] = (parts[h][at, :] + new).astype(BF16)
            copies.append(pltpu.make_async_copy(out.at[at], hbm.at[at], sems.at[j, n]))
            copies[-1].start()
    for copy in copies:
        copy.wait()


def all_parts(values, axis):
    size = len(values)
    power = size & (size - 1) == 0
    parts = [values[0]]
    for by in reversed(range(1, size)):
        pairs = [(i, i ^ by if power else (i + by) % size) for i in range(size)]
        parts.append(lax.ppermute(values[by], axis, pairs))
    return parts


def shards(sizes, queries, keys, values, grad_out):
    seq, head_size = sizes
    rows, cols = queries.shape
    chunks = rows // CHUNK
    blocks = rows // HEAD_DIM
    scan = quad_scan if seq == 2 * QUAD else doubling_scan

    def shape(count, lanes, kind=F32):
        return jax.ShapeDtypeStruct((count, lanes), kind)

    wide, narrow = shape(rows, cols), shape(rows, cols, BF16)
    head_wide, head_narrow = shape(rows, HEAD_DIM), shape(rows, HEAD_DIM, BF16)
    pieces_shape = [shape(HEAD_DIM, HEAD_DIM)] * QUAD
    states_shape = shape((chunks - 1) * cols, HEAD_DIM)
    pieces_scratch = pltpu.VMEM((cols, HEAD_DIM), F32)
    head_flops = 2 * rows * HEAD_DIM * HEAD_DIM
    chunk_flops = 2 * rows * CHUNK * HEAD_DIM

    *pieces, keys, values = call(
        state_kernel,
        pieces_shape + [pltpu.VMEM((rows, cols), BF16)] * 2,
        [pltpu.with_memory_space_constraint(a, pltpu.HBM) for a in (keys, values)],
        QUAD * head_flops,
        "local_state",
        spaces={0: pltpu.HBM, 1: pltpu.HBM},
        scratch=[pieces_scratch, pltpu.SemaphoreType.DMA((2, chunks))],
    )

    def forward(phase, token):
        if phase == 2:
            return []
        if phase == 1:
            return call(
                scores_kernel,
                [shape(QUAD * rows, CHUNK, BF16)],
                [queries, keys, token],
                QUAD * chunk_flops,
                "scores",
                spaces={2: pl.ANY},
            )
        return call(
            intra_kernel,
            [wide, states_shape, shape(cols, rows, BF16)],
            [queries, keys, values],
            QUAD * (2 * chunk_flops + 2 * head_flops),
            "intra",
        )

    prefixes, (intra, states, queries_t, scores) = scan(pieces, sizes, False, forward)
    stats_shape = shape(2 * blocks, HEAD_DIM)

    def mix(is_own, pieces, count, *before):
        return call(
            functools.partial(mixed_kernel, is_own),
            [shape(rows, PAIR), shape(cols, HEAD_DIM, BF16)] + [stats_shape] * count,
            [intra, queries, grad_out, *pieces, *before],
            2 * head_flops,
            "mixed",
            scratch=[pltpu.VMEM((cols, HEAD_DIM), BF16)],
        )

    mixed, prefix, stats = mix(True, prefixes[:2], 1)
    oth_mixed, prefix, *stats = mix(False, prefixes[2:], head_size, stats, prefix)
    gm, inverse, after, *pieces = call(
        functools.partial(norm_kernel, cols * head_size),
        [narrow, shape(blocks, HEAD_DIM), states_shape] + pieces_shape,
        [mixed, oth_mixed, queries_t, grad_out, *all_parts(stats, "head")],
        QUAD * head_flops,
        "norm",
        scratch=[pieces_scratch],
    )
    args = [queries, keys, values, gm, prefix, states, after, scores]
    grads_flops = 5 * chunk_flops + 3 * head_flops

    def backward(phase, token):
        if phase == 0:
            parts = call(
                first_grads_kernel,
                [head_narrow] * 2 + [head_wide] * 4,
                args,
                2 * grads_flops,
                "first_grads",
            )
        elif phase == 1:
            parts = call(
                second_grads_kernel,
                [head_narrow] + [head_wide] * 2 + [narrow],
                args + [mixed, oth_mixed, inverse, token],
                grads_flops,
                "second_grads",
                spaces={len(args) + 3: pl.ANY},
                outs={3: pl.ANY},
                scratch=[pltpu.VMEM((rows, cols), BF16), pltpu.SemaphoreType.DMA((chunks,))],
            )
        else:
            parts = call(
                third_grads_kernel,
                [head_wide] * 2 + [narrow],
                args + gqs + [token],
                grads_flops,
                "third_grads",
                spaces={len(args) + 3: pl.ANY},
                outs={2: pl.ANY},
                scratch=[
                    pltpu.VMEM((rows, HEAD_DIM), BF16),
                    pltpu.SemaphoreType.DMA((3 + chunks,)),
                ],
            )
        if phase < 2:
            count = 2 - phase
            gqs.extend(parts[:count])
            parts = parts[count:]
        count = 2 if phase == 0 else 1
        gks.extend(parts[:count])
        gvs.extend(parts[count : 2 * count])
        results.extend(parts[2 * count :])
        return gks[-1:]

    gqs, gks, gvs, results = [], [], [], []
    suffixes, unused = scan(pieces, sizes, True, backward)
    output, grad_q = results
    grad_k, grad_v = call(
        last_kernel,
        [narrow, narrow],
        [keys, values, *gks, *gvs, *suffixes],
        2 * QUAD * head_flops,
        "last",
        outs={0: pl.ANY, 1: pl.ANY},
        scratch=[pltpu.VMEM((rows, cols), BF16)] * 2
        + [pltpu.VMEM((cols, HEAD_DIM), BF16), pltpu.SemaphoreType.DMA((2, chunks))],
    )
    return output, grad_q, grad_k, grad_v


def solution(mesh):
    sizes = (mesh.shape["seq"], mesh.shape["head"])
    spec = P("seq", "head")
    return jax.shard_map(
        functools.partial(shards, sizes),
        mesh=mesh,
        in_specs=(spec,) * 4,
        out_specs=(spec,) * 4,
        check_vma=False,
    )
```

```python
import functools
import math

import jax
import jax.numpy as jnp
from jax import lax
from jax.experimental import pallas as pl
from jax.experimental.pallas import tpu as pltpu
from jax.sharding import PartitionSpec as P

HEAD_DIM = 128
EPSILON = 1e-06
CHUNK = 256
PAIR = 2 * HEAD_DIM
QUAD = 4
ORDERS = {
    False: (((3, 2, 1), (3, 2, 1)), ((3, 2, 1), (3, 2, 1))),
    True: (((3, 1, 2), (3, 1, 2)), ((3, 1, 2), (3, 1, 2))),
}
F32 = jnp.float32
BF16 = jnp.bfloat16


def dot(a, b, ca, cb):
    return lax.dot_general(a, b, (((ca,), (cb,)), ((), ())), preferred_element_type=F32)


def head_slice(h):
    return slice(h * HEAD_DIM, (h + 1) * HEAD_DIM)


def chunk_slices(rows, size=CHUNK):
    return [slice(start, start + size) for start in range(0, rows, size)]


def causal(transposed=False):
    rows = lax.broadcasted_iota(jnp.int32, (CHUNK, CHUNK), 0)
    cols = lax.broadcasted_iota(jnp.int32, (CHUNK, CHUNK), 1)
    return cols >= rows if transposed else rows >= cols


def call(body, out_shape, args, flops, name, spaces=None, outs=None, scratch=()):
    size = sum(a.size * a.dtype.itemsize for a in args)
    size += sum(math.prod(a.shape) * a.dtype.itemsize for a in out_shape)
    spaces, outs = spaces or {}, outs or {}
    kernel = pl.pallas_call(
        body,
        out_shape=out_shape,
        in_specs=[
            pl.BlockSpec(memory_space=spaces.get(i, pltpu.VMEM)) for i in range(len(args))
        ],
        out_specs=[
            pl.BlockSpec(memory_space=outs.get(i, pltpu.VMEM)) for i in range(len(out_shape))
        ],
        scratch_shapes=list(scratch),
        compiler_params=pltpu.CompilerParams(vmem_limit_bytes=20 * 2**20),
        cost_estimate=pl.CostEstimate(flops=flops, bytes_accessed=size, transcendentals=0),
        name=name,
    )
    return list(kernel(*args))


def partner(order, slot):
    if slot == 0:
        return 0
    even, odd = (choice[slot - 1] for choice in order)
    if even == odd:
        return even
    return jnp.where(lax.rem(lax.axis_index("head"), 2) == 1, odd, even)


def number_at(order, slot):
    return lax.rem(lax.axis_index("seq"), QUAD) ^ partner(order, slot)


def pair_of(number):
    return lax.rem(number, 2) ^ (number // 2)


def head_at(order, slot):
    number = number_at(order, slot)
    return 2 * pair_of(number) + number // 2


def rows_at(order, slot):
    return pl.ds(pl.multiple_of(head_at(order, slot) * HEAD_DIM, HEAD_DIM), HEAD_DIM)


def by_pair(body, mine, other):
    pair = pair_of(lax.rem(lax.axis_index("seq"), QUAD))
    pl.when(pair == 0)(functools.partial(body, mine, other))
    pl.when(pair == 1)(functools.partial(body, other, mine))


def exchange(value, sizes, by):
    size, heads = sizes
    pairs = [
        (i * heads + h, (i ^ by[h % 2]) * heads + h) for i in range(size) for h in range(heads)
    ]
    return lax.ppermute(value, ("seq", "head"), pairs)


def exchange_all(pieces, sizes, order):
    even, odd = order
    return pieces[:1] + [exchange(p, sizes, by) for p, by in zip(pieces[1:], zip(even, odd))]


def quad_kernel(*refs):
    refs[-1][...] = (refs[0][...] + refs[1][...]) + (refs[2][...] + refs[3][...])


def finish_kernel(reverse, *refs):
    into, out_of = ORDERS[reverse]
    place = lax.axis_index("seq")
    zero = jnp.zeros(refs[0].shape, F32)
    second = place < QUAD if reverse else place >= QUAD
    before = jnp.where(second, refs[QUAD][...], zero)
    for to, out in enumerate(refs[-QUAD:]):
        here = number_at(out_of, to)
        total = before
        for slot in range(QUAD):
            number = number_at(into, slot)
            ahead = number > here if reverse else number < here
            total = total + jnp.where(ahead, refs[slot][...], zero)
        out[...] = total


def quad_scan(pieces, sizes, reverse, between):
    head = jax.ShapeDtypeStruct((HEAD_DIM, HEAD_DIM), F32)
    into, out_of = ORDERS[reverse]
    pieces = exchange_all(pieces, sizes, into)
    first = between(0, None)
    (total,) = call(
        quad_kernel, [head], [*pieces, *first[-1:]], 0, "quad_sum", spaces={4: pl.ANY}
    )
    far = exchange(total, sizes, (QUAD, QUAD))
    second = between(1, total)
    finished = call(
        functools.partial(finish_kernel, reverse),
        [head] * QUAD,
        [*pieces, far, *second[-1:]],
        0,
        "finish",
        spaces={5: pl.ANY},
    )
    third = between(2, finished[0])
    return exchange_all(finished, sizes, out_of), first + second + third


def doubling_scan(pieces, sizes, reverse, between):
    size = sizes[0]

    def shift(value, by):
        pairs = [(i, i + by) for i in range(size - by)]
        if reverse:
            pairs = [(b, a) for a, b in pairs]
        return lax.ppermute(value, "seq", pairs)

    into, out_of = (
        jnp.stack([head_at(order, slot) for slot in range(QUAD)]) for order in ORDERS[reverse]
    )
    state = jnp.stack(pieces)[jnp.argsort(into)]
    by = 1
    while by < size:
        state = state + shift(state, by)
        by *= 2
    state = shift(state, 1)[out_of]
    done = []
    for phase in range(3):
        done += between(phase, done[-1] if done else None)
    return [state[n] for n in range(QUAD)], done


def store_pieces(states, order, pieces, scratch):
    for h, state in enumerate(states):
        scratch[head_slice(h), :] = state
    for slot, piece in enumerate(pieces):
        piece[...] = scratch[rows_at(order, slot), :]


def load_pieces(pieces, order, rounded, first=0):
    for slot, piece in enumerate(pieces, first):
        rounded[rows_at(order, slot), :] = piece[...].astype(BF16)


def pair_blocks(left, right, contract):
    blocks = []
    for p in range(right.shape[1] // PAIR):
        cols = slice(p * PAIR, (p + 1) * PAIR)
        full = dot(left[:, cols] if contract == 0 else left[cols, :], right[:, cols], contract, 0)
        blocks += [full[:HEAD_DIM, :HEAD_DIM], full[HEAD_DIM:, HEAD_DIM:]]
    return blocks


def add_all(a, b):
    return b if a is None else [x + y for x, y in zip(a, b)]


def state_kernel(k_hbm, v_hbm, *refs):
    pieces, (k, v, scratch, sems) = refs[:QUAD], refs[QUAD:]
    chunks = chunk_slices(k.shape[0])
    copies = []
    for n, at in enumerate(chunks):
        for j, (src, dst) in enumerate(((k_hbm, k), (v_hbm, v))):
            copies.append(pltpu.make_async_copy(src.at[at], dst.at[at], sems.at[j, n]))
            copies[-1].start()
    total = None
    for n, at in enumerate(chunks):
        copies[2 * n].wait()
        copies[2 * n + 1].wait()
        total = add_all(total, pair_blocks(k[at, :], v[at, :], 0))
    store_pieces(total, ORDERS[False][0], pieces, scratch)


def intra_kernel(q, k, v, intra, states, q_t):
    keep = causal()
    cols = q.shape[1]
    q_t[...] = q[...].T
    for h in range(cols // HEAD_DIM):
        part = head_slice(h)
        state = None
        for n, at in enumerate(chunk_slices(q.shape[0])):
            qi, ki, vi = q[at, part], k[at, part], v[at, part]
            scores = jnp.where(keep, dot(qi, ki, 1, 1), 0.0).astype(BF16)
            out = dot(scores, vi, 1, 0)
            if n:
                out = out + dot(qi, state.astype(BF16), 1, 0)
                states[(n - 1) * cols + part.start : (n - 1) * cols + part.stop, :] = state
            intra[at, part] = out
            new = dot(ki, vi, 0, 0)
            state = state + new if n else new


def row_sums(tile):
    return jnp.sum(tile.T, axis=0, keepdims=True)


def mixed_kernel(is_own, intra, q, g, *refs):
    pieces, refs = refs[:2], refs[2:]
    before, refs = ([], refs) if is_own else (refs[:2], refs[2:])
    mixed, prefix, *stats = refs
    in_order = number_at(ORDERS[False][1], 0 if is_own else 2) // 2 == 0
    one, two = (piece[...].astype(BF16) for piece in pieces)
    states = [jnp.where(in_order, one, two), jnp.where(in_order, two, one)]
    blocks = q.shape[0] // HEAD_DIM

    def pair(p):
        for at in chunk_slices(q.shape[0]):
            square = cross = None
            for j in range(2):
                part, whole = head_slice(j), head_slice(2 * p + j)
                m = intra[at, whole] + dot(q[at, whole], states[j], 1, 0)
                mixed[at, part] = m
                s, c = m * m, m * g[at, whole].astype(F32)
                square = s if square is None else square + s
                cross = c if cross is None else cross + c
            for n in range(CHUNK // HEAD_DIM):
                for first, value in ((0, square), (blocks, cross)):
                    i = first + at.start // HEAD_DIM + n
                    sums = row_sums(value[head_slice(n)])
                    if before:
                        sums = sums + before[0][i : i + 1, :]
                    stats[0][i : i + 1, :] = sums
        for j in range(2):
            prefix[head_slice(2 * p + j), :] = states[j]
        if before:
            part = slice((1 - p) * PAIR, (2 - p) * PAIR)
            prefix[part, :] = before[1][part, :]

    by_pair(lambda mine, other: pair(0 if mine else 1), is_own, not is_own)
    for copy in stats[1:]:
        copy[...] = stats[0][...]


def norm_kernel(width, mixed, oth_mixed, q_t, g, *refs):
    stats, (gm, inverse_out, states, *pieces, scratch) = refs[: -4 - QUAD], refs[-4 - QUAD :]
    total = stats[0][...]
    for r in stats[1:]:
        total = total + r[...]
    rows, cols = gm.shape
    blocks = rows // HEAD_DIM
    inverse = lax.rsqrt(total[:blocks] / width + EPSILON)
    cross_mean = total[blocks:] * inverse / width
    scale = inverse * inverse * cross_mean
    inverse_out[...] = inverse
    shape = (HEAD_DIM, HEAD_DIM)

    def body(*pairs):
        after = None
        for n, at in reversed(list(enumerate(chunk_slices(rows)))):
            for i in range(at.start // HEAD_DIM, at.stop // HEAD_DIM):
                block = head_slice(i)
                a = jnp.broadcast_to(inverse[i : i + 1], shape).T
                b = jnp.broadcast_to(scale[i : i + 1], shape).T
                for h in range(cols // HEAD_DIM):
                    part = head_slice(h)
                    value = pairs[h // 2][block, head_slice(h % 2)]
                    grad = g[block, part].astype(F32)
                    gm[block, part] = (grad * a - value * b).astype(BF16)
            after = add_all(after, pair_blocks(q_t[:, at], gm[at, :], 1))
            if n:
                for h, state in enumerate(after):
                    first = (n - 1) * cols + h * HEAD_DIM
                    states[first : first + HEAD_DIM, :] = state
        for h, state in enumerate(after):
            scratch[head_slice(h), :] = state

    by_pair(body, mixed, oth_mixed)
    for slot, piece in enumerate(pieces):
        piece[...] = scratch[rows_at(ORDERS[True][0], slot), :]


def head_grads(h, q, k, v, gm, prefix, states, after, gq, gk, gv, finished=None):
    cols, part = q.shape[1], head_slice(h)
    keep, keep_t = causal(), causal(True)
    chunks = chunk_slices(q.shape[0])
    first = prefix[part, :].astype(F32)
    for n, at in enumerate(chunks):
        qi, ki, vi, gi = q[at, part], k[at, part], v[at, part], gm[at, part]
        scores_t = jnp.where(keep_t, dot(ki, qi, 1, 1), 0.0).astype(BF16)
        grad_scores = jnp.where(keep, dot(gi, vi, 1, 1), 0.0).astype(BF16)
        grad_scores_t = jnp.where(keep_t, dot(vi, gi, 1, 1), 0.0).astype(BF16)
        entering = first
        if n:
            entering = first + states[pl.ds((n - 1) * cols + part.start, HEAD_DIM), :]
        gq_i = dot(grad_scores, ki, 1, 0) + dot(gi, entering.astype(BF16), 1, 1)
        gk_i = dot(grad_scores_t, qi, 1, 0)
        gv_i = dot(scores_t, gi, 1, 0)
        if n < len(chunks) - 1:
            later = after[pl.ds(n * cols + part.start, HEAD_DIM), :].astype(BF16)
            gk_i = gk_i + dot(vi, later, 1, 1)
            gv_i = gv_i + dot(ki, later, 1, 0)
        gq[at, :] = gq_i.astype(BF16)
        gk[at, :] = gk_i
        gv[at, :] = gv_i
        if finished is not None:
            finished(n, at)


def first_grads_kernel(q, k, v, gm, prefix, states, after, *refs):
    gqs, gks, gvs = refs[:2], refs[2:4], refs[4:]
    for h in range(2):
        head_grads(h, q, k, v, gm, prefix, states, after, gqs[h], gks[h], gvs[h])


def second_grads_kernel(q, k, v, gm, prefix, states, after, mixed, oth_mixed, inverse, *refs):
    gq, gk, gv, out_hbm, out, sems = refs[-6:]
    shape = (HEAD_DIM, HEAD_DIM)

    def body(*pairs):
        copies = []
        for n, at in enumerate(chunk_slices(q.shape[0])):
            for i in range(at.start // HEAD_DIM, at.stop // HEAD_DIM):
                a = jnp.broadcast_to(inverse[i : i + 1, :], shape).T
                for h in range(q.shape[1] // HEAD_DIM):
                    value = pairs[h // 2][head_slice(i), head_slice(h % 2)]
                    out[head_slice(i), head_slice(h)] = (value * a).astype(BF16)
            copies.append(pltpu.make_async_copy(out.at[at], out_hbm.at[at], sems.at[n]))
            copies[-1].start()
        head_grads(2, q, k, v, gm, prefix, states, after, gq, gk, gv)
        for copy in copies:
            copy.wait()

    by_pair(body, mixed, oth_mixed)


def third_grads_kernel(q, k, v, gm, prefix, states, after, *refs):
    gqs, (gk, gv, gq_hbm, gq, sems) = refs[:3], refs[-5:]
    copies = []

    def send(src, h, at, sem):
        copies.append(pltpu.make_async_copy(src.at[at], gq_hbm.at[at, head_slice(h)], sem))
        copies[-1].start()

    for h in range(3):
        send(gqs[h], h, slice(0, q.shape[0]), sems.at[h])
    head_grads(
        3, q, k, v, gm, prefix, states, after, gq, gk, gv, lambda n, at: send(gq, 3, at, sems.at[3 + n])
    )
    for copy in copies:
        copy.wait()


def last_kernel(k, v, *refs):
    gks, gvs, pieces = (refs[i * QUAD : (i + 1) * QUAD] for i in range(3))
    gk_hbm, gv_hbm, gk, gv, suffix, sems = refs[-6:]
    load_pieces(pieces, ORDERS[True][1], suffix)
    copies = []
    for j, (parts, left, contract, out, hbm) in enumerate(
        ((gvs, k, 0, gv, gv_hbm), (gks, v, 1, gk, gk_hbm))
    ):
        for n, at in enumerate(chunk_slices(k.shape[0])):
            for h in range(QUAD):
                part = head_slice(h)
                new = dot(left[at, part], suffix[part, :], 1, contract)
                out[at, part] = (parts[h][at, :] + new).astype(BF16)
            copies.append(pltpu.make_async_copy(out.at[at], hbm.at[at], sems.at[j, n]))
            copies[-1].start()
    for copy in copies:
        copy.wait()


def all_parts(values, axis):
    size = len(values)
    power = size & (size - 1) == 0
    parts = [values[0]]
    for by in reversed(range(1, size)):
        pairs = [(i, i ^ by if power else (i + by) % size) for i in range(size)]
        parts.append(lax.ppermute(values[by], axis, pairs))
    return parts


def shards(sizes, queries, keys, values, grad_out):
    seq, head_size = sizes
    rows, cols = queries.shape
    chunks = rows // CHUNK
    blocks = rows // HEAD_DIM
    scan = quad_scan if seq == 2 * QUAD else doubling_scan

    def shape(count, lanes, kind=F32):
        return jax.ShapeDtypeStruct((count, lanes), kind)

    wide, narrow = shape(rows, cols), shape(rows, cols, BF16)
    head_wide, head_narrow = shape(rows, HEAD_DIM), shape(rows, HEAD_DIM, BF16)
    pieces_shape = [shape(HEAD_DIM, HEAD_DIM)] * QUAD
    states_shape = shape((chunks - 1) * cols, HEAD_DIM)
    pieces_scratch = pltpu.VMEM((cols, HEAD_DIM), F32)
    head_flops = 2 * rows * HEAD_DIM * HEAD_DIM
    chunk_flops = 2 * rows * CHUNK * HEAD_DIM

    *pieces, keys, values = call(
        state_kernel,
        pieces_shape + [pltpu.VMEM((rows, cols), BF16)] * 2,
        [pltpu.with_memory_space_constraint(a, pltpu.HBM) for a in (keys, values)],
        QUAD * head_flops,
        "local_state",
        spaces={0: pltpu.HBM, 1: pltpu.HBM},
        scratch=[pieces_scratch, pltpu.SemaphoreType.DMA((2, chunks))],
    )

    def forward(phase, token):
        if phase:
            return []
        return call(
            intra_kernel,
            [wide, states_shape, shape(cols, rows, BF16)],
            [queries, keys, values],
            QUAD * (2 * chunk_flops + 2 * head_flops),
            "intra",
        )

    prefixes, (intra, states, queries_t) = scan(pieces, sizes, False, forward)
    stats_shape = shape(2 * blocks, HEAD_DIM)

    def mix(is_own, pieces, count, *before):
        return call(
            functools.partial(mixed_kernel, is_own),
            [shape(rows, PAIR), shape(cols, HEAD_DIM, BF16)] + [stats_shape] * count,
            [intra, queries, grad_out, *pieces, *before],
            2 * head_flops,
            "mixed",
        )

    mixed, prefix, stats = mix(True, prefixes[:2], 1)
    oth_mixed, prefix, *stats = mix(False, prefixes[2:], head_size, stats, prefix)
    gm, inverse, after, *pieces = call(
        functools.partial(norm_kernel, cols * head_size),
        [narrow, shape(blocks, HEAD_DIM), states_shape] + pieces_shape,
        [mixed, oth_mixed, queries_t, grad_out, *all_parts(stats, "head")],
        QUAD * head_flops,
        "norm",
        scratch=[pieces_scratch],
    )
    args = [queries, keys, values, gm, prefix, states, after]
    grads_flops = 6 * chunk_flops + 3 * head_flops

    def backward(phase, token):
        if phase == 0:
            parts = call(
                first_grads_kernel,
                [head_narrow] * 2 + [head_wide] * 4,
                args,
                2 * grads_flops,
                "first_grads",
            )
        elif phase == 1:
            parts = call(
                second_grads_kernel,
                [head_narrow] + [head_wide] * 2 + [narrow],
                args + [mixed, oth_mixed, inverse, token],
                grads_flops,
                "second_grads",
                spaces={len(args) + 3: pl.ANY},
                outs={3: pl.ANY},
                scratch=[pltpu.VMEM((rows, cols), BF16), pltpu.SemaphoreType.DMA((chunks,))],
            )
        else:
            parts = call(
                third_grads_kernel,
                [head_wide] * 2 + [narrow],
                args + gqs + [token],
                grads_flops,
                "third_grads",
                spaces={len(args) + 3: pl.ANY},
                outs={2: pl.ANY},
                scratch=[
                    pltpu.VMEM((rows, HEAD_DIM), BF16),
                    pltpu.SemaphoreType.DMA((3 + chunks,)),
                ],
            )
        if phase < 2:
            count = 2 - phase
            gqs.extend(parts[:count])
            parts = parts[count:]
        count = 2 if phase == 0 else 1
        gks.extend(parts[:count])
        gvs.extend(parts[count : 2 * count])
        results.extend(parts[2 * count :])
        return gks[-1:]

    gqs, gks, gvs, results = [], [], [], []
    suffixes, unused = scan(pieces, sizes, True, backward)
    output, grad_q = results
    grad_k, grad_v = call(
        last_kernel,
        [narrow, narrow],
        [keys, values, *gks, *gvs, *suffixes],
        2 * QUAD * head_flops,
        "last",
        outs={0: pl.ANY, 1: pl.ANY},
        scratch=[pltpu.VMEM((rows, cols), BF16)] * 2
        + [pltpu.VMEM((cols, HEAD_DIM), BF16), pltpu.SemaphoreType.DMA((2, chunks))],
    )
    return output, grad_q, grad_k, grad_v


def solution(mesh):
    sizes = (mesh.shape["seq"], mesh.shape["head"])
    spec = P("seq", "head")
    return jax.shard_map(
        functools.partial(shards, sizes),
        mesh=mesh,
        in_specs=(spec,) * 4,
        out_specs=(spec,) * 4,
        check_vma=False,
    )
```

```python
import functools
import math

import jax
import jax.numpy as jnp
from jax import lax
from jax.experimental import pallas as pl
from jax.experimental.pallas import tpu as pltpu
from jax.sharding import PartitionSpec as P

HEAD_DIM = 128
EPSILON = 1e-06
CHUNK = 256
PAIR = 2 * HEAD_DIM
QUAD = 4
ORDERS = {
    False: (((3, 2, 1), (3, 2, 1)), ((3, 2, 1), (3, 2, 1))),
    True: (((3, 1, 2), (3, 1, 2)), ((3, 1, 2), (3, 1, 2))),
}
F32 = jnp.float32
BF16 = jnp.bfloat16


def dot(a, b, ca, cb):
    return lax.dot_general(a, b, (((ca,), (cb,)), ((), ())), preferred_element_type=F32)


def head_slice(h):
    return slice(h * HEAD_DIM, (h + 1) * HEAD_DIM)


def chunk_slices(rows, size=CHUNK):
    return [slice(start, start + size) for start in range(0, rows, size)]


def causal(transposed=False):
    rows = lax.broadcasted_iota(jnp.int32, (CHUNK, CHUNK), 0)
    cols = lax.broadcasted_iota(jnp.int32, (CHUNK, CHUNK), 1)
    return cols >= rows if transposed else rows >= cols


def call(body, out_shape, args, flops, name, spaces=None, outs=None, scratch=()):
    size = sum(a.size * a.dtype.itemsize for a in args)
    size += sum(math.prod(a.shape) * a.dtype.itemsize for a in out_shape)
    spaces, outs = spaces or {}, outs or {}
    kernel = pl.pallas_call(
        body,
        out_shape=out_shape,
        in_specs=[
            pl.BlockSpec(memory_space=spaces.get(i, pltpu.VMEM)) for i in range(len(args))
        ],
        out_specs=[
            pl.BlockSpec(memory_space=outs.get(i, pltpu.VMEM)) for i in range(len(out_shape))
        ],
        scratch_shapes=list(scratch),
        compiler_params=pltpu.CompilerParams(vmem_limit_bytes=20 * 2**20),
        cost_estimate=pl.CostEstimate(flops=flops, bytes_accessed=size, transcendentals=0),
        name=name,
    )
    return list(kernel(*args))


def partner(order, slot):
    if slot == 0:
        return 0
    even, odd = (choice[slot - 1] for choice in order)
    if even == odd:
        return even
    return jnp.where(lax.rem(lax.axis_index("head"), 2) == 1, odd, even)


def number_at(order, slot):
    return lax.rem(lax.axis_index("seq"), QUAD) ^ partner(order, slot)


def pair_of(number):
    return lax.rem(number, 2) ^ (number // 2)


def head_at(order, slot):
    number = number_at(order, slot)
    return 2 * pair_of(number) + number // 2


def rows_at(order, slot):
    return pl.ds(pl.multiple_of(head_at(order, slot) * HEAD_DIM, HEAD_DIM), HEAD_DIM)


def by_pair(body, mine, other):
    pair = pair_of(lax.rem(lax.axis_index("seq"), QUAD))
    pl.when(pair == 0)(functools.partial(body, mine, other))
    pl.when(pair == 1)(functools.partial(body, other, mine))


def exchange(value, sizes, by):
    size, heads = sizes
    pairs = [
        (i * heads + h, (i ^ by[h % 2]) * heads + h) for i in range(size) for h in range(heads)
    ]
    return lax.ppermute(value, ("seq", "head"), pairs)


def exchange_all(pieces, sizes, order):
    even, odd = order
    return pieces[:1] + [exchange(p, sizes, by) for p, by in zip(pieces[1:], zip(even, odd))]


def quad_kernel(*refs):
    refs[-1][...] = (refs[0][...] + refs[1][...]) + (refs[2][...] + refs[3][...])


def finish_kernel(reverse, *refs):
    into, out_of = ORDERS[reverse]
    place = lax.axis_index("seq")
    zero = jnp.zeros(refs[0].shape, F32)
    second = place < QUAD if reverse else place >= QUAD
    before = jnp.where(second, refs[QUAD][...], zero)
    for to, out in enumerate(refs[-QUAD:]):
        here = number_at(out_of, to)
        total = before
        for slot in range(QUAD):
            number = number_at(into, slot)
            ahead = number > here if reverse else number < here
            total = total + jnp.where(ahead, refs[slot][...], zero)
        out[...] = total


def quad_scan(pieces, sizes, reverse, between):
    head = jax.ShapeDtypeStruct((HEAD_DIM, HEAD_DIM), F32)
    into, out_of = ORDERS[reverse]
    pieces = exchange_all(pieces, sizes, into)
    first = between(0, None)
    (total,) = call(
        quad_kernel, [head], [*pieces, *first[-1:]], 0, "quad_sum", spaces={4: pl.ANY}
    )
    far = exchange(total, sizes, (QUAD, QUAD))
    second = between(1, total)
    finished = call(
        functools.partial(finish_kernel, reverse),
        [head] * QUAD,
        [*pieces, far, *second[-1:]],
        0,
        "finish",
        spaces={5: pl.ANY},
    )
    third = between(2, finished[0])
    return exchange_all(finished, sizes, out_of), first + second + third


def doubling_scan(pieces, sizes, reverse, between):
    size = sizes[0]

    def shift(value, by):
        pairs = [(i, i + by) for i in range(size - by)]
        if reverse:
            pairs = [(b, a) for a, b in pairs]
        return lax.ppermute(value, "seq", pairs)

    into, out_of = (
        jnp.stack([head_at(order, slot) for slot in range(QUAD)]) for order in ORDERS[reverse]
    )
    state = jnp.stack(pieces)[jnp.argsort(into)]
    by = 1
    while by < size:
        state = state + shift(state, by)
        by *= 2
    state = shift(state, 1)[out_of]
    done = []
    for phase in range(3):
        done += between(phase, done[-1] if done else None)
    return [state[n] for n in range(QUAD)], done


def store_pieces(states, order, pieces, scratch):
    for h, state in enumerate(states):
        scratch[head_slice(h), :] = state
    for slot, piece in enumerate(pieces):
        piece[...] = scratch[rows_at(order, slot), :]


def load_pieces(pieces, order, rounded, first=0):
    for slot, piece in enumerate(pieces, first):
        rounded[rows_at(order, slot), :] = piece[...].astype(BF16)


def pair_blocks(left, right, contract):
    blocks = []
    for p in range(right.shape[1] // PAIR):
        cols = slice(p * PAIR, (p + 1) * PAIR)
        full = dot(left[:, cols] if contract == 0 else left[cols, :], right[:, cols], contract, 0)
        blocks += [full[:HEAD_DIM, :HEAD_DIM], full[HEAD_DIM:, HEAD_DIM:]]
    return blocks


def add_all(a, b):
    return b if a is None else [x + y for x, y in zip(a, b)]


def state_kernel(k_hbm, v_hbm, *refs):
    pieces, (k, v, scratch, sems) = refs[:QUAD], refs[QUAD:]
    chunks = chunk_slices(k.shape[0])
    copies = []
    for n, at in enumerate(chunks):
        for j, (src, dst) in enumerate(((k_hbm, k), (v_hbm, v))):
            copies.append(pltpu.make_async_copy(src.at[at], dst.at[at], sems.at[j, n]))
            copies[-1].start()
    total = None
    for n, at in enumerate(chunks):
        copies[2 * n].wait()
        copies[2 * n + 1].wait()
        total = add_all(total, pair_blocks(k[at, :], v[at, :], 0))
    store_pieces(total, ORDERS[False][0], pieces, scratch)


def intra_kernel(q, k, v, intra, states, q_t):
    keep = causal()
    cols = q.shape[1]
    q_t[...] = q[...].T
    for h in range(cols // HEAD_DIM):
        part = head_slice(h)
        state = None
        for n, at in enumerate(chunk_slices(q.shape[0])):
            qi, ki, vi = q[at, part], k[at, part], v[at, part]
            scores = jnp.where(keep, dot(qi, ki, 1, 1), 0.0).astype(BF16)
            out = dot(scores, vi, 1, 0)
            if n:
                out = out + dot(qi, state.astype(BF16), 1, 0)
                states[(n - 1) * cols + part.start : (n - 1) * cols + part.stop, :] = state
            intra[at, part] = out
            new = dot(ki, vi, 0, 0)
            state = state + new if n else new


def scores_kernel(q, k, token, scores_t):
    keep = causal(True)
    rows = q.shape[0]
    for h in range(q.shape[1] // HEAD_DIM):
        part = head_slice(h)
        for at in chunk_slices(rows):
            raw = dot(k[at, part], q[at, part], 1, 1)
            to = slice(h * rows + at.start, h * rows + at.stop)
            scores_t[to, :] = jnp.where(keep, raw, 0.0).astype(BF16)


def row_sums(tile):
    return jnp.sum(tile.T, axis=0, keepdims=True)


def mixed_kernel(is_own, intra, q, g, *refs):
    pieces, refs = refs[:2], refs[2:]
    before, refs = ([], refs) if is_own else (refs[:2], refs[2:])
    mixed, prefix, *stats = refs
    in_order = number_at(ORDERS[False][1], 0 if is_own else 2) // 2 == 0
    one, two = (piece[...].astype(BF16) for piece in pieces)
    states = [jnp.where(in_order, one, two), jnp.where(in_order, two, one)]
    blocks = q.shape[0] // HEAD_DIM

    def pair(p):
        for at in chunk_slices(q.shape[0]):
            square = cross = None
            for j in range(2):
                part, whole = head_slice(j), head_slice(2 * p + j)
                m = intra[at, whole] + dot(q[at, whole], states[j], 1, 0)
                mixed[at, part] = m
                s, c = m * m, m * g[at, whole].astype(F32)
                square = s if square is None else square + s
                cross = c if cross is None else cross + c
            for n in range(CHUNK // HEAD_DIM):
                for first, value in ((0, square), (blocks, cross)):
                    i = first + at.start // HEAD_DIM + n
                    sums = row_sums(value[head_slice(n)])
                    if before:
                        sums = sums + before[0][i : i + 1, :]
                    stats[0][i : i + 1, :] = sums
        for j in range(2):
            prefix[head_slice(2 * p + j), :] = states[j]
        if before:
            part = slice((1 - p) * PAIR, (2 - p) * PAIR)
            prefix[part, :] = before[1][part, :]

    by_pair(lambda mine, other: pair(0 if mine else 1), is_own, not is_own)
    for copy in stats[1:]:
        copy[...] = stats[0][...]


def norm_kernel(width, mixed, oth_mixed, q_t, g, *refs):
    stats, (gm, inverse_out, states, *pieces, scratch) = refs[: -4 - QUAD], refs[-4 - QUAD :]
    total = stats[0][...]
    for r in stats[1:]:
        total = total + r[...]
    rows, cols = gm.shape
    blocks = rows // HEAD_DIM
    inverse = lax.rsqrt(total[:blocks] / width + EPSILON)
    cross_mean = total[blocks:] * inverse / width
    scale = inverse * inverse * cross_mean
    inverse_out[...] = inverse
    shape = (HEAD_DIM, HEAD_DIM)

    def body(*pairs):
        after = None
        for n, at in reversed(list(enumerate(chunk_slices(rows)))):
            for i in range(at.start // HEAD_DIM, at.stop // HEAD_DIM):
                block = head_slice(i)
                a = jnp.broadcast_to(inverse[i : i + 1], shape).T
                b = jnp.broadcast_to(scale[i : i + 1], shape).T
                for h in range(cols // HEAD_DIM):
                    part = head_slice(h)
                    value = pairs[h // 2][block, head_slice(h % 2)]
                    grad = g[block, part].astype(F32)
                    gm[block, part] = (grad * a - value * b).astype(BF16)
            after = add_all(after, pair_blocks(q_t[:, at], gm[at, :], 1))
            if n:
                for h, state in enumerate(after):
                    first = (n - 1) * cols + h * HEAD_DIM
                    states[first : first + HEAD_DIM, :] = state
        for h, state in enumerate(after):
            scratch[head_slice(h), :] = state

    by_pair(body, mixed, oth_mixed)
    for slot, piece in enumerate(pieces):
        piece[...] = scratch[rows_at(ORDERS[True][0], slot), :]


def head_grads(h, q, k, v, gm, prefix, states, after, scores, gq, gk, gv, finished=None):
    (rows, cols), part = q.shape, head_slice(h)
    keep, keep_t = causal(), causal(True)
    chunks = chunk_slices(q.shape[0])
    first = prefix[part, :].astype(F32)
    for n, at in enumerate(chunks):
        qi, ki, vi, gi = q[at, part], k[at, part], v[at, part], gm[at, part]
        scores_t = scores[h * rows + at.start : h * rows + at.stop, :]
        grad_scores = jnp.where(keep, dot(gi, vi, 1, 1), 0.0).astype(BF16)
        grad_scores_t = jnp.where(keep_t, dot(vi, gi, 1, 1), 0.0).astype(BF16)
        entering = first
        if n:
            entering = first + states[pl.ds((n - 1) * cols + part.start, HEAD_DIM), :]
        gq_i = dot(grad_scores, ki, 1, 0) + dot(gi, entering.astype(BF16), 1, 1)
        gk_i = dot(grad_scores_t, qi, 1, 0)
        gv_i = dot(scores_t, gi, 1, 0)
        if n < len(chunks) - 1:
            later = after[pl.ds(n * cols + part.start, HEAD_DIM), :].astype(BF16)
            gk_i = gk_i + dot(vi, later, 1, 1)
            gv_i = gv_i + dot(ki, later, 1, 0)
        gq[at, :] = gq_i.astype(BF16)
        gk[at, :] = gk_i
        gv[at, :] = gv_i
        if finished is not None:
            finished(n, at)


def first_grads_kernel(q, k, v, gm, prefix, states, after, scores, *refs):
    gqs, gks, gvs = refs[:2], refs[2:4], refs[4:]
    for h in range(2):
        head_grads(h, q, k, v, gm, prefix, states, after, scores, gqs[h], gks[h], gvs[h])


def second_grads_kernel(q, k, v, gm, prefix, states, after, scores, *refs):
    mixed, oth_mixed, inverse = refs[:3]
    gq, gk, gv, out_hbm, out, sems = refs[-6:]
    shape = (HEAD_DIM, HEAD_DIM)

    def body(*pairs):
        copies = []
        for n, at in enumerate(chunk_slices(q.shape[0])):
            for i in range(at.start // HEAD_DIM, at.stop // HEAD_DIM):
                a = jnp.broadcast_to(inverse[i : i + 1, :], shape).T
                for h in range(q.shape[1] // HEAD_DIM):
                    value = pairs[h // 2][head_slice(i), head_slice(h % 2)]
                    out[head_slice(i), head_slice(h)] = (value * a).astype(BF16)
            copies.append(pltpu.make_async_copy(out.at[at], out_hbm.at[at], sems.at[n]))
            copies[-1].start()
        head_grads(2, q, k, v, gm, prefix, states, after, scores, gq, gk, gv)
        for copy in copies:
            copy.wait()

    by_pair(body, mixed, oth_mixed)


def third_grads_kernel(q, k, v, gm, prefix, states, after, scores, *refs):
    gqs, (gk, gv, gq_hbm, gq, sems) = refs[:3], refs[-5:]
    copies = []

    def send(src, h, at, sem):
        copies.append(pltpu.make_async_copy(src.at[at], gq_hbm.at[at, head_slice(h)], sem))
        copies[-1].start()

    for h in range(3):
        send(gqs[h], h, slice(0, q.shape[0]), sems.at[h])
    head_grads(
        3, q, k, v, gm, prefix, states, after, scores, gq, gk, gv, lambda n, at: send(gq, 3, at, sems.at[3 + n])
    )
    for copy in copies:
        copy.wait()


def last_kernel(k, v, *refs):
    gks, gvs, pieces = (refs[i * QUAD : (i + 1) * QUAD] for i in range(3))
    gk_hbm, gv_hbm, gk, gv, suffix, sems = refs[-6:]
    load_pieces(pieces, ORDERS[True][1], suffix)
    copies = []
    for j, (parts, left, contract, out, hbm) in enumerate(
        ((gvs, k, 0, gv, gv_hbm), (gks, v, 1, gk, gk_hbm))
    ):
        for n, at in enumerate(chunk_slices(k.shape[0])):
            for h in range(QUAD):
                part = head_slice(h)
                new = dot(left[at, part], suffix[part, :], 1, contract)
                out[at, part] = (parts[h][at, :] + new).astype(BF16)
            copies.append(pltpu.make_async_copy(out.at[at], hbm.at[at], sems.at[j, n]))
            copies[-1].start()
    for copy in copies:
        copy.wait()


def all_parts(values, axis):
    size = len(values)
    power = size & (size - 1) == 0
    parts = [values[0]]
    for by in reversed(range(1, size)):
        pairs = [(i, i ^ by if power else (i + by) % size) for i in range(size)]
        parts.append(lax.ppermute(values[by], axis, pairs))
    return parts


def shards(sizes, queries, keys, values, grad_out):
    seq, head_size = sizes
    rows, cols = queries.shape
    chunks = rows // CHUNK
    blocks = rows // HEAD_DIM
    scan = quad_scan if seq == 2 * QUAD else doubling_scan

    def shape(count, lanes, kind=F32):
        return jax.ShapeDtypeStruct((count, lanes), kind)

    wide, narrow = shape(rows, cols), shape(rows, cols, BF16)
    head_wide, head_narrow = shape(rows, HEAD_DIM), shape(rows, HEAD_DIM, BF16)
    pieces_shape = [shape(HEAD_DIM, HEAD_DIM)] * QUAD
    states_shape = shape((chunks - 1) * cols, HEAD_DIM)
    pieces_scratch = pltpu.VMEM((cols, HEAD_DIM), F32)
    head_flops = 2 * rows * HEAD_DIM * HEAD_DIM
    chunk_flops = 2 * rows * CHUNK * HEAD_DIM

    *pieces, keys, values = call(
        state_kernel,
        pieces_shape + [pltpu.VMEM((rows, cols), BF16)] * 2,
        [pltpu.with_memory_space_constraint(a, pltpu.HBM) for a in (keys, values)],
        QUAD * head_flops,
        "local_state",
        spaces={0: pltpu.HBM, 1: pltpu.HBM},
        scratch=[pieces_scratch, pltpu.SemaphoreType.DMA((2, chunks))],
    )

    def forward(phase, token):
        if phase == 2:
            return []
        if phase == 1:
            return call(
                scores_kernel,
                [shape(QUAD * rows, CHUNK, BF16)],
                [queries, keys, token],
                QUAD * chunk_flops,
                "scores",
                spaces={2: pl.ANY},
            )
        return call(
            intra_kernel,
            [wide, states_shape, shape(cols, rows, BF16)],
            [queries, keys, values],
            QUAD * (2 * chunk_flops + 2 * head_flops),
            "intra",
        )

    prefixes, (intra, states, queries_t, scores) = scan(pieces, sizes, False, forward)
    stats_shape = shape(2 * blocks, HEAD_DIM)

    def mix(is_own, pieces, count, *before):
        return call(
            functools.partial(mixed_kernel, is_own),
            [shape(rows, PAIR), shape(cols, HEAD_DIM, BF16)] + [stats_shape] * count,
            [intra, queries, grad_out, *pieces, *before],
            2 * head_flops,
            "mixed",
        )

    mixed, prefix, stats = mix(True, prefixes[:2], 1)
    oth_mixed, prefix, *stats = mix(False, prefixes[2:], head_size, stats, prefix)
    gm, inverse, after, *pieces = call(
        functools.partial(norm_kernel, cols * head_size),
        [narrow, shape(blocks, HEAD_DIM), states_shape] + pieces_shape,
        [mixed, oth_mixed, queries_t, grad_out, *all_parts(stats, "head")],
        QUAD * head_flops,
        "norm",
        scratch=[pieces_scratch],
    )
    args = [queries, keys, values, gm, prefix, states, after, scores]
    grads_flops = 5 * chunk_flops + 3 * head_flops

    def backward(phase, token):
        if phase == 0:
            parts = call(
                first_grads_kernel,
                [head_narrow] * 2 + [head_wide] * 4,
                args,
                2 * grads_flops,
                "first_grads",
            )
        elif phase == 1:
            parts = call(
                second_grads_kernel,
                [head_narrow] + [head_wide] * 2 + [narrow],
                args + [mixed, oth_mixed, inverse, token],
                grads_flops,
                "second_grads",
                spaces={len(args) + 3: pl.ANY},
                outs={3: pl.ANY},
                scratch=[pltpu.VMEM((rows, cols), BF16), pltpu.SemaphoreType.DMA((chunks,))],
            )
        else:
            parts = call(
                third_grads_kernel,
                [head_wide] * 2 + [narrow],
                args + gqs + [token],
                grads_flops,
                "third_grads",
                spaces={len(args) + 3: pl.ANY},
                outs={2: pl.ANY},
                scratch=[
                    pltpu.VMEM((rows, HEAD_DIM), BF16),
                    pltpu.SemaphoreType.DMA((3 + chunks,)),
                ],
            )
        if phase < 2:
            count = 2 - phase
            gqs.extend(parts[:count])
            parts = parts[count:]
        count = 2 if phase == 0 else 1
        gks.extend(parts[:count])
        gvs.extend(parts[count : 2 * count])
        results.extend(parts[2 * count :])
        return gks[-1:]

    gqs, gks, gvs, results = [], [], [], []
    suffixes, unused = scan(pieces, sizes, True, backward)
    output, grad_q = results
    grad_k, grad_v = call(
        last_kernel,
        [narrow, narrow],
        [keys, values, *gks, *gvs, *suffixes],
        2 * QUAD * head_flops,
        "last",
        outs={0: pl.ANY, 1: pl.ANY},
        scratch=[pltpu.VMEM((rows, cols), BF16)] * 2
        + [pltpu.VMEM((cols, HEAD_DIM), BF16), pltpu.SemaphoreType.DMA((2, chunks))],
    )
    return output, grad_q, grad_k, grad_v


def solution(mesh):
    sizes = (mesh.shape["seq"], mesh.shape["head"])
    spec = P("seq", "head")
    return jax.shard_map(
        functools.partial(shards, sizes),
        mesh=mesh,
        in_specs=(spec,) * 4,
        out_specs=(spec,) * 4,
        check_vma=False,
    )
```
